32 devices in a mesh: region: 8 (over z, core), group: 4 (over y, x).
Axes of the slice: x: 2, y: 2, z: 4, core: 2. Of those that a mesh axis runs over, the one named last changes fastest.
Arguments:
- object_slab: float32 [4096, 2, 2048], P('region', None, 'group'), may hold values from -6 to 6
- probe: float32 [4, 2, 256, 256], replicated, may hold values from -6 to 6
- diffraction: float32 [128, 256, 256], P(('region', 'group')), may hold values from 0.25 to 16
- positions: int32 [128, 2], P(('region', 'group')), may hold values from 0 to 3840, as said below
- slot_counts: int32 [4, 8], P('group', 'region'), may hold values from 1 to 4, 20 in all within a row
Outputs:
- new_object: float32 [4096, 2, 2048], P('region', None, 'group')
- new_probe: float32 [4, 2, 256, 256], replicated
The draws below stay inside these ranges and needn't reach their ends.
Inputs may be any that keep to these rules, and one draw needn't show every extreme that they name: `positions`: A slot of region index r has its row in r * 512 to min(r * 512 + 511, 3840); columns lie in 0 to 256; rows 0 and 3840 and columns 0 and 256 are each taken by some slot.
All inputs are finite; a program needn't handle non-finite values. No bound on the sum of `slot_counts` on one device may be relied on, other than what follows from the above.
Results may differ from the reference program's by a relative error of at most 0.0003.
Values sent between devices are 32-bit elements; how exact they have to be, the bound alone decides.
No kernel may reach another device: no remote copies, remote signals or barrier semaphores. Data moves between devices by JAX's collectives and lax.ppermute only.
A program may use at most 128 MiB of HBM per device.

```python
import math
import jax
import jax.numpy as jnp
import numpy as np
from jax import lax

P_SIZE = 256
MODES = 4
CAP = 4
TH = 512
SW = 512
ITERS = 1
OH = 4096
OW = 2048
PATTERNS = 128
LIVE = 20
N_REGION = 8
N_GROUP = 4


def draw_positions(key, part):
    k_rows, k_cols, k_pick = jax.random.split(key, 3)
    index = jnp.arange(PATTERNS, dtype=jnp.int32)
    region_of = index // (N_GROUP * CAP)
    offsets = jax.random.randint(k_rows, (PATTERNS,), 0, TH)
    rows = jnp.minimum(region_of * TH + offsets, OH - P_SIZE)
    rows = rows.at[0].set(0).at[PATTERNS - 1].set(OH - P_SIZE)
    cols = jax.random.randint(k_cols, (PATTERNS,), 0, SW - P_SIZE + 1)
    picks = jax.random.permutation(k_pick, PATTERNS)
    cols = cols.at[picks[0]].set(0).at[picks[1]].set(SW - P_SIZE)
    return jnp.stack([rows, cols], axis=1).astype(jnp.int32)


def shard_levels(stream_key, shape, shards, low, high):
    loudness = 1.0
    for axis_at, parts in shards:
        heights = jax.random.uniform(jax.random.fold_in(jax.random.fold_in(stream_key, 6), axis_at), (parts,), jnp.float32, low / len(shards), high / len(shards))
        loudness = loudness * jnp.repeat(jnp.exp(heights), shape[axis_at] // parts).reshape((-1,) + (1,) * (len(shape) - 1 - axis_at))
    return loudness


def length_profile(amount, total, most, lean):
    weights = [(1 << 20) // math.isqrt(grade ** lean) + 1 for grade in range(2, amount + 1)]
    surplus, holding = total - most - (amount - 1), [1] * (amount - 1)
    while surplus > 0:
        free = [i for i in range(amount - 1) if holding[i] < most]
        mass, remaining = sum([weights[i] for i in free]), surplus
        for i in free:
            more = min(most - holding[i], max(1, remaining * weights[i] // mass), surplus)
            holding[i] = holding[i] + more
            surplus = surplus - more
    return np.array([most] + holding)


def ragged(own_key, count, total, most, skew):
    if count == 2:
        one = jax.random.randint(own_key, (), max(1, total - most), min(most, total - 1) + 1)
        return jnp.stack([one, total - one])
    sizes = jnp.asarray(length_profile(count, total, most, skew), jnp.int32)
    couples = (count - 1) // 2
    donor, taker = sizes[1:1 + 2 * couples:2], sizes[2:2 + 2 * couples:2]
    slack = jnp.minimum(donor - 1, most - taker)
    shifted = jax.random.randint(jax.random.fold_in(own_key, 1), (couples,), 0, 1 << 20) % (slack + 1)
    sizes = sizes.at[1:1 + 2 * couples:2].set(donor - shifted).at[2:2 + 2 * couples:2].set(taker + shifted)
    return sizes[jax.random.permutation(jax.random.fold_in(own_key, 2), count)]


def noise(stream_key, dims, width, bound, cuts=(), kind=jnp.bfloat16):
    factor_of = shard_levels(stream_key, dims, cuts, -0.22, 0.18) if cuts else 1.0
    array = jax.random.normal(stream_key, dims, jnp.float32) * width * factor_of
    return jnp.minimum(jnp.maximum(array, -bound), bound).astype(kind)


def setup_inputs(seed: int = 0) -> dict:
    key_of = jax.random.split(jax.random.key(seed), 6)
    object_slab = noise(key_of[0], (OH, 2, OW), 1.0, 6.0, ((0, 8), (2, 4)), jnp.float32)
    probe = noise(key_of[1], (MODES, 2, P_SIZE, P_SIZE), 1.0, 6.0, (), jnp.float32)
    diffraction = jnp.clip(jnp.exp(math.log(16.0) - 4.158883 * jax.random.uniform(key_of[2], (PATTERNS, P_SIZE, P_SIZE), jnp.float32) ** shard_levels(key_of[2], (PATTERNS, P_SIZE, P_SIZE), ((0, 32),), -0.2, 0.2)), 0.25, 16.0)
    positions = draw_positions(jax.random.fold_in(key_of[5], 71), 0)
    slot_counts = jax.vmap(lambda own: ragged(own, N_REGION, LIVE, CAP, 2))(jax.random.split(key_of[4], N_GROUP)).reshape((N_GROUP, N_REGION)).astype(jnp.int32)
    return {"object_slab": object_slab, "probe": probe, "diffraction": diffraction, "positions": positions, "slot_counts": slot_counts}


def reference(object_slab, probe, diffraction, positions, slot_counts):
    obj = object_slab
    prb = probe
    for step in range(ITERS):
        probe_c = lax.complex(prb[:, 0], prb[:, 1])
        peak = jnp.max(lax.optimization_barrier(jnp.sum(prb[:, 0] * prb[:, 0] + prb[:, 1] * prb[:, 1], axis=0)))

        def one(carry, index):
            ograd, pgrad, cover = carry
            position_entry = index % CAP
            device = index // CAP
            grp = device % N_GROUP
            reg = device // N_GROUP
            live = (position_entry < slot_counts[grp, reg]).astype(jnp.float32)
            row = positions[index, 0].astype(jnp.int32)
            col = (positions[index, 1] + grp * SW).astype(jnp.int32)
            win = lax.dynamic_slice(obj, (row, jnp.int32(0), col), (P_SIZE, 2, P_SIZE))
            win_c = lax.complex(win[:, 0, :], win[:, 1, :])
            far = jnp.fft.fft2(probe_c * win_c[None], norm='ortho')
            model_intensity = lax.optimization_barrier(jnp.sum(far.real * far.real + far.imag * far.imag, axis=0))
            update_ratio = 1.0 - jnp.sqrt(diffraction[index]) / jnp.sqrt(jnp.maximum(model_intensity, 1.0))
            chi = jnp.fft.ifft2(far * update_ratio[None], norm='ortho')
            chi_r = chi.real * live
            chi_i = chi.imag * live
            pr = probe_c.real
            pim = probe_c.imag
            go_r = lax.optimization_barrier(jnp.sum(pr * chi_r + pim * chi_i, axis=0))
            go_i = lax.optimization_barrier(jnp.sum(pr * chi_i - pim * chi_r, axis=0))
            wr = win_c.real
            wi = win_c.imag
            gp = jnp.stack([wr[None] * chi_r + wi[None] * chi_i, wr[None] * chi_i - wi[None] * chi_r], axis=1)
            current = lax.dynamic_slice(ograd, (row, jnp.int32(0), col), (P_SIZE, 2, P_SIZE))
            ograd = lax.dynamic_update_slice(ograd, current + jnp.stack([go_r, go_i], axis=1), (row, jnp.int32(0), col))
            return ((ograd, pgrad + gp, cover + live * (wr * wr + wi * wi)), None)
        start = (jnp.zeros(obj.shape, jnp.float32), jnp.zeros(prb.shape, jnp.float32), jnp.zeros((P_SIZE, P_SIZE), jnp.float32))
        (ograd, pgrad, cover), unused = lax.scan(one, start, jnp.arange(PATTERNS, dtype=jnp.int32))
        obj = obj - ograd / peak
        prb = prb - pgrad / (cover + 1e-06)[None, None]
    return (obj, prb)
```

```python
import functools
import math

import jax
import jax.numpy as jnp
import numpy as np
from jax import lax
from jax.experimental import pallas as pl
from jax.experimental.pallas import tpu as pltpu
from jax.sharding import PartitionSpec as P

LANES = 128
SUBLANES = 8
EPSILON = 1e-06


def shifted(block, axis, distance):
    devices = range(lax.axis_size(axis))
    route = [(i - distance, i) for i in devices if i - distance in devices]
    return lax.ppermute(block, axis, route)


def packed(block):
    rows, parts, columns = block.shape
    cut = block.reshape(rows, parts, columns // LANES, LANES).transpose(0, 2, 1, 3)
    return cut.reshape(rows * parts * columns // LANES, LANES)


def unpacked(block, shape):
    rows, parts, columns = shape
    cut = block.reshape(rows, columns // LANES, parts, LANES).transpose(0, 2, 1, 3)
    return cut.reshape(rows, parts, columns)


def tables(side):
    half = side // 2
    n, q = np.arange(half)[:, None], np.arange(half)[None, :]
    made = []
    for odd in range(2):
        angle = 2.0 * math.pi * ((n * (2 * q + odd)) % side) / side
        re, im = np.cos(angle) / math.sqrt(side), -np.sin(angle) / math.sqrt(side)
        made.append(np.block([[re, im], [-im, re]]))
    exact = np.stack([made[0], made[1], made[0].T, made[1].T]).astype(np.float32)
    high = exact.astype(jnp.bfloat16)
    low = (exact - high.astype(np.float32)).astype(jnp.bfloat16)
    return np.stack([high, low])


def parity_order(side):
    half = side // 2
    order = np.concatenate([np.arange(0, side, 2), np.arange(1, side, 2)])
    move = np.zeros((side, side), np.float32)
    move[order, np.arange(side)] = 1.0
    return np.stack([move, move.T]).astype(jnp.bfloat16)


def split(x):
    high = x.astype(jnp.bfloat16)
    low = (x - high.astype(jnp.float32)).astype(jnp.bfloat16)
    return high, low


def dot(a, b):
    return jnp.dot(a, b, preferred_element_type=jnp.float32)


def by_lanes(x, table_ref, index):
    high, low = split(x)
    t_high, t_low = table_ref[0, index], table_ref[1, index]
    return dot(
        jnp.concatenate([high, low, high], axis=1),
        jnp.concatenate([t_high, t_high, t_low], axis=0),
    )


def by_rows(x, table_ref, index):
    high, low = split(x)
    t_high, t_low = table_ref[0, index], table_ref[1, index]
    return dot(
        jnp.concatenate([t_high, t_high, t_low], axis=1),
        jnp.concatenate([high, low, high], axis=0),
    )


def moved(x, product):
    first, _ = split(x)
    rest = x - first.astype(jnp.float32)
    return product([first, *split(rest)])


def step_kernel(
    place_ref,
    count_ref,
    core_ref,
    object_hbm,
    halo_hbm,
    probe_ref,
    diffraction_ref,
    table_ref,
    order_ref,
    object_out,
    spill_out,
    mine_out,
    theirs_out,
    extended,
    gradient,
    sums,
    window,
    power,
    far,
    back,
    semaphores,
):
    modes, _, side, _ = probe_ref.shape
    half = side // 2
    tile_rows = object_hbm.shape[0]
    halo_rows = halo_hbm.shape[0]
    per_row = object_out.shape[0] // (object_out.shape[0] // SUBLANES)
    chunks = sums.shape[0]
    copies = [
        pltpu.make_async_copy(object_hbm, extended.at[pl.ds(0, tile_rows)], semaphores.at[0]),
        pltpu.make_async_copy(halo_hbm, extended.at[pl.ds(tile_rows, halo_rows)], semaphores.at[1]),
    ]
    for copy in copies:
        copy.start()
    gradient[...] = jnp.zeros_like(gradient)
    sums[...] = jnp.zeros_like(sums)
    total = jnp.zeros((side, side), jnp.float32)
    for mode in range(modes):
        total = total + probe_ref[mode, 0] * probe_ref[mode, 0] + probe_ref[mode, 1] * probe_ref[mode, 1]
    power[...] = total
    scale = 1.0 / jnp.max(total)
    for copy in copies:
        copy.wait()
    lane = lax.broadcasted_iota(jnp.int32, (side, LANES), 1)
    blocks = side // LANES

    def slot(index, carry):
        row = place_ref[index, 0]
        column = place_ref[index, 1]
        first = column // LANES
        shift = column - first * LANES
        back_shift = lax.rem(LANES - shift, LANES)
        last = per_row // 2 - 1

        def rows_of(block, part):
            at = row * per_row + jnp.minimum(first + block, last) * 2 + part
            return pl.ds(at, side, stride=per_row)

        for part in range(2):
            rolled = [
                pltpu.roll(extended[rows_of(block, part), :], back_shift, 1)
                for block in range(blocks + 1)
            ]
            for block in range(blocks):
                window[part, :, pl.ds(block * LANES, LANES)] = jnp.where(
                    lane < LANES - shift, rolled[block], rolled[block + 1]
                )

        def forward(mode, carry):
            w_r, w_i = window[0], window[1]
            p_r, p_i = probe_ref[mode, 0], probe_ref[mode, 1]
            e_r = p_r * w_r - p_i * w_i
            e_i = p_r * w_i + p_i * w_r
            plus = jnp.concatenate([e_r[:, :half] + e_r[:, half:], e_i[:, :half] + e_i[:, half:]], axis=1)
            minus = jnp.concatenate([e_r[:, :half] - e_r[:, half:], e_i[:, :half] - e_i[:, half:]], axis=1)
            even = by_lanes(plus, table_ref, 0)
            odd = by_lanes(minus, table_ref, 1)
            real = jnp.concatenate([even[:, :half], odd[:, :half]], axis=1)
            imag = jnp.concatenate([even[:, half:], odd[:, half:]], axis=1)
            plus = jnp.concatenate([real[:half] + real[half:], imag[:half] + imag[half:]], axis=0)
            minus = jnp.concatenate([real[:half] - real[half:], imag[:half] - imag[half:]], axis=0)
            far[mode, 0] = by_rows(plus, table_ref, 2)
            far[mode, 1] = by_rows(minus, table_ref, 3)
            return carry

        lax.fori_loop(0, modes, forward, 0)

        move = order_ref[0]
        measured = moved(diffraction_ref[index], lambda terms: dot(
            jnp.concatenate([order_ref[1]] * 3, axis=1), jnp.concatenate(terms, axis=0)
        ))
        measured = moved(measured, lambda terms: dot(
            jnp.concatenate(terms, axis=1), jnp.concatenate([move] * 3, axis=0)
        ))
        for odd in range(2):
            seen = measured[odd * half : (odd + 1) * half]
            intensity = jnp.zeros((half, side), jnp.float32)
            for mode in range(modes):
                re, im = far[mode, odd, pl.ds(0, half), :], far[mode, odd, pl.ds(half, half), :]
                intensity = intensity + re * re + im * im
            ratio = seen * lax.rsqrt(seen * jnp.maximum(intensity, 1.0))
            for mode in range(modes):
                far[mode, odd, pl.ds(0, half), :] = far[mode, odd, pl.ds(0, half), :] * ratio
                far[mode, odd, pl.ds(half, half), :] = far[mode, odd, pl.ds(half, half), :] * ratio

        back[0] = power[...] * window[0]
        back[1] = power[...] * window[1]

        def backward(mode, carry):
            even = by_rows(far[mode, 0], table_ref, 0)
            odd = by_rows(far[mode, 1], table_ref, 1)
            plus, minus = even + odd, even - odd
            real = jnp.concatenate([plus[:half], minus[:half]], axis=0)
            imag = jnp.concatenate([plus[half:], minus[half:]], axis=0)
            even = by_lanes(jnp.concatenate([real[:, :half], imag[:, :half]], axis=1), table_ref, 2)
            odd = by_lanes(jnp.concatenate([real[:, half:], imag[:, half:]], axis=1), table_ref, 3)
            plus, minus = even + odd, even - odd
            c_r = jnp.concatenate([plus[:, :half], minus[:, :half]], axis=1)
            c_i = jnp.concatenate([plus[:, half:], minus[:, half:]], axis=1)
            p_r, p_i = probe_ref[mode, 0], probe_ref[mode, 1]
            back[0] = back[0] - (p_r * c_r + p_i * c_i)
            back[1] = back[1] - (p_r * c_i - p_i * c_r)
            w_r, w_i = window[0], window[1]
            by_chunk = (chunks, SUBLANES, side)
            sums[:, 2 * mode] += (w_r * c_r + w_i * c_i).reshape(by_chunk)
            sums[:, 2 * mode + 1] += (w_r * c_i - w_i * c_r).reshape(by_chunk)
            return carry

        lax.fori_loop(0, modes, backward, 0)
        w_r, w_i = window[0], window[1]
        sums[:, 2 * modes] += (w_r * w_r + w_i * w_i).reshape(chunks, SUBLANES, side)

        for part in range(2):
            rolled = [
                pltpu.roll(back[part, :, pl.ds(block * LANES, LANES)], shift, 1) for block in range(blocks)
            ]
            zero = jnp.zeros((side, LANES), jnp.float32)
            for block in range(blocks + 1):
                here = rolled[block] if block < blocks else zero
                before = rolled[block - 1] if block else zero
                at = rows_of(block, part)
                gradient[at, :] = gradient[at, :] + jnp.where(lane >= shift, here, before)
        return carry

    lax.fori_loop(0, count_ref[0, 0], slot, 0)
    object_out[...] = extended[pl.ds(0, tile_rows), :] - gradient[pl.ds(0, tile_rows), :] * scale
    spill_out[...] = gradient[pl.ds(tile_rows, halo_rows), :] * scale
    share = chunks // 2
    core = core_ref[0, 0]
    mine_out[...] = sums[pl.ds(core * share, share)]
    theirs_out[...] = sums[pl.ds((1 - core) * share, share)]


def gradient_step(place, count, core, tile, halo, probe, diffraction):
    modes, parts, side, _ = probe.shape
    planes = parts * modes + 1
    chunks = side // SUBLANES
    f32 = jnp.float32
    smem = pl.BlockSpec(memory_space=pltpu.SMEM)
    vmem = pl.BlockSpec(memory_space=pltpu.VMEM)
    anywhere = pl.BlockSpec(memory_space=pl.ANY)
    share = jax.ShapeDtypeStruct((chunks // 2, planes, SUBLANES, side), f32)
    products = 3 * 16 * modes * diffraction.shape[0] * side**3
    return pl.pallas_call(
        step_kernel,
        out_shape=(
            jax.ShapeDtypeStruct(tile.shape, f32),
            jax.ShapeDtypeStruct(halo.shape, f32),
            share,
            share,
        ),
        in_specs=[smem, smem, smem, anywhere, anywhere, vmem, vmem, vmem, vmem],
        out_specs=(vmem, vmem, vmem, vmem),
        scratch_shapes=[
            pltpu.VMEM((tile.shape[0] + halo.shape[0], LANES), f32),
            pltpu.VMEM((tile.shape[0] + halo.shape[0], LANES), f32),
            pltpu.VMEM((chunks, planes, SUBLANES, side), f32),
            pltpu.VMEM((2, side, side), f32),
            pltpu.VMEM((side, side), f32),
            pltpu.VMEM((modes, 2, side, side), f32),
            pltpu.VMEM((2, side, side), f32),
            pltpu.SemaphoreType.DMA((2,)),
        ],
        compiler_params=pltpu.CompilerParams(vmem_limit_bytes=48 * 1024 * 1024),
        cost_estimate=pl.CostEstimate(flops=2 * products, bytes_accessed=16 << 20, transcendentals=0),
        name="gradient_step",
    )(place, count, core, tile, halo, probe, diffraction, jnp.asarray(tables(side)), jnp.asarray(parity_order(side)))


def on_device(object_slab, probe, diffraction, positions, slot_counts):
    modes, parts, side, _ = probe.shape
    tile_rows, _, columns = object_slab.shape
    regions, groups = lax.axis_size("region"), lax.axis_size("group")
    region, group = lax.axis_index("region"), lax.axis_index("group")
    core, layer = region % 2, region // 2
    layers = regions // 2
    per_row = parts * columns // LANES
    assert per_row == SUBLANES
    tile = packed(object_slab)
    halo = shifted(tile[: side * per_row], "region", -1)
    place = positions - jnp.stack([region * tile_rows, jnp.zeros_like(region)])[None, :].astype(jnp.int32)
    core_entry = core.astype(jnp.int32).reshape(1, 1)
    new_tile, spill, mine, theirs = gradient_step(place, slot_counts, core_entry, tile, halo, probe, diffraction)

    partner = [(i, i ^ 1) for i in range(regions)]
    arrived = shifted(spill, "region", 1)
    mine = mine + lax.ppermute(theirs, "region", partner)
    same_core = [[2 * i + c for i in range(layers)] for c in range(2)]
    planes = parts * modes + 1
    mine = lax.all_to_all(mine, "group", 0, 0, tiled=True)
    mine = jnp.sum(mine.reshape(groups, -1, planes, SUBLANES, side), axis=0)
    rows = mine.shape[0] * SUBLANES // layers
    mine = mine.reshape(-1, planes, SUBLANES // min(rows, SUBLANES), min(rows, SUBLANES), side)
    mine = mine.transpose(0, 2, 1, 3, 4).reshape(layers, planes, rows, side)
    mine = lax.all_to_all(mine, "region", 0, 0, axis_index_groups=same_core, tiled=True)
    mine = jnp.sum(mine.reshape(layers, planes, rows, side), axis=0)
    start = core * (side // 2) + group * (rows * layers) + layer * rows
    old = lax.dynamic_slice(probe.reshape(planes - 1, side, side), (0, start, 0), (planes - 1, rows, side))
    fresh = (EPSILON * old + mine[:-1]) / (mine[-1:] + EPSILON)
    fresh = lax.all_gather(fresh, "region", axis_index_groups=same_core)
    fresh = lax.all_gather(fresh, "group")
    other = lax.ppermute(fresh, "region", partner)
    whole = jnp.where(core == 0, jnp.stack([fresh, other]), jnp.stack([other, fresh]))
    new_probe = whole.transpose(3, 0, 1, 2, 4, 5).reshape(probe.shape)

    overlap = spill.shape[0]
    new_tile = lax.dynamic_update_slice(new_tile, new_tile[:overlap] - arrived, (0, 0))
    return (unpacked(new_tile, object_slab.shape), new_probe)


def solution(mesh):
    placed = (
        P("region", None, "group"),
        P(),
        P(("region", "group"), None, None),
        P(("region", "group"), None),
        P("group", "region"),
    )
    return jax.shard_map(
        on_device,
        mesh=mesh,
        in_specs=placed,
        out_specs=(P("region", None, "group"), P()),
        check_vma=False,
    )
```

```python
import functools
import math

import jax
import jax.numpy as jnp
import numpy as np
from jax import lax
from jax.experimental import pallas as pl
from jax.experimental.pallas import tpu as pltpu
from jax.sharding import PartitionSpec as P

LANES = 128
SUBLANES = 8
EPSILON = 1e-06


def shifted(block, axis, distance):
    devices = range(lax.axis_size(axis))
    route = [(i - distance, i) for i in devices if i - distance in devices]
    return lax.ppermute(block, axis, route)


def packed(block):
    rows, parts, columns = block.shape
    cut = block.reshape(rows, parts, columns // LANES, LANES).transpose(0, 2, 1, 3)
    return cut.reshape(rows * parts * columns // LANES, LANES)


def unpacked(block, shape):
    rows, parts, columns = shape
    cut = block.reshape(rows, columns // LANES, parts, LANES).transpose(0, 2, 1, 3)
    return cut.reshape(rows, parts, columns)


def tables(side):
    half = side // 2
    n, q = np.arange(half)[:, None], np.arange(half)[None, :]
    made = []
    for odd in range(2):
        angle = 2.0 * math.pi * ((n * (2 * q + odd)) % side) / side
        re, im = np.cos(angle) / math.sqrt(side), -np.sin(angle) / math.sqrt(side)
        made.append(np.block([[re, im], [-im, re]]))
    exact = np.stack([made[0], made[1], made[0].T, made[1].T]).astype(np.float32)
    high = exact.astype(jnp.bfloat16)
    low = (exact - high.astype(np.float32)).astype(jnp.bfloat16)
    return np.stack([high, low])


def parity_order(side):
    half = side // 2
    order = np.concatenate([np.arange(0, side, 2), np.arange(1, side, 2)])
    move = np.zeros((side, side), np.float32)
    move[order, np.arange(side)] = 1.0
    return np.stack([move, move.T]).astype(jnp.bfloat16)


def split(x):
    high = x.astype(jnp.bfloat16)
    low = (x - high.astype(jnp.float32)).astype(jnp.bfloat16)
    return high, low


def dot(a, b):
    return jnp.dot(a, b, preferred_element_type=jnp.float32)


def by_lanes(x, table_ref, index):
    high, low = split(x)
    t_high, t_low = table_ref[0, index], table_ref[1, index]
    return dot(
        jnp.concatenate([high, low, high], axis=1),
        jnp.concatenate([t_high, t_high, t_low], axis=0),
    )


def by_rows(x, table_ref, index):
    high, low = split(x)
    t_high, t_low = table_ref[0, index], table_ref[1, index]
    return dot(
        jnp.concatenate([t_high, t_high, t_low], axis=1),
        jnp.concatenate([high, low, high], axis=0),
    )


def moved(x, product):
    first, _ = split(x)
    rest = x - first.astype(jnp.float32)
    return product([first, *split(rest)])


def step_kernel(
    place_ref,
    count_ref,
    here_ref,
    object_hbm,
    halo_hbm,
    probe_ref,
    diffraction_ref,
    table_ref,
    order_ref,
    object_out,
    spill_out,
    mine_out,
    near_out,
    far_out,
    extended,
    gradient,
    sums,
    window,
    power,
    far,
    back,
    semaphores,
):
    modes, _, side, _ = probe_ref.shape
    half = side // 2
    tile_rows = object_hbm.shape[0]
    halo_rows = halo_hbm.shape[0]
    per_row = object_out.shape[0] // (object_out.shape[0] // SUBLANES)
    chunks = sums.shape[0]
    copies = [
        pltpu.make_async_copy(object_hbm, extended.at[pl.ds(0, tile_rows)], semaphores.at[0]),
        pltpu.make_async_copy(halo_hbm, extended.at[pl.ds(tile_rows, halo_rows)], semaphores.at[1]),
    ]
    for copy in copies:
        copy.start()
    gradient[...] = jnp.zeros_like(gradient)
    sums[...] = jnp.zeros_like(sums)
    total = jnp.zeros((side, side), jnp.float32)
    for mode in range(modes):
        total = total + probe_ref[mode, 0] * probe_ref[mode, 0] + probe_ref[mode, 1] * probe_ref[mode, 1]
    power[...] = total
    scale = 1.0 / jnp.max(total)
    for copy in copies:
        copy.wait()
    lane = lax.broadcasted_iota(jnp.int32, (side, LANES), 1)
    blocks = side // LANES

    def slot(index, carry):
        row = place_ref[index, 0]
        column = place_ref[index, 1]
        first = column // LANES
        shift = column - first * LANES
        back_shift = lax.rem(LANES - shift, LANES)
        last = per_row // 2 - 1

        def rows_of(block, part):
            at = row * per_row + jnp.minimum(first + block, last) * 2 + part
            return pl.ds(at, side, stride=per_row)

        for part in range(2):
            rolled = [
                pltpu.roll(extended[rows_of(block, part), :], back_shift, 1)
                for block in range(blocks + 1)
            ]
            for block in range(blocks):
                window[part, :, pl.ds(block * LANES, LANES)] = jnp.where(
                    lane < LANES - shift, rolled[block], rolled[block + 1]
                )

        for mode in range(modes):
            w_r, w_i = window[0], window[1]
            p_r, p_i = probe_ref[mode, 0], probe_ref[mode, 1]
            e_r = p_r * w_r - p_i * w_i
            e_i = p_r * w_i + p_i * w_r
            plus = jnp.concatenate([e_r[:, :half] + e_r[:, half:], e_i[:, :half] + e_i[:, half:]], axis=1)
            minus = jnp.concatenate([e_r[:, :half] - e_r[:, half:], e_i[:, :half] - e_i[:, half:]], axis=1)
            even = by_lanes(plus, table_ref, 0)
            odd = by_lanes(minus, table_ref, 1)
            real = jnp.concatenate([even[:, :half], odd[:, :half]], axis=1)
            imag = jnp.concatenate([even[:, half:], odd[:, half:]], axis=1)
            plus = jnp.concatenate([real[:half] + real[half:], imag[:half] + imag[half:]], axis=0)
            minus = jnp.concatenate([real[:half] - real[half:], imag[:half] - imag[half:]], axis=0)
            far[mode, 0] = by_rows(plus, table_ref, 2)
            far[mode, 1] = by_rows(minus, table_ref, 3)

        move = order_ref[0]
        measured = moved(diffraction_ref[index], lambda terms: dot(
            jnp.concatenate([order_ref[1]] * 3, axis=1), jnp.concatenate(terms, axis=0)
        ))
        measured = moved(measured, lambda terms: dot(
            jnp.concatenate(terms, axis=1), jnp.concatenate([move] * 3, axis=0)
        ))
        for odd in range(2):
            seen = measured[odd * half : (odd + 1) * half]
            intensity = jnp.zeros((half, side), jnp.float32)
            for mode in range(modes):
                re, im = far[mode, odd, pl.ds(0, half), :], far[mode, odd, pl.ds(half, half), :]
                intensity = intensity + re * re + im * im
            ratio = seen * lax.rsqrt(seen * jnp.maximum(intensity, 1.0))
            for mode in range(modes):
                far[mode, odd, pl.ds(0, half), :] = far[mode, odd, pl.ds(0, half), :] * ratio
                far[mode, odd, pl.ds(half, half), :] = far[mode, odd, pl.ds(half, half), :] * ratio

        back[0] = power[...] * window[0]
        back[1] = power[...] * window[1]

        for mode in range(modes):
            even = by_rows(far[mode, 0], table_ref, 0)
            odd = by_rows(far[mode, 1], table_ref, 1)
            plus, minus = even + odd, even - odd
            real = jnp.concatenate([plus[:half], minus[:half]], axis=0)
            imag = jnp.concatenate([plus[half:], minus[half:]], axis=0)
            even = by_lanes(jnp.concatenate([real[:, :half], imag[:, :half]], axis=1), table_ref, 2)
            odd = by_lanes(jnp.concatenate([real[:, half:], imag[:, half:]], axis=1), table_ref, 3)
            plus, minus = even + odd, even - odd
            c_r = jnp.concatenate([plus[:, :half], minus[:, :half]], axis=1)
            c_i = jnp.concatenate([plus[:, half:], minus[:, half:]], axis=1)
            p_r, p_i = probe_ref[mode, 0], probe_ref[mode, 1]
            back[0] = back[0] - (p_r * c_r + p_i * c_i)
            back[1] = back[1] - (p_r * c_i - p_i * c_r)
            w_r, w_i = window[0], window[1]
            by_chunk = (chunks, SUBLANES, side)
            sums[:, 2 * mode] += (w_r * c_r + w_i * c_i).reshape(by_chunk)
            sums[:, 2 * mode + 1] += (w_r * c_i - w_i * c_r).reshape(by_chunk)
        w_r, w_i = window[0], window[1]
        sums[:, 2 * modes] += (w_r * w_r + w_i * w_i).reshape(chunks, SUBLANES, side)

        for part in range(2):
            rolled = [
                pltpu.roll(back[part, :, pl.ds(block * LANES, LANES)], shift, 1) for block in range(blocks)
            ]
            zero = jnp.zeros((side, LANES), jnp.float32)
            for block in range(blocks + 1):
                here = rolled[block] if block < blocks else zero
                before = rolled[block - 1] if block else zero
                at = rows_of(block, part)
                gradient[at, :] = gradient[at, :] + jnp.where(lane >= shift, here, before)
        return carry

    lax.fori_loop(0, count_ref[0, 0], slot, 0)
    object_out[...] = extended[pl.ds(0, tile_rows), :] - gradient[pl.ds(0, tile_rows), :] * scale
    spill_out[...] = gradient[pl.ds(tile_rows, halo_rows), :] * scale
    core, group, layer = here_ref[0, 0], here_ref[0, 1], here_ref[0, 2]
    groups, layers = mine_out.shape[0], mine_out.shape[1]
    for hop in range(groups):
        for step in range(layers):
            at = (group ^ hop) * layers + lax.rem(layer + step, layers)
            mine_out[hop, step] = sums[core * (chunks // 2) + at]
            if hop < groups - 1:
                near_out[hop, step] = sums[(1 - core) * (chunks // 2) + at]
            else:
                far_out[step] = sums[(1 - core) * (chunks // 2) + at]


def gradient_step(place, count, here, tile, halo, probe, diffraction, groups, layers):
    modes, parts, side, _ = probe.shape
    planes = parts * modes + 1
    chunks = side // SUBLANES
    f32 = jnp.float32
    smem = pl.BlockSpec(memory_space=pltpu.SMEM)
    vmem = pl.BlockSpec(memory_space=pltpu.VMEM)
    anywhere = pl.BlockSpec(memory_space=pl.ANY)
    chunk = (planes, SUBLANES, side)
    products = 3 * 16 * modes * diffraction.shape[0] * side**3
    return pl.pallas_call(
        step_kernel,
        out_shape=(
            jax.ShapeDtypeStruct(tile.shape, f32),
            jax.ShapeDtypeStruct(halo.shape, f32),
            jax.ShapeDtypeStruct((groups, layers, *chunk), f32),
            jax.ShapeDtypeStruct((groups - 1, layers, *chunk), f32),
            jax.ShapeDtypeStruct((layers, *chunk), f32),
        ),
        in_specs=[smem, smem, smem, anywhere, anywhere, vmem, vmem, vmem, vmem],
        out_specs=(vmem, vmem, vmem, vmem, vmem),
        scratch_shapes=[
            pltpu.VMEM((tile.shape[0] + halo.shape[0], LANES), f32),
            pltpu.VMEM((tile.shape[0] + halo.shape[0], LANES), f32),
            pltpu.VMEM((chunks, *chunk), f32),
            pltpu.VMEM((2, side, side), f32),
            pltpu.VMEM((side, side), f32),
            pltpu.VMEM((modes, 2, side, side), f32),
            pltpu.VMEM((2, side, side), f32),
            pltpu.SemaphoreType.DMA((2,)),
        ],
        compiler_params=pltpu.CompilerParams(vmem_limit_bytes=48 * 1024 * 1024),
        cost_estimate=pl.CostEstimate(flops=2 * products, bytes_accessed=16 << 20, transcendentals=0),
        name="gradient_step",
    )(place, count, here, tile, halo, probe, diffraction, jnp.asarray(tables(side)), jnp.asarray(parity_order(side)))


def place_kernel(layers, pieces, here_ref, *refs):
    *sources, out = refs
    core, group, layer = here_ref[0, 0], here_ref[0, 1], here_ref[0, 2]
    for source, (flip, hop, first) in zip(sources, pieces):
        for j in range(source.shape[0]):
            from_layer = lax.rem(layer + layers - (first + j), layers)
            at = (core ^ flip) * (out.shape[1] // 2) + (group ^ hop) * layers + from_layer
            out[:, at] = source[j]


def put_in_place(here, layers, pieces, arrays, planes, side):
    vmem = pl.BlockSpec(memory_space=pltpu.VMEM)
    return pl.pallas_call(
        functools.partial(place_kernel, layers, pieces),
        out_shape=jax.ShapeDtypeStruct((planes, side // SUBLANES, SUBLANES, side), jnp.float32),
        in_specs=[pl.BlockSpec(memory_space=pltpu.SMEM)] + [vmem] * len(arrays),
        out_specs=vmem,
        compiler_params=pltpu.CompilerParams(vmem_limit_bytes=24 * 1024 * 1024),
        cost_estimate=pl.CostEstimate(flops=0, bytes_accessed=4 << 20, transcendentals=0),
        name="put_in_place",
    )(here, *arrays)


def across(block, hop):
    return lax.ppermute(block, "group", [(i, i ^ hop) for i in range(lax.axis_size("group"))])


def from_partner(block):
    return lax.ppermute(block, "region", [(i, i ^ 1) for i in range(lax.axis_size("region"))])


def up_layers(block, step):
    regions = lax.axis_size("region")
    return lax.ppermute(block, "region", [(i, (i + 2 * step) % regions) for i in range(regions)])


def probe_by_shards(probe, mine, near, far, here, layers, arrived):
    modes, parts, side, _ = probe.shape
    planes = modes * parts
    half = layers // 2
    near, other_far = lax.optimization_barrier((near, from_partner(far)))
    other_near = from_partner(near)
    far_sum = mine[3] + other_far
    by_x, by_y = across(far_sum[:half], 1), across(far_sum[half:], 2)
    near_sum = mine[:3] + other_near
    to_x = near_sum[1].at[half:].add(by_y)
    to_y = near_sum[2].at[:half].add(by_x)
    summed = near_sum[0] + across(to_x, 1) + across(to_y, 2)
    summed, arrived = lax.optimization_barrier((summed, arrived))
    total = summed[0]
    for step in range(1, layers):
        total = total + up_layers(summed[step], step)
    core, group, layer = here[0, 0], here[0, 1], here[0, 2]
    start = core * (side // 2) + (group * layers + layer) * SUBLANES
    old = lax.dynamic_slice(probe.reshape(planes, side, side), (0, start, 0), (planes, SUBLANES, side))
    fresh = (EPSILON * old + total[:-1]) / (total[-1:] + EPSILON)
    own = jnp.stack([fresh] + [up_layers(fresh, step) for step in range(1, layers)])
    x, y = across(own, 1), across(own, 2)
    arrays = [own, x, y, across(x[:half], 2), across(y[half:], 1)]
    pieces = [(0, 0), (1, 0), (2, 0), (3, 0), (3, half)]
    arrays = arrays + [from_partner(array) for array in arrays]
    pieces = tuple((flip, hop, first) for flip in range(2) for hop, first in pieces)
    return put_in_place(here, layers, pieces, arrays, planes, side).reshape(probe.shape), arrived


def probe_from_whole(probe, mine, near, far):
    side = probe.shape[2]
    own = mine.reshape(-1, *mine.shape[2:])
    rest = jnp.concatenate([near.reshape(-1, *near.shape[2:]), far])
    whole = lax.psum(jnp.concatenate([own, rest]), ("region", "group"))
    whole = whole.transpose(1, 0, 2, 3).reshape(-1, side, side)
    old = probe.reshape(-1, side, side)
    return ((EPSILON * old + whole[:-1]) / (whole[-1:] + EPSILON)).reshape(probe.shape)


def on_device(object_slab, probe, diffraction, positions, slot_counts):
    modes, parts, side, _ = probe.shape
    tile_rows, _, columns = object_slab.shape
    regions, groups = lax.axis_size("region"), lax.axis_size("group")
    region, group = lax.axis_index("region"), lax.axis_index("group")
    per_row = parts * columns // LANES
    assert per_row == SUBLANES
    layers = regions // 2
    sharded = groups == 4 and 2 * groups * layers * SUBLANES == side
    tile = packed(object_slab)
    halo = shifted(tile[: side * per_row], "region", -1)
    place = positions - jnp.stack([region * tile_rows, jnp.zeros_like(region)])[None, :].astype(jnp.int32)
    if sharded:
        here = jnp.stack([region % 2, group, region // 2]).astype(jnp.int32).reshape(1, 3)
    else:
        here = jnp.zeros((1, 3), jnp.int32)
        groups, layers = 4, side // SUBLANES // 8
    new_tile, spill, mine, near, far = gradient_step(
        place, slot_counts, here, tile, halo, probe, diffraction, groups, layers
    )
    arrived = shifted(spill, "region", 1)
    if sharded:
        new_probe, arrived = probe_by_shards(probe, mine, near, far, here, layers, arrived)
    else:
        new_probe = probe_from_whole(probe, mine, near, far)
    overlap = spill.shape[0]
    new_tile = lax.dynamic_update_slice(new_tile, new_tile[:overlap] - arrived, (0, 0))
    return (unpacked(new_tile, object_slab.shape), new_probe)


def solution(mesh):
    placed = (
        P("region", None, "group"),
        P(),
        P(("region", "group"), None, None),
        P(("region", "group"), None),
        P("group", "region"),
    )
    return jax.shard_map(
        on_device,
        mesh=mesh,
        in_specs=placed,
        out_specs=(P("region", None, "group"), P()),
        check_vma=False,
    )
```

```python
import functools
import math

import jax
import jax.numpy as jnp
import numpy as np
from jax import lax
from jax.experimental import pallas as pl
from jax.experimental.pallas import tpu as pltpu
from jax.sharding import PartitionSpec as P

LANES = 128
SUBLANES = 8
ROWS = 32
EPSILON = 1e-06


def shifted(block, axis, distance):
    devices = range(lax.axis_size(axis))
    route = [(i - distance, i) for i in devices if i - distance in devices]
    return lax.ppermute(block, axis, route)


def packed(block):
    rows, parts, columns = block.shape
    cut = block.reshape(rows, parts, columns // LANES, LANES).transpose(0, 2, 1, 3)
    return cut.reshape(rows * parts * columns // LANES, LANES)


def unpacked(block, shape):
    rows, parts, columns = shape
    cut = block.reshape(rows, columns // LANES, parts, LANES).transpose(0, 2, 1, 3)
    return cut.reshape(rows, parts, columns)


def tables(side):
    half = side // 2
    n, q = np.arange(half)[:, None], np.arange(half)[None, :]
    made = []
    for odd in range(2):
        angle = 2.0 * math.pi * ((n * (2 * q + odd)) % side) / side
        re, im = np.cos(angle) / math.sqrt(side), -np.sin(angle) / math.sqrt(side)
        made.append(np.block([[re, im], [-im, re]]))
    exact = np.stack([made[0], made[1], made[0].T, made[1].T]).astype(np.float32)
    high = exact.astype(jnp.bfloat16)
    low = (exact - high.astype(np.float32)).astype(jnp.bfloat16)
    return np.stack([high, low])


def parity_order(side):
    half = side // 2
    order = np.concatenate([np.arange(0, side, 2), np.arange(1, side, 2)])
    move = np.zeros((side, side), np.float32)
    move[order, np.arange(side)] = 1.0
    return np.stack([move, move.T]).astype(jnp.bfloat16)


def split(x):
    high = x.astype(jnp.bfloat16)
    low = (x - high.astype(jnp.float32)).astype(jnp.bfloat16)
    return high, low


def dot(a, b):
    return jnp.dot(a, b, preferred_element_type=jnp.float32)


def transform(terms, rows, table_ref, table, out):
    side = out.shape[2]
    for half in range(2):
        high = terms[half, rows, pl.ds(0, side)]
        low = terms[half, rows, pl.ds(side, side)]
        t_high, t_low = table_ref[0, table + half], table_ref[1, table + half]
        out[half, rows, :] = dot(
            jnp.concatenate([high, low, high], axis=1),
            jnp.concatenate([t_high, t_high, t_low], axis=0),
        )


def keep(terms, half, start, real, imag):
    rows = pl.ds(start, real.shape[0])
    side = 2 * real.shape[1]
    high, low = split(jnp.concatenate([real, imag], axis=1))
    terms[half, rows, pl.ds(0, side)] = high
    terms[half, rows, pl.ds(side, side)] = low


def moved(x, product):
    first, _ = split(x)
    rest = x - first.astype(jnp.float32)
    return product([first, *split(rest)])


def step_kernel(
    place_ref,
    count_ref,
    here_ref,
    object_hbm,
    halo_hbm,
    probe_ref,
    diffraction_ref,
    table_ref,
    order_ref,
    object_out,
    spill_out,
    mine_out,
    near_out,
    far_out,
    old_out,
    extended,
    gradient,
    sums,
    window,
    power,
    measured,
    terms,
    result,
    back,
    semaphores,
):
    modes, _, side, _ = probe_ref.shape
    half = side // 2
    tile_rows = object_hbm.shape[0]
    halo_rows = halo_hbm.shape[0]
    per_row = SUBLANES
    chunks = sums.shape[0]
    copies = [
        pltpu.make_async_copy(object_hbm, extended.at[pl.ds(0, tile_rows)], semaphores.at[0]),
        pltpu.make_async_copy(halo_hbm, extended.at[pl.ds(tile_rows, halo_rows)], semaphores.at[1]),
    ]
    for copy in copies:
        copy.start()
    gradient[...] = jnp.zeros_like(gradient)
    sums[...] = jnp.zeros_like(sums)
    total = jnp.zeros((side, side), jnp.float32)
    for mode in range(modes):
        total = total + probe_ref[mode, 0] * probe_ref[mode, 0] + probe_ref[mode, 1] * probe_ref[mode, 1]
    power[...] = total
    scale = 1.0 / jnp.max(total)
    for copy in copies:
        copy.wait()
    lane = lax.broadcasted_iota(jnp.int32, (side, LANES), 1)
    blocks = side // LANES
    left, right = pl.ds(0, half), pl.ds(half, half)
    pieces = [pl.ds(start, ROWS) for start in range(0, side, ROWS)]
    streams = [range(start, min(start + 2, modes)) for start in range(0, modes, 2)]

    def rows_of(stream):
        return pl.ds(stream[0] * side, len(stream) * side)

    def slot(index, carry):
        row = place_ref[index, 0]
        column = place_ref[index, 1]
        first = column // LANES
        shift = column - first * LANES
        back_shift = lax.rem(LANES - shift, LANES)
        last = per_row // 2 - 1

        def strided(block, part):
            at = row * per_row + jnp.minimum(first + block, last) * 2 + part
            return pl.ds(at, side, stride=per_row)

        for part in range(2):
            rolled = [
                pltpu.roll(extended[strided(block, part), :], back_shift, 1) for block in range(blocks + 1)
            ]
            for block in range(blocks):
                window[part, :, pl.ds(block * LANES, LANES)] = jnp.where(
                    lane < LANES - shift, rolled[block], rolled[block + 1]
                )
        move = order_ref[0]
        seen = moved(diffraction_ref[index], lambda bits: dot(
            jnp.concatenate([order_ref[1]] * 3, axis=1), jnp.concatenate(bits, axis=0)
        ))
        seen = moved(seen, lambda bits: dot(
            jnp.concatenate(bits, axis=1), jnp.concatenate([move] * 3, axis=0)
        ))
        measured[...] = seen.T

        for stream in streams:
            for mode in stream:
                for rows in pieces:
                    w = [window[part, rows, side_] for part in range(2) for side_ in (left, right)]
                    p = [probe_ref[mode, part, rows, side_] for part in range(2) for side_ in (left, right)]
                    real = [p[k] * w[k] - p[2 + k] * w[2 + k] for k in range(2)]
                    imag = [p[k] * w[2 + k] + p[2 + k] * w[k] for k in range(2)]
                    start = mode * side + rows.start
                    keep(terms, 0, start, real[0] + real[1], imag[0] + imag[1])
                    keep(terms, 1, start, real[0] - real[1], imag[0] - imag[1])
            transform(terms, rows_of(stream), table_ref, 0, result)
        for stream in streams:
            for mode in stream:
                for odd in range(2):
                    top, bottom = pl.ds(mode * side, half), pl.ds(mode * side + half, half)
                    a = [result[odd, top, side_] for side_ in (left, right)]
                    b = [result[odd, bottom, side_] for side_ in (left, right)]
                    start = mode * side + odd * half
                    keep(terms, 0, start, (a[0] + b[0]).T, (a[1] + b[1]).T)
                    keep(terms, 1, start, (a[0] - b[0]).T, (a[1] - b[1]).T)
            transform(terms, rows_of(stream), table_ref, 0, result)
        for odd in range(2):
            for rows in pieces:
                far = [
                    [result[odd, pl.ds(mode * side + rows.start, ROWS), side_] for side_ in (left, right)]
                    for mode in range(modes)
                ]
                intensity = jnp.zeros((ROWS, half), jnp.float32)
                for real, imag in far:
                    intensity = intensity + real * real + imag * imag
                amount = measured[rows, pl.ds(odd * half, half)]
                ratio = amount * lax.rsqrt(amount * jnp.maximum(intensity, 1.0))
                for mode, (real, imag) in enumerate(far):
                    keep(terms, odd, mode * side + rows.start, real * ratio, imag * ratio)
        for stream in streams:
            transform(terms, rows_of(stream), table_ref, 2, result)
        for stream in streams:
            for mode in stream:
                for odd in range(2):
                    rows = pl.ds(mode * side + odd * half, half)
                    a = [result[0, rows, side_] for side_ in (left, right)]
                    b = [result[1, rows, side_] for side_ in (left, right)]
                    start = mode * side
                    keep(terms, odd, start, (a[0] + b[0]).T, (a[1] + b[1]).T)
                    keep(terms, odd, start + half, (a[0] - b[0]).T, (a[1] - b[1]).T)
            transform(terms, rows_of(stream), table_ref, 2, result)
        for number, stream in enumerate(streams):
            for rows in pieces:
                chunk = pl.ds(rows.start // SUBLANES, ROWS // SUBLANES)
                by_chunk = (ROWS // SUBLANES, SUBLANES, half)
                for lower, side_ in enumerate((left, right)):
                    w_r, w_i = window[0, rows, side_], window[1, rows, side_]
                    if number:
                        g_r, g_i = back[0, rows, side_], back[1, rows, side_]
                    else:
                        strength = power[rows, side_]
                        g_r, g_i = strength * w_r, strength * w_i
                    for mode in stream:
                        at = pl.ds(mode * side + rows.start, ROWS)
                        if lower:
                            c_r = result[0, at, left] - result[1, at, left]
                            c_i = result[0, at, right] - result[1, at, right]
                        else:
                            c_r = result[0, at, left] + result[1, at, left]
                            c_i = result[0, at, right] + result[1, at, right]
                        p_r, p_i = probe_ref[mode, 0, rows, side_], probe_ref[mode, 1, rows, side_]
                        g_r = g_r - (p_r * c_r + p_i * c_i)
                        g_i = g_i - (p_r * c_i - p_i * c_r)
                        sums[chunk, 2 * mode, :, side_] += (w_r * c_r + w_i * c_i).reshape(by_chunk)
                        sums[chunk, 2 * mode + 1, :, side_] += (w_r * c_i - w_i * c_r).reshape(by_chunk)
                    back[0, rows, side_] = g_r
                    back[1, rows, side_] = g_i
                    if not number:
                        sums[chunk, 2 * modes, :, side_] += (w_r * w_r + w_i * w_i).reshape(by_chunk)

        for part in range(2):
            rolled = [
                pltpu.roll(back[part, :, pl.ds(block * LANES, LANES)], shift, 1) for block in range(blocks)
            ]
            zero = jnp.zeros((side, LANES), jnp.float32)
            for block in range(blocks + 1):
                here = rolled[block] if block < blocks else zero
                before = rolled[block - 1] if block else zero
                at = strided(block, part)
                gradient[at, :] = gradient[at, :] + jnp.where(lane >= shift, here, before)
        return carry

    lax.fori_loop(0, count_ref[0, 0], slot, 0)
    object_out[...] = extended[pl.ds(0, tile_rows), :] - gradient[pl.ds(0, tile_rows), :] * scale
    spill_out[...] = gradient[pl.ds(tile_rows, halo_rows), :] * scale
    core, group, layer = here_ref[0, 0], here_ref[0, 1], here_ref[0, 2]
    groups, layers = mine_out.shape[0], mine_out.shape[1]
    for hop in range(groups):
        for step in range(layers):
            at = (group ^ hop) * layers + lax.rem(layer + step, layers)
            mine_out[hop, step] = sums[core * (chunks // 2) + at]
            if hop < groups - 1:
                near_out[hop, step] = sums[(1 - core) * (chunks // 2) + at]
            else:
                far_out[step] = sums[(1 - core) * (chunks // 2) + at]
    start = pl.multiple_of(((core * groups + group) * layers + layer) * SUBLANES, SUBLANES)
    for mode in range(modes):
        for part in range(2):
            old_out[2 * mode + part] = probe_ref[mode, part, pl.ds(start, SUBLANES), :]


def gradient_step(place, count, here, tile, halo, probe, diffraction, groups, layers):
    modes, parts, side, _ = probe.shape
    planes = parts * modes + 1
    chunks = side // SUBLANES
    f32 = jnp.float32
    smem = pl.BlockSpec(memory_space=pltpu.SMEM)
    vmem = pl.BlockSpec(memory_space=pltpu.VMEM)
    anywhere = pl.BlockSpec(memory_space=pl.ANY)
    chunk = (planes, SUBLANES, side)
    products = 3 * 16 * modes * diffraction.shape[0] * side**3
    return pl.pallas_call(
        step_kernel,
        out_shape=(
            jax.ShapeDtypeStruct(tile.shape, f32),
            jax.ShapeDtypeStruct(halo.shape, f32),
            jax.ShapeDtypeStruct((groups, layers, *chunk), f32),
            jax.ShapeDtypeStruct((groups - 1, layers, *chunk), f32),
            jax.ShapeDtypeStruct((layers, *chunk), f32),
            jax.ShapeDtypeStruct((planes - 1, SUBLANES, side), f32),
        ),
        in_specs=[smem, smem, smem, pl.BlockSpec(memory_space=pltpu.HBM), anywhere, vmem, vmem, vmem, vmem],
        out_specs=(vmem,) * 6,
        scratch_shapes=[
            pltpu.VMEM((tile.shape[0] + halo.shape[0], LANES), f32),
            pltpu.VMEM((tile.shape[0] + halo.shape[0], LANES), f32),
            pltpu.VMEM((chunks, *chunk), f32),
            pltpu.VMEM((2, side, side), f32),
            pltpu.VMEM((side, side), f32),
            pltpu.VMEM((side, side), f32),
            pltpu.VMEM((2, modes * side, 2 * side), jnp.bfloat16),
            pltpu.VMEM((2, modes * side, side), f32),
            pltpu.VMEM((2, side, side), f32),
            pltpu.SemaphoreType.DMA((2,)),
        ],
        compiler_params=pltpu.CompilerParams(vmem_limit_bytes=30 * 1024 * 1024),
        cost_estimate=pl.CostEstimate(flops=2 * products, bytes_accessed=16 << 20, transcendentals=0),
        name="gradient_step",
    )(place, count, here, tile, halo, probe, diffraction, jnp.asarray(tables(side)), jnp.asarray(parity_order(side)))


def first_rows(tile, rows):
    def kernel(tile_ref, out_ref, semaphore):
        copy = pltpu.make_async_copy(tile_ref.at[pl.ds(0, rows)], out_ref, semaphore)
        copy.start()
        copy.wait()

    return pl.pallas_call(
        kernel,
        out_shape=jax.ShapeDtypeStruct((rows, LANES), jnp.float32),
        in_specs=[pl.BlockSpec(memory_space=pltpu.HBM)],
        out_specs=pl.BlockSpec(memory_space=pl.ANY),
        scratch_shapes=[pltpu.SemaphoreType.DMA],
        compiler_params=pltpu.CompilerParams(vmem_limit_bytes=62 * 1024 * 1024),
        name="first_rows",
    )(tile)


def divide_kernel(old_ref, *refs):
    *parts, out_ref = refs
    total = parts[0][...]
    for part in parts[1:]:
        total = total + part[...]
    out_ref[...] = (EPSILON * old_ref[...] + total[:-1]) / (total[-1:] + EPSILON)


def divided(old, parts):
    return pl.pallas_call(
        divide_kernel, out_shape=jax.ShapeDtypeStruct(old.shape, jnp.float32), name="divided"
    )(old, *parts)


def place_kernel(layers, pieces, here_ref, *refs):
    *sources, out = refs
    core, group, layer = here_ref[0, 0], here_ref[0, 1], here_ref[0, 2]
    for source, (flip, hop, first) in zip(sources, pieces):
        for j in range(source.shape[0]):
            from_layer = lax.rem(layer + layers - (first + j), layers)
            at = (core ^ flip) * (out.shape[1] // 2) + (group ^ hop) * layers + from_layer
            out[:, at] = source[j]


def put_in_place(here, layers, pieces, arrays, planes, side):
    vmem = pl.BlockSpec(memory_space=pltpu.VMEM)
    return pl.pallas_call(
        functools.partial(place_kernel, layers, pieces),
        out_shape=jax.ShapeDtypeStruct((planes, side // SUBLANES, SUBLANES, side), jnp.float32),
        in_specs=[pl.BlockSpec(memory_space=pltpu.SMEM)] + [vmem] * len(arrays),
        out_specs=vmem,
        compiler_params=pltpu.CompilerParams(vmem_limit_bytes=24 * 1024 * 1024),
        cost_estimate=pl.CostEstimate(flops=0, bytes_accessed=4 << 20, transcendentals=0),
        name="put_in_place",
    )(here, *arrays)


def across(block, hop):
    return lax.ppermute(block, "group", [(i, i ^ hop) for i in range(lax.axis_size("group"))])


def from_partner(block):
    return lax.ppermute(block, "region", [(i, i ^ 1) for i in range(lax.axis_size("region"))])


def up_layers(block, step):
    regions = lax.axis_size("region")
    return lax.ppermute(block, "region", [(i, (i + 2 * step) % regions) for i in range(regions)])


def probe_by_shards(probe, mine, near, far, old, here, layers, arrived):
    modes, parts, side, _ = probe.shape
    planes = modes * parts
    half = layers // 2
    near, other_far = lax.optimization_barrier((near, from_partner(far)))
    other_near = from_partner(near)
    far_sum = mine[3] + other_far
    by_x, by_y = across(far_sum[:half], 1), across(far_sum[half:], 2)
    near_sum = mine[:3] + other_near
    to_x = near_sum[1].at[half:].add(by_y)
    to_y = near_sum[2].at[:half].add(by_x)
    by_x, by_y = across(to_x, 1), across(to_y, 2)
    summed = [near_sum[0, step] + by_x[step] + by_y[step] for step in range(layers)]
    summed, arrived = lax.optimization_barrier((summed, arrived))
    fresh = divided(old, [summed[0]] + [up_layers(summed[step], step) for step in range(1, layers)])
    own = jnp.stack([fresh] + [up_layers(fresh, step) for step in range(1, layers)])
    x, y = across(own, 1), across(own, 2)
    arrays = [own, x, y, across(x[:half], 2), across(y[half:], 1)]
    pieces = [(0, 0), (1, 0), (2, 0), (3, 0), (3, half)]
    arrays = arrays + [from_partner(array) for array in arrays]
    pieces = tuple((flip, hop, first) for flip in range(2) for hop, first in pieces)
    return put_in_place(here, layers, pieces, arrays, planes, side).reshape(probe.shape), arrived


def probe_from_whole(probe, mine, near, far):
    side = probe.shape[2]
    own = mine.reshape(-1, *mine.shape[2:])
    rest = jnp.concatenate([near.reshape(-1, *near.shape[2:]), far])
    whole = lax.psum(jnp.concatenate([own, rest]), ("region", "group"))
    whole = whole.transpose(1, 0, 2, 3).reshape(-1, side, side)
    old = probe.reshape(-1, side, side)
    return ((EPSILON * old + whole[:-1]) / (whole[-1:] + EPSILON)).reshape(probe.shape)


def on_device(object_slab, probe, diffraction, positions, slot_counts):
    modes, parts, side, _ = probe.shape
    tile_rows, _, columns = object_slab.shape
    regions, groups = lax.axis_size("region"), lax.axis_size("group")
    region, group = lax.axis_index("region"), lax.axis_index("group")
    per_row = parts * columns // LANES
    assert per_row == SUBLANES
    layers = regions // 2
    sharded = groups == 4 and 2 * groups * layers * SUBLANES == side
    tile = packed(object_slab)
    halo = shifted(first_rows(tile, side * per_row), "region", -1)
    place = positions - jnp.stack([region * tile_rows, jnp.zeros_like(region)])[None, :].astype(jnp.int32)
    if sharded:
        here = jnp.stack([region % 2, group, region // 2]).astype(jnp.int32).reshape(1, 3)
    else:
        here = jnp.zeros((1, 3), jnp.int32)
        groups, layers = 4, side // SUBLANES // 8
    new_tile, spill, mine, near, far, old = gradient_step(
        place, slot_counts, here, tile, halo, probe, diffraction, groups, layers
    )
    arrived = shifted(spill, "region", 1)
    if sharded:
        new_probe, arrived = probe_by_shards(probe, mine, near, far, old, here, layers, arrived)
    else:
        new_probe = probe_from_whole(probe, mine, near, far)
    overlap = spill.shape[0]
    new_tile = lax.dynamic_update_slice(new_tile, new_tile[:overlap] - arrived, (0, 0))
    return (unpacked(new_tile, object_slab.shape), new_probe)


def solution(mesh):
    placed = (
        P("region", None, "group"),
        P(),
        P(("region", "group"), None, None),
        P(("region", "group"), None),
        P("group", "region"),
    )
    return jax.shard_map(
        on_device,
        mesh=mesh,
        in_specs=placed,
        out_specs=(P("region", None, "group"), P()),
        check_vma=False,
    )
```

```python
import functools
import math

import jax
import jax.numpy as jnp
import numpy as np
from jax import lax
from jax.experimental import pallas as pl
from jax.experimental.pallas import tpu as pltpu
from jax.sharding import PartitionSpec as P

LANES = 128
SUBLANES = 8
ROWS = 32
EPSILON = 1e-06


def shifted(block, axis, distance):
    devices = range(lax.axis_size(axis))
    route = [(i - distance, i) for i in devices if i - distance in devices]
    return lax.ppermute(block, axis, route)


def packed(block):
    rows, parts, columns = block.shape
    cut = block.reshape(rows, parts, columns // LANES, LANES).transpose(0, 2, 1, 3)
    return cut.reshape(rows * parts * columns // LANES, LANES)


def unpacked(block, shape):
    rows, parts, columns = shape
    cut = block.reshape(rows, columns // LANES, parts, LANES).transpose(0, 2, 1, 3)
    return cut.reshape(rows, parts, columns)


def tables(side):
    half = side // 2
    n, q = np.arange(half)[:, None], np.arange(half)[None, :]
    made = []
    for odd in range(2):
        angle = 2.0 * math.pi * ((n * (2 * q + odd)) % side) / side
        re, im = np.cos(angle) / math.sqrt(side), -np.sin(angle) / math.sqrt(side)
        made.append(np.block([[re, im], [-im, re]]))
    exact = np.stack([made[0], made[1], made[0].T, made[1].T]).astype(np.float32)
    high = exact.astype(jnp.bfloat16)
    low = (exact - high.astype(np.float32)).astype(jnp.bfloat16)
    return np.stack([high, low])


def parity_order(side):
    half = side // 2
    order = np.concatenate([np.arange(0, side, 2), np.arange(1, side, 2)])
    move = np.zeros((side, side), np.float32)
    move[order, np.arange(side)] = 1.0
    return np.stack([move, move.T]).astype(jnp.bfloat16)


def split(x):
    high = x.astype(jnp.bfloat16)
    low = (x - high.astype(jnp.float32)).astype(jnp.bfloat16)
    return high, low


def dot(a, b):
    return jnp.dot(a, b, preferred_element_type=jnp.float32)


def transform(terms, rows, table_ref, table, out):
    side = out.shape[2]
    for half in range(2):
        high = terms[half, rows, pl.ds(0, side)]
        low = terms[half, rows, pl.ds(side, side)]
        t_high, t_low = table_ref[0, table + half], table_ref[1, table + half]
        out[half, rows, :] = dot(
            jnp.concatenate([high, low, high], axis=1),
            jnp.concatenate([t_high, t_high, t_low], axis=0),
        )


def keep(terms, half, start, real, imag):
    rows = pl.ds(start, real.shape[0])
    side = 2 * real.shape[1]
    high, low = split(jnp.concatenate([real, imag], axis=1))
    terms[half, rows, pl.ds(0, side)] = high
    terms[half, rows, pl.ds(side, side)] = low


def moved(x, product):
    first, _ = split(x)
    rest = x - first.astype(jnp.float32)
    return product([first, *split(rest)])


def all_slots(
    local,
    tile_rows,
    place_ref,
    count_ref,
    probe_ref,
    table_ref,
    extended,
    gradient,
    sums,
    power,
    measured,
    window,
    terms,
    result,
    back,
):
    modes, _, side, _ = probe_ref.shape
    half = side // 2
    per_row = SUBLANES
    lane = lax.broadcasted_iota(jnp.int32, (side, LANES), 1)
    blocks = side // LANES
    left, right = pl.ds(0, half), pl.ds(half, half)
    pieces = [pl.ds(start, ROWS) for start in range(0, side, ROWS)]
    streams = [range(start, min(start + 2, modes)) for start in range(0, modes, 2)]

    def rows_of(stream):
        return pl.ds(stream[0] * side, len(stream) * side)

    def slot(index):
        row = place_ref[index, 0]
        column = place_ref[index, 1]
        first = column // LANES
        shift = column - first * LANES
        back_shift = lax.rem(LANES - shift, LANES)
        last = per_row // 2 - 1

        def strided(block, part):
            at = row * per_row + jnp.minimum(first + block, last) * 2 + part
            return pl.ds(at, side, stride=per_row)

        for part in range(2):
            rolled = [
                pltpu.roll(extended[strided(block, part), :], back_shift, 1) for block in range(blocks + 1)
            ]
            for block in range(blocks):
                window[part, :, pl.ds(block * LANES, LANES)] = jnp.where(
                    lane < LANES - shift, rolled[block], rolled[block + 1]
                )
        for stream in streams:
            for mode in stream:
                for rows in pieces:
                    w = [window[part, rows, side_] for part in range(2) for side_ in (left, right)]
                    p = [probe_ref[mode, part, rows, side_] for part in range(2) for side_ in (left, right)]
                    real = [p[k] * w[k] - p[2 + k] * w[2 + k] for k in range(2)]
                    imag = [p[k] * w[2 + k] + p[2 + k] * w[k] for k in range(2)]
                    start = mode * side + rows.start
                    keep(terms, 0, start, real[0] + real[1], imag[0] + imag[1])
                    keep(terms, 1, start, real[0] - real[1], imag[0] - imag[1])
            transform(terms, rows_of(stream), table_ref, 0, result)
        for stream in streams:
            for mode in stream:
                for odd in range(2):
                    top, bottom = pl.ds(mode * side, half), pl.ds(mode * side + half, half)
                    a = [result[odd, top, side_] for side_ in (left, right)]
                    b = [result[odd, bottom, side_] for side_ in (left, right)]
                    start = mode * side + odd * half
                    keep(terms, 0, start, (a[0] + b[0]).T, (a[1] + b[1]).T)
                    keep(terms, 1, start, (a[0] - b[0]).T, (a[1] - b[1]).T)
            transform(terms, rows_of(stream), table_ref, 0, result)
        for odd in range(2):
            for rows in pieces:
                far = [
                    [result[odd, pl.ds(mode * side + rows.start, ROWS), side_] for side_ in (left, right)]
                    for mode in range(modes)
                ]
                intensity = jnp.zeros((ROWS, half), jnp.float32)
                for real, imag in far:
                    intensity = intensity + real * real + imag * imag
                amount = measured[index, rows, pl.ds(odd * half, half)]
                ratio = amount * lax.rsqrt(amount * jnp.maximum(intensity, 1.0))
                for mode, (real, imag) in enumerate(far):
                    keep(terms, odd, mode * side + rows.start, real * ratio, imag * ratio)
        for stream in streams:
            transform(terms, rows_of(stream), table_ref, 2, result)
        for stream in streams:
            for mode in stream:
                for odd in range(2):
                    rows = pl.ds(mode * side + odd * half, half)
                    a = [result[0, rows, side_] for side_ in (left, right)]
                    b = [result[1, rows, side_] for side_ in (left, right)]
                    start = mode * side
                    keep(terms, odd, start, (a[0] + b[0]).T, (a[1] + b[1]).T)
                    keep(terms, odd, start + half, (a[0] - b[0]).T, (a[1] - b[1]).T)
            transform(terms, rows_of(stream), table_ref, 2, result)
        for number, stream in enumerate(streams):
            for rows in pieces:
                chunk = pl.ds(rows.start // SUBLANES, ROWS // SUBLANES)
                by_chunk = (ROWS // SUBLANES, SUBLANES, half)
                for lower, side_ in enumerate((left, right)):
                    w_r, w_i = window[0, rows, side_], window[1, rows, side_]
                    if number:
                        g_r, g_i = back[0, rows, side_], back[1, rows, side_]
                    else:
                        strength = power[rows, side_]
                        g_r, g_i = strength * w_r, strength * w_i
                    for mode in stream:
                        at = pl.ds(mode * side + rows.start, ROWS)
                        if lower:
                            c_r = result[0, at, left] - result[1, at, left]
                            c_i = result[0, at, right] - result[1, at, right]
                        else:
                            c_r = result[0, at, left] + result[1, at, left]
                            c_i = result[0, at, right] + result[1, at, right]
                        p_r, p_i = probe_ref[mode, 0, rows, side_], probe_ref[mode, 1, rows, side_]
                        g_r = g_r - (p_r * c_r + p_i * c_i)
                        g_i = g_i - (p_r * c_i - p_i * c_r)
                        sums[chunk, 2 * mode, :, side_] += (w_r * c_r + w_i * c_i).reshape(by_chunk)
                        sums[chunk, 2 * mode + 1, :, side_] += (w_r * c_i - w_i * c_r).reshape(by_chunk)
                    back[0, rows, side_] = g_r
                    back[1, rows, side_] = g_i
                    if not number:
                        sums[chunk, 2 * modes, :, side_] += (w_r * w_r + w_i * w_i).reshape(by_chunk)

        for part in range(2):
            rolled = [
                pltpu.roll(back[part, :, pl.ds(block * LANES, LANES)], shift, 1) for block in range(blocks)
            ]
            zero = jnp.zeros((side, LANES), jnp.float32)
            for block in range(blocks + 1):
                here = rolled[block] if block < blocks else zero
                before = rolled[block - 1] if block else zero
                at = strided(block, part)
                gradient[at, :] = gradient[at, :] + jnp.where(lane >= shift, here, before)

    def visit(index, carry):
        inside = place_ref[index, 0] + side <= tile_rows
        pl.when(inside if local else jnp.logical_not(inside))(lambda: slot(index))
        return carry

    lax.fori_loop(0, count_ref[0, 0], visit, 0)


def first_kernel(
    place_ref,
    count_ref,
    tile_hbm,
    probe_ref,
    diffraction_ref,
    table_ref,
    order_ref,
    tile_out,
    gradient,
    sums,
    measured,
    power,
    probe_out,
    table_out,
    window,
    terms,
    result,
    back,
    semaphore,
):
    modes, _, side, _ = probe_ref.shape
    copy = pltpu.make_async_copy(tile_hbm, tile_out, semaphore)
    copy.start()
    gradient[...] = jnp.zeros_like(gradient)
    sums[...] = jnp.zeros_like(sums)
    total = jnp.zeros((side, side), jnp.float32)
    for mode in range(modes):
        total = total + probe_ref[mode, 0] * probe_ref[mode, 0] + probe_ref[mode, 1] * probe_ref[mode, 1]
    power[...] = total
    probe_out[...] = probe_ref[...]
    table_out[...] = table_ref[...]
    move = order_ref[0]

    def order(index, carry):
        seen = moved(diffraction_ref[index], lambda bits: dot(
            jnp.concatenate([order_ref[1]] * 3, axis=1), jnp.concatenate(bits, axis=0)
        ))
        seen = moved(seen, lambda bits: dot(
            jnp.concatenate(bits, axis=1), jnp.concatenate([move] * 3, axis=0)
        ))
        measured[index] = seen.T
        return carry

    lax.fori_loop(0, count_ref[0, 0], order, 0)
    copy.wait()
    all_slots(
        True, tile_out.shape[0] // SUBLANES, place_ref, count_ref, probe_ref, table_ref, tile_out,
        gradient, sums, power, measured, window, terms, result, back,
    )


def second_kernel(
    place_ref,
    count_ref,
    here_ref,
    halo_ref,
    tile_ref,
    gradient_ref,
    sums_ref,
    measured,
    power,
    probe_ref,
    table_ref,
    object_out,
    top_out,
    spill_out,
    mine_out,
    near_out,
    far_out,
    old_out,
    extended,
    gradient,
    sums,
    window,
    terms,
    result,
    back,
):
    modes = probe_ref.shape[0]
    tile_rows, halo_rows, chunks = tile_ref.shape[0], halo_ref.shape[0], sums.shape[0]
    extended[pl.ds(0, tile_rows), :] = tile_ref[...]
    extended[pl.ds(tile_rows, halo_rows), :] = halo_ref[...]
    gradient[pl.ds(0, tile_rows), :] = gradient_ref[...]
    gradient[pl.ds(tile_rows, halo_rows), :] = jnp.zeros((halo_rows, LANES), jnp.float32)
    sums[...] = sums_ref[...]
    scale = 1.0 / jnp.max(power[...])
    all_slots(
        False, tile_rows // SUBLANES, place_ref, count_ref, probe_ref, table_ref, extended,
        gradient, sums, power, measured, window, terms, result, back,
    )
    object_out[...] = extended[pl.ds(0, tile_rows), :] - gradient[pl.ds(0, tile_rows), :] * scale
    top_out[...] = object_out[pl.ds(0, halo_rows), :]
    spill_out[...] = gradient[pl.ds(tile_rows, halo_rows), :] * scale
    core, group, layer = here_ref[0, 0], here_ref[0, 1], here_ref[0, 2]
    groups, layers = mine_out.shape[0], mine_out.shape[1]
    for hop in range(groups):
        for step in range(layers):
            at = (group ^ hop) * layers + lax.rem(layer + step, layers)
            mine_out[hop, step] = sums[core * (chunks // 2) + at]
            if hop < groups - 1:
                near_out[hop, step] = sums[(1 - core) * (chunks // 2) + at]
            else:
                far_out[step] = sums[(1 - core) * (chunks // 2) + at]
    start = pl.multiple_of(((core * groups + group) * layers + layer) * SUBLANES, SUBLANES)
    for mode in range(modes):
        for part in range(2):
            old_out[2 * mode + part] = probe_ref[mode, part, pl.ds(start, SUBLANES), :]


def gradient_step(place, count, here, tile, halo, probe, diffraction, groups, layers):
    modes, parts, side, _ = probe.shape
    planes = parts * modes + 1
    chunks = side // SUBLANES
    f32 = jnp.float32
    smem = pl.BlockSpec(memory_space=pltpu.SMEM)
    vmem = pl.BlockSpec(memory_space=pltpu.VMEM)
    chunk = (planes, SUBLANES, side)
    products = 3 * 16 * modes * diffraction.shape[0] * side**3 // 2
    table, order = jnp.asarray(tables(side)), jnp.asarray(parity_order(side))
    work = [
        pltpu.VMEM((2, side, side), f32),
        pltpu.VMEM((2, modes * side, 2 * side), jnp.bfloat16),
        pltpu.VMEM((2, modes * side, side), f32),
        pltpu.VMEM((2, side, side), f32),
    ]
    shape = jax.ShapeDtypeStruct
    cost = pl.CostEstimate(flops=2 * products, bytes_accessed=16 << 20, transcendentals=0)
    begun = pl.pallas_call(
        first_kernel,
        out_shape=(
            shape(tile.shape, f32),
            shape(tile.shape, f32),
            shape((chunks, *chunk), f32),
            shape(diffraction.shape, f32),
            shape((side, side), f32),
            shape(probe.shape, f32),
            shape(table.shape, table.dtype),
        ),
        in_specs=[smem, smem, pl.BlockSpec(memory_space=pl.ANY), vmem, vmem, vmem, vmem],
        out_specs=(vmem,) * 7,
        scratch_shapes=work + [pltpu.SemaphoreType.DMA],
        compiler_params=pltpu.CompilerParams(vmem_limit_bytes=28 * 1024 * 1024),
        cost_estimate=cost,
        name="slots_inside",
    )(place, count, tile, probe, diffraction, table, order)
    return pl.pallas_call(
        second_kernel,
        out_shape=(
            shape(tile.shape, f32),
            shape(halo.shape, f32),
            shape(halo.shape, f32),
            shape((groups, layers, *chunk), f32),
            shape((groups - 1, layers, *chunk), f32),
            shape((layers, *chunk), f32),
            shape((planes - 1, SUBLANES, side), f32),
        ),
        in_specs=[smem, smem, smem] + [vmem] * 8,
        out_specs=(vmem,) * 7,
        scratch_shapes=[
            pltpu.VMEM((tile.shape[0] + halo.shape[0], LANES), f32),
            pltpu.VMEM((tile.shape[0] + halo.shape[0], LANES), f32),
            pltpu.VMEM((chunks, *chunk), f32),
        ]
        + work,
        compiler_params=pltpu.CompilerParams(vmem_limit_bytes=30 * 1024 * 1024),
        cost_estimate=cost,
        name="slots_across",
    )(place, count, here, halo, *begun)


def first_rows(tile, rows):
    def kernel(tile_ref, out_ref):
        out_ref[...] = tile_ref[...]

    block = pl.BlockSpec((rows // 4, LANES), lambda i: (i, 0))
    return pl.pallas_call(
        kernel,
        grid=(4,),
        out_shape=jax.ShapeDtypeStruct((rows, LANES), jnp.float32),
        in_specs=[block],
        out_specs=block,
        compiler_params=pltpu.CompilerParams(vmem_limit_bytes=62 * 1024 * 1024),
        name="first_rows",
    )(tile)


def divide_kernel(old_ref, *refs):
    *parts, out_ref = refs
    total = parts[0][...]
    for part in parts[1:]:
        total = total + part[...]
    out_ref[...] = (EPSILON * old_ref[...] + total[:-1]) / (total[-1:] + EPSILON)


def divided(old, parts):
    return pl.pallas_call(
        divide_kernel,
        out_shape=jax.ShapeDtypeStruct(old.shape, jnp.float32),
        compiler_params=pltpu.CompilerParams(vmem_limit_bytes=4 * 1024 * 1024),
        name="divided",
    )(old, *parts)


def place_kernel(layers, pieces, here_ref, *refs):
    sources, out, semaphores = refs[: len(pieces)], refs[-2], refs[-1]
    core, group, layer = here_ref[0, 0], here_ref[0, 1], here_ref[0, 2]
    copies = []
    for source, (flip, hop, start) in zip(sources, pieces):
        for j in range(source.shape[0]):
            from_layer = lax.rem(layer + layers - (start + j), layers)
            at = (core ^ flip) * (out.shape[1] // 2) + (group ^ hop) * layers + from_layer
            copies.append(pltpu.make_async_copy(source.at[j], out.at[:, at], semaphores.at[len(copies)]))
    for copy in copies:
        copy.start()
    for copy in copies:
        copy.wait()


def put_in_place(here, layers, pieces, arrays, planes, side, held=None):
    vmem, anywhere = pl.BlockSpec(memory_space=pltpu.VMEM), pl.BlockSpec(memory_space=pl.ANY)
    rest = [] if held is None else [held]
    return pl.pallas_call(
        functools.partial(place_kernel, layers, pieces),
        out_shape=jax.ShapeDtypeStruct((planes, side // SUBLANES, SUBLANES, side), jnp.float32),
        in_specs=[pl.BlockSpec(memory_space=pltpu.SMEM)] + [vmem] * len(arrays) + [anywhere] * len(rest),
        out_specs=anywhere,
        scratch_shapes=[pltpu.SemaphoreType.DMA((sum(array.shape[0] for array in arrays),))],
        input_output_aliases={} if held is None else {1 + len(arrays): 0},
        compiler_params=pltpu.CompilerParams(vmem_limit_bytes=8 * 1024 * 1024),
        cost_estimate=pl.CostEstimate(flops=0, bytes_accessed=4 << 20, transcendentals=0),
        name="put_in_place",
    )(here, *arrays, *rest)


def top_kernel(held_ref, top_ref, arrived_ref, out_ref, rows, semaphore):
    rows[...] = top_ref[...] - arrived_ref[...]
    copy = pltpu.make_async_copy(rows, out_ref.at[pl.ds(0, rows.shape[0])], semaphore)
    copy.start()
    copy.wait()


def with_top(tile, top, arrived):
    vmem, anywhere = pl.BlockSpec(memory_space=pltpu.VMEM), pl.BlockSpec(memory_space=pl.ANY)
    return pl.pallas_call(
        top_kernel,
        out_shape=jax.ShapeDtypeStruct(tile.shape, jnp.float32),
        in_specs=[anywhere, vmem, vmem],
        out_specs=anywhere,
        scratch_shapes=[pltpu.VMEM(top.shape, jnp.float32), pltpu.SemaphoreType.DMA],
        input_output_aliases={0: 0},
        compiler_params=pltpu.CompilerParams(vmem_limit_bytes=8 * 1024 * 1024),
        cost_estimate=pl.CostEstimate(flops=0, bytes_accessed=2 << 20, transcendentals=0),
        name="with_top",
    )(tile, top, arrived)


def across(block, hop):
    return lax.ppermute(block, "group", [(i, i ^ hop) for i in range(lax.axis_size("group"))])


def from_partner(block):
    return lax.ppermute(block, "region", [(i, i ^ 1) for i in range(lax.axis_size("region"))])


def up_layers(block, step):
    regions = lax.axis_size("region")
    return lax.ppermute(block, "region", [(i, (i + 2 * step) % regions) for i in range(regions)])


def probe_by_shards(probe, mine, near, far, old, here, layers, spill):
    modes, parts, side, _ = probe.shape
    planes = modes * parts
    half = layers // 2
    near, other_far = lax.optimization_barrier((near, from_partner(far)))
    other_near = from_partner(near)
    far_sum = mine[3] + other_far
    by_x, by_y = across(far_sum[:half], 1), across(far_sum[half:], 2)
    near_sum = mine[:3] + other_near
    to_x = near_sum[1].at[half:].add(by_y)
    to_y = near_sum[2].at[:half].add(by_x)
    by_x, by_y = across(to_x, 1), across(to_y, 2)
    summed = [near_sum[0, step] + by_x[step] + by_y[step] for step in range(layers)]
    fresh = divided(old, [summed[0]] + [up_layers(summed[step], step) for step in range(1, layers)])
    own = jnp.stack([fresh] + [up_layers(fresh, step) for step in range(1, layers)])
    own, spill = lax.optimization_barrier((own, spill))
    x, y = across(own, 1), across(own, 2)
    arrived = shifted(spill, "region", 1)
    near = [own, x, y]
    near = near + [from_partner(array) for array in near]
    placed = put_in_place(
        here, layers, tuple((flip, hop, 0) for flip in range(2) for hop in range(3)), near, planes, side
    )
    far = [across(x[:half], 2), across(y[half:], 1)]
    far = far + [from_partner(array) for array in far]
    pieces = tuple((flip, 3, start) for flip in range(2) for start in (0, half))
    placed = put_in_place(here, layers, pieces, far, planes, side, placed)
    return placed.reshape(probe.shape), arrived


def probe_from_whole(probe, mine, near, far):
    side = probe.shape[2]
    own = mine.reshape(-1, *mine.shape[2:])
    rest = jnp.concatenate([near.reshape(-1, *near.shape[2:]), far])
    whole = lax.psum(jnp.concatenate([own, rest]), ("region", "group"))
    whole = whole.transpose(1, 0, 2, 3).reshape(-1, side, side)
    old = probe.reshape(-1, side, side)
    return ((EPSILON * old + whole[:-1]) / (whole[-1:] + EPSILON)).reshape(probe.shape)


def on_device(object_slab, probe, diffraction, positions, slot_counts):
    modes, parts, side, _ = probe.shape
    tile_rows, _, columns = object_slab.shape
    regions, groups = lax.axis_size("region"), lax.axis_size("group")
    region, group = lax.axis_index("region"), lax.axis_index("group")
    per_row = parts * columns // LANES
    assert per_row == SUBLANES
    layers = regions // 2
    sharded = groups == 4 and 2 * groups * layers * SUBLANES == side
    tile = packed(object_slab)
    halo = shifted(first_rows(tile, side * per_row), "region", -1)
    place = positions - jnp.stack([region * tile_rows, jnp.zeros_like(region)])[None, :].astype(jnp.int32)
    if sharded:
        here = jnp.stack([region % 2, group, region // 2]).astype(jnp.int32).reshape(1, 3)
    else:
        here = jnp.zeros((1, 3), jnp.int32)
        groups, layers = 4, side // SUBLANES // 8
    new_tile, top, spill, mine, near, far, old = gradient_step(
        place, slot_counts, here, tile, halo, probe, diffraction, groups, layers
    )
    if sharded:
        new_probe, arrived = probe_by_shards(probe, mine, near, far, old, here, layers, spill)
    else:
        arrived = shifted(spill, "region", 1)
        new_probe = probe_from_whole(probe, mine, near, far)
    new_tile = with_top(new_tile, top, arrived)
    return (unpacked(new_tile, object_slab.shape), new_probe)


def solution(mesh):
    placed = (
        P("region", None, "group"),
        P(),
        P(("region", "group"), None, None),
        P(("region", "group"), None),
        P("group", "region"),
    )
    return jax.shard_map(
        on_device,
        mesh=mesh,
        in_specs=placed,
        out_specs=(P("region", None, "group"), P()),
        check_vma=False,
    )
```

```python
import functools
import math

import jax
import jax.numpy as jnp
import numpy as np
from jax import lax
from jax.experimental import pallas as pl
from jax.experimental.pallas import tpu as pltpu
from jax.sharding import PartitionSpec as P

LANES = 128
SUBLANES = 8
ROWS = 32
EPSILON = 1e-06


def shifted(block, axis, distance):
    devices = range(lax.axis_size(axis))
    route = [(i - distance, i) for i in devices if i - distance in devices]
    return lax.ppermute(block, axis, route)


def packed(block):
    rows, parts, columns = block.shape
    cut = block.reshape(rows, parts, columns // LANES, LANES).transpose(0, 2, 1, 3)
    return cut.reshape(rows * parts * columns // LANES, LANES)


def unpacked(block, shape):
    rows, parts, columns = shape
    cut = block.reshape(rows, columns // LANES, parts, LANES).transpose(0, 2, 1, 3)
    return cut.reshape(rows, parts, columns)


def tables(side):
    half = side // 2
    n, q = np.arange(half)[:, None], np.arange(half)[None, :]
    made = []
    for odd in range(2):
        angle = 2.0 * math.pi * ((n * (2 * q + odd)) % side) / side
        re, im = np.cos(angle) / math.sqrt(side), -np.sin(angle) / math.sqrt(side)
        made.append(np.block([[re, im], [-im, re]]))
    exact = np.stack([made[0], made[1], made[0].T, made[1].T]).astype(np.float32)
    high = exact.astype(jnp.bfloat16)
    low = (exact - high.astype(np.float32)).astype(jnp.bfloat16)
    return np.stack([high, low])


def parity_order(side):
    half = side // 2
    order = np.concatenate([np.arange(0, side, 2), np.arange(1, side, 2)])
    move = np.zeros((side, side), np.float32)
    move[order, np.arange(side)] = 1.0
    return np.stack([move, move.T]).astype(jnp.bfloat16)


def split(x):
    high = x.astype(jnp.bfloat16)
    low = (x - high.astype(jnp.float32)).astype(jnp.bfloat16)
    return high, low


def dot(a, b):
    return jnp.dot(a, b, preferred_element_type=jnp.float32)


def transform(terms, rows, table_ref, table, out):
    side = out.shape[2]
    for half in range(2):
        high = terms[half, rows, pl.ds(0, side)]
        low = terms[half, rows, pl.ds(side, side)]
        t_high, t_low = table_ref[0, table + half], table_ref[1, table + half]
        out[half, rows, :] = dot(
            jnp.concatenate([high, low, high], axis=1),
            jnp.concatenate([t_high, t_high, t_low], axis=0),
        )


def keep(terms, half, start, real, imag):
    rows = pl.ds(start, real.shape[0])
    side = 2 * real.shape[1]
    high, low = split(jnp.concatenate([real, imag], axis=1))
    terms[half, rows, pl.ds(0, side)] = high
    terms[half, rows, pl.ds(side, side)] = low


def moved(x, product):
    first, _ = split(x)
    rest = x - first.astype(jnp.float32)
    return product([first, *split(rest)])


def all_slots(
    local,
    tile_rows,
    place_ref,
    count_ref,
    probe_ref,
    table_ref,
    extended,
    gradient,
    sums,
    power,
    measured,
    window,
    terms,
    result,
    back,
):
    modes, _, side, _ = probe_ref.shape
    half = side // 2
    per_row = SUBLANES
    lane = lax.broadcasted_iota(jnp.int32, (side, LANES), 1)
    blocks = side // LANES
    left, right = pl.ds(0, half), pl.ds(half, half)
    pieces = [pl.ds(start, ROWS) for start in range(0, side, ROWS)]
    streams = [range(start, min(start + 2, modes)) for start in range(0, modes, 2)]

    def rows_of(stream):
        return pl.ds(stream[0] * side, len(stream) * side)

    def slot(index):
        row = place_ref[index, 0]
        column = place_ref[index, 1]
        first = column // LANES
        shift = column - first * LANES
        back_shift = lax.rem(LANES - shift, LANES)
        last = per_row // 2 - 1

        def strided(block, part):
            at = row * per_row + jnp.minimum(first + block, last) * 2 + part
            return pl.ds(at, side, stride=per_row)

        for part in range(2):
            rolled = [
                pltpu.roll(extended[strided(block, part), :], back_shift, 1) for block in range(blocks + 1)
            ]
            for block in range(blocks):
                window[part, :, pl.ds(block * LANES, LANES)] = jnp.where(
                    lane < LANES - shift, rolled[block], rolled[block + 1]
                )
        for stream in streams:
            for mode in stream:
                for rows in pieces:
                    w = [window[part, rows, side_] for part in range(2) for side_ in (left, right)]
                    p = [probe_ref[mode, part, rows, side_] for part in range(2) for side_ in (left, right)]
                    real = [p[k] * w[k] - p[2 + k] * w[2 + k] for k in range(2)]
                    imag = [p[k] * w[2 + k] + p[2 + k] * w[k] for k in range(2)]
                    start = mode * side + rows.start
                    keep(terms, 0, start, real[0] + real[1], imag[0] + imag[1])
                    keep(terms, 1, start, real[0] - real[1], imag[0] - imag[1])
            transform(terms, rows_of(stream), table_ref, 0, result)
        for stream in streams:
            for mode in stream:
                for odd in range(2):
                    top, bottom = pl.ds(mode * side, half), pl.ds(mode * side + half, half)
                    a = [result[odd, top, side_] for side_ in (left, right)]
                    b = [result[odd, bottom, side_] for side_ in (left, right)]
                    start = mode * side + odd * half
                    keep(terms, 0, start, (a[0] + b[0]).T, (a[1] + b[1]).T)
                    keep(terms, 1, start, (a[0] - b[0]).T, (a[1] - b[1]).T)
            transform(terms, rows_of(stream), table_ref, 0, result)
        for odd in range(2):
            for rows in pieces:
                far = [
                    [result[odd, pl.ds(mode * side + rows.start, ROWS), side_] for side_ in (left, right)]
                    for mode in range(modes)
                ]
                intensity = jnp.zeros((ROWS, half), jnp.float32)
                for real, imag in far:
                    intensity = intensity + real * real + imag * imag
                amount = measured[index, rows, pl.ds(odd * half, half)]
                ratio = amount * lax.rsqrt(amount * jnp.maximum(intensity, 1.0))
                for mode, (real, imag) in enumerate(far):
                    keep(terms, odd, mode * side + rows.start, real * ratio, imag * ratio)
        for stream in streams:
            transform(terms, rows_of(stream), table_ref, 2, result)
        for stream in streams:
            for mode in stream:
                for odd in range(2):
                    rows = pl.ds(mode * side + odd * half, half)
                    a = [result[0, rows, side_] for side_ in (left, right)]
                    b = [result[1, rows, side_] for side_ in (left, right)]
                    start = mode * side
                    keep(terms, odd, start, (a[0] + b[0]).T, (a[1] + b[1]).T)
                    keep(terms, odd, start + half, (a[0] - b[0]).T, (a[1] - b[1]).T)
            transform(terms, rows_of(stream), table_ref, 2, result)
        for number, stream in enumerate(streams):
            for rows in pieces:
                chunk = pl.ds(rows.start // SUBLANES, ROWS // SUBLANES)
                by_chunk = (ROWS // SUBLANES, SUBLANES, half)
                for lower, side_ in enumerate((left, right)):
                    w_r, w_i = window[0, rows, side_], window[1, rows, side_]
                    if number:
                        g_r, g_i = back[0, rows, side_], back[1, rows, side_]
                    else:
                        strength = power[rows, side_]
                        g_r, g_i = strength * w_r, strength * w_i
                    for mode in stream:
                        at = pl.ds(mode * side + rows.start, ROWS)
                        if lower:
                            c_r = result[0, at, left] - result[1, at, left]
                            c_i = result[0, at, right] - result[1, at, right]
                        else:
                            c_r = result[0, at, left] + result[1, at, left]
                            c_i = result[0, at, right] + result[1, at, right]
                        p_r, p_i = probe_ref[mode, 0, rows, side_], probe_ref[mode, 1, rows, side_]
                        g_r = g_r - (p_r * c_r + p_i * c_i)
                        g_i = g_i - (p_r * c_i - p_i * c_r)
                        sums[chunk, 2 * mode, :, side_] += (w_r * c_r + w_i * c_i).reshape(by_chunk)
                        sums[chunk, 2 * mode + 1, :, side_] += (w_r * c_i - w_i * c_r).reshape(by_chunk)
                    back[0, rows, side_] = g_r
                    back[1, rows, side_] = g_i
                    if not number:
                        sums[chunk, 2 * modes, :, side_] += (w_r * w_r + w_i * w_i).reshape(by_chunk)

        for part in range(2):
            rolled = [
                pltpu.roll(back[part, :, pl.ds(block * LANES, LANES)], shift, 1) for block in range(blocks)
            ]
            zero = jnp.zeros((side, LANES), jnp.float32)
            for block in range(blocks + 1):
                here = rolled[block] if block < blocks else zero
                before = rolled[block - 1] if block else zero
                at = strided(block, part)
                gradient[at, :] = gradient[at, :] + jnp.where(lane >= shift, here, before)

    def visit(index, carry):
        inside = place_ref[index, 0] + side <= tile_rows
        pl.when(inside if local else jnp.logical_not(inside))(lambda: slot(index))
        return carry

    lax.fori_loop(0, count_ref[0, 0], visit, 0)


def first_kernel(
    place_ref,
    count_ref,
    tile_hbm,
    probe_ref,
    diffraction_ref,
    table_ref,
    order_ref,
    tile_out,
    gradient,
    sums,
    measured,
    power,
    probe_out,
    table_out,
    scale_out,
    window,
    terms,
    result,
    back,
    semaphore,
):
    modes, _, side, _ = probe_ref.shape
    copy = pltpu.make_async_copy(tile_hbm, tile_out, semaphore)
    copy.start()
    gradient[...] = jnp.zeros_like(gradient)
    sums[...] = jnp.zeros_like(sums)
    total = jnp.zeros((side, side), jnp.float32)
    for mode in range(modes):
        total = total + probe_ref[mode, 0] * probe_ref[mode, 0] + probe_ref[mode, 1] * probe_ref[mode, 1]
    power[...] = total
    scale_out[...] = jnp.full(scale_out.shape, 1.0 / jnp.max(total))
    probe_out[...] = probe_ref[...]
    table_out[...] = table_ref[...]
    move = order_ref[0]

    def order(index, carry):
        seen = moved(diffraction_ref[index], lambda bits: dot(
            jnp.concatenate([order_ref[1]] * 3, axis=1), jnp.concatenate(bits, axis=0)
        ))
        seen = moved(seen, lambda bits: dot(
            jnp.concatenate(bits, axis=1), jnp.concatenate([move] * 3, axis=0)
        ))
        measured[index] = seen.T
        return carry

    lax.fori_loop(0, count_ref[0, 0], order, 0)
    copy.wait()
    all_slots(
        True, tile_out.shape[0] // SUBLANES, place_ref, count_ref, probe_ref, table_ref, tile_out,
        gradient, sums, power, measured, window, terms, result, back,
    )


def second_kernel(
    place_ref,
    count_ref,
    here_ref,
    halo_ref,
    tile_ref,
    gradient_ref,
    sums_ref,
    measured,
    power,
    probe_ref,
    table_ref,
    gradient,
    spill_out,
    mine_out,
    near_out,
    far_out,
    old_out,
    extended,
    sums,
    window,
    terms,
    result,
    back,
):
    modes = probe_ref.shape[0]
    tile_rows, halo_rows, chunks = tile_ref.shape[0], halo_ref.shape[0], sums.shape[0]
    extended[pl.ds(0, tile_rows), :] = tile_ref[...]
    extended[pl.ds(tile_rows, halo_rows), :] = halo_ref[...]
    gradient[pl.ds(0, tile_rows), :] = gradient_ref[...]
    gradient[pl.ds(tile_rows, halo_rows), :] = jnp.zeros((halo_rows, LANES), jnp.float32)
    sums[...] = sums_ref[...]
    all_slots(
        False, tile_rows // SUBLANES, place_ref, count_ref, probe_ref, table_ref, extended,
        gradient, sums, power, measured, window, terms, result, back,
    )
    spill_out[...] = gradient[pl.ds(tile_rows, halo_rows), :]
    core, group, layer = here_ref[0, 0], here_ref[0, 1], here_ref[0, 2]
    groups, layers = mine_out.shape[0], mine_out.shape[1]
    for hop in range(groups):
        for step in range(layers):
            at = (group ^ hop) * layers + lax.rem(layer + step, layers)
            mine_out[hop, step] = sums[core * (chunks // 2) + at]
            if hop < groups - 1:
                near_out[hop, step] = sums[(1 - core) * (chunks // 2) + at]
            else:
                far_out[step] = sums[(1 - core) * (chunks // 2) + at]
    start = pl.multiple_of(((core * groups + group) * layers + layer) * SUBLANES, SUBLANES)
    for mode in range(modes):
        for part in range(2):
            old_out[2 * mode + part] = probe_ref[mode, part, pl.ds(start, SUBLANES), :]


def gradient_step(place, count, here, tile, halo, probe, diffraction, groups, layers):
    modes, parts, side, _ = probe.shape
    planes = parts * modes + 1
    chunks = side // SUBLANES
    f32 = jnp.float32
    smem = pl.BlockSpec(memory_space=pltpu.SMEM)
    vmem = pl.BlockSpec(memory_space=pltpu.VMEM)
    chunk = (planes, SUBLANES, side)
    products = 3 * 16 * modes * diffraction.shape[0] * side**3 // 2
    table, order = jnp.asarray(tables(side)), jnp.asarray(parity_order(side))
    work = [
        pltpu.VMEM((2, side, side), f32),
        pltpu.VMEM((2, modes * side, 2 * side), jnp.bfloat16),
        pltpu.VMEM((2, modes * side, side), f32),
        pltpu.VMEM((2, side, side), f32),
    ]
    shape = jax.ShapeDtypeStruct
    cost = pl.CostEstimate(flops=2 * products, bytes_accessed=16 << 20, transcendentals=0)
    *begun, scale = pl.pallas_call(
        first_kernel,
        out_shape=(
            shape(tile.shape, f32),
            shape(tile.shape, f32),
            shape((chunks, *chunk), f32),
            shape(diffraction.shape, f32),
            shape((side, side), f32),
            shape(probe.shape, f32),
            shape(table.shape, table.dtype),
            shape((1, LANES), f32),
        ),
        in_specs=[smem, smem, pl.BlockSpec(memory_space=pl.ANY), vmem, vmem, vmem, vmem],
        out_specs=(vmem,) * 8,
        scratch_shapes=work + [pltpu.SemaphoreType.DMA],
        compiler_params=pltpu.CompilerParams(vmem_limit_bytes=28 * 1024 * 1024),
        cost_estimate=cost,
        name="slots_inside",
    )(place, count, tile, probe, diffraction, table, order)
    gradient, *rest = pl.pallas_call(
        second_kernel,
        out_shape=(
            shape((tile.shape[0] + halo.shape[0], LANES), f32),
            shape(halo.shape, f32),
            shape((groups, layers, *chunk), f32),
            shape((groups - 1, layers, *chunk), f32),
            shape((layers, *chunk), f32),
            shape((planes - 1, SUBLANES, side), f32),
        ),
        in_specs=[smem, smem, smem] + [vmem] * 8,
        out_specs=(vmem,) * 6,
        scratch_shapes=[
            pltpu.VMEM((tile.shape[0] + halo.shape[0], LANES), f32),
            pltpu.VMEM((chunks, *chunk), f32),
        ]
        + work,
        compiler_params=pltpu.CompilerParams(vmem_limit_bytes=30 * 1024 * 1024),
        cost_estimate=cost,
        name="slots_across",
    )(place, count, here, halo, *begun)
    new_tile, top = written(begun[0], gradient, scale, halo.shape[0])
    return new_tile, top, scale, *rest


def write_kernel(tile_ref, gradient_ref, scale_ref, out_ref, top_ref, rows, semaphores):
    scale = scale_ref[...]
    step = out_ref.shape[0] // 4
    copies = []
    for part in range(4):
        at = pl.ds(part * step, step)
        rows[at, :] = tile_ref[at, :] - gradient_ref[at, :] * scale
        copies.append(pltpu.make_async_copy(rows.at[at], out_ref.at[at], semaphores.at[part]))
        copies[-1].start()
    top_ref[...] = rows[pl.ds(0, top_ref.shape[0]), :]
    for copy in copies:
        copy.wait()


def written(tile, gradient, scale, top_rows):
    vmem, anywhere = pl.BlockSpec(memory_space=pltpu.VMEM), pl.BlockSpec(memory_space=pl.ANY)
    return pl.pallas_call(
        write_kernel,
        out_shape=(
            jax.ShapeDtypeStruct(tile.shape, jnp.float32),
            jax.ShapeDtypeStruct((top_rows, LANES), jnp.float32),
        ),
        in_specs=[vmem, vmem, vmem],
        out_specs=(anywhere, vmem),
        scratch_shapes=[pltpu.VMEM(tile.shape, jnp.float32), pltpu.SemaphoreType.DMA((4,))],
        compiler_params=pltpu.CompilerParams(vmem_limit_bytes=10 * 1024 * 1024),
        cost_estimate=pl.CostEstimate(flops=0, bytes_accessed=4 << 20, transcendentals=0),
        name="written",
    )(tile, gradient, scale)


def first_rows(tile, rows):
    def kernel(tile_ref, out_ref, semaphore):
        copy = pltpu.make_async_copy(tile_ref.at[pl.ds(0, rows)], out_ref, semaphore)
        copy.start()
        copy.wait()

    return pl.pallas_call(
        kernel,
        out_shape=jax.ShapeDtypeStruct((rows, LANES), jnp.float32),
        in_specs=[pl.BlockSpec(memory_space=pl.ANY)],
        out_specs=pl.BlockSpec(memory_space=pltpu.VMEM),
        scratch_shapes=[pltpu.SemaphoreType.DMA],
        compiler_params=pltpu.CompilerParams(vmem_limit_bytes=4 * 1024 * 1024),
        name="first_rows",
    )(tile)


def divide_kernel(old_ref, *refs):
    *parts, out_ref = refs
    total = parts[0][...]
    for part in parts[1:]:
        total = total + part[...]
    out_ref[...] = (EPSILON * old_ref[...] + total[:-1]) / (total[-1:] + EPSILON)


def divided(old, parts):
    return pl.pallas_call(
        divide_kernel,
        out_shape=jax.ShapeDtypeStruct(old.shape, jnp.float32),
        compiler_params=pltpu.CompilerParams(vmem_limit_bytes=4 * 1024 * 1024),
        name="divided",
    )(old, *parts)


def place_kernel(layers, pieces, here_ref, *refs):
    sources, out, semaphores = refs[: len(pieces)], refs[-2], refs[-1]
    core, group, layer = here_ref[0, 0], here_ref[0, 1], here_ref[0, 2]
    copies = []
    for source, (flip, hop, start) in zip(sources, pieces):
        for j in range(source.shape[0]):
            from_layer = lax.rem(layer + layers - (start + j), layers)
            at = (core ^ flip) * (out.shape[1] // 2) + (group ^ hop) * layers + from_layer
            copies.append(pltpu.make_async_copy(source.at[j], out.at[:, at], semaphores.at[len(copies)]))
    for copy in copies:
        copy.start()
    for copy in copies:
        copy.wait()


def put_in_place(here, layers, pieces, arrays, planes, side, held=None):
    vmem, anywhere = pl.BlockSpec(memory_space=pltpu.VMEM), pl.BlockSpec(memory_space=pl.ANY)
    rest = [] if held is None else [held]
    return pl.pallas_call(
        functools.partial(place_kernel, layers, pieces),
        out_shape=jax.ShapeDtypeStruct((planes, side // SUBLANES, SUBLANES, side), jnp.float32),
        in_specs=[pl.BlockSpec(memory_space=pltpu.SMEM)] + [vmem] * len(arrays) + [anywhere] * len(rest),
        out_specs=anywhere,
        scratch_shapes=[pltpu.SemaphoreType.DMA((sum(array.shape[0] for array in arrays),))],
        input_output_aliases={} if held is None else {1 + len(arrays): 0},
        compiler_params=pltpu.CompilerParams(vmem_limit_bytes=8 * 1024 * 1024),
        cost_estimate=pl.CostEstimate(flops=0, bytes_accessed=4 << 20, transcendentals=0),
        name="put_in_place",
    )(here, *arrays, *rest)


def top_kernel(held_ref, top_ref, arrived_ref, scale_ref, out_ref, rows, semaphore):
    rows[...] = top_ref[...] - arrived_ref[...] * scale_ref[...]
    copy = pltpu.make_async_copy(rows, out_ref.at[pl.ds(0, rows.shape[0])], semaphore)
    copy.start()
    copy.wait()


def with_top(tile, top, arrived, scale):
    vmem, anywhere = pl.BlockSpec(memory_space=pltpu.VMEM), pl.BlockSpec(memory_space=pl.ANY)
    return pl.pallas_call(
        top_kernel,
        out_shape=jax.ShapeDtypeStruct(tile.shape, jnp.float32),
        in_specs=[anywhere, vmem, vmem, vmem],
        out_specs=anywhere,
        scratch_shapes=[pltpu.VMEM(top.shape, jnp.float32), pltpu.SemaphoreType.DMA],
        input_output_aliases={0: 0},
        compiler_params=pltpu.CompilerParams(vmem_limit_bytes=8 * 1024 * 1024),
        cost_estimate=pl.CostEstimate(flops=0, bytes_accessed=2 << 20, transcendentals=0),
        name="with_top",
    )(tile, top, arrived, scale)


def across(block, hop):
    return lax.ppermute(block, "group", [(i, i ^ hop) for i in range(lax.axis_size("group"))])


def from_partner(block):
    return lax.ppermute(block, "region", [(i, i ^ 1) for i in range(lax.axis_size("region"))])


def up_layers(block, step):
    regions = lax.axis_size("region")
    return lax.ppermute(block, "region", [(i, (i + 2 * step) % regions) for i in range(regions)])


def probe_by_shards(probe, mine, near, far, old, here, layers, spill, new_tile, top, scale):
    modes, parts, side, _ = probe.shape
    planes = modes * parts
    half = layers // 2
    near, other_far = lax.optimization_barrier((near, from_partner(far)))
    other_near, spill = lax.optimization_barrier((from_partner(near), spill))
    arrived = shifted(spill, "region", 1)
    far_sum = mine[3] + other_far
    by_x, by_y = across(far_sum[:half], 1), across(far_sum[half:], 2)
    near_sum = mine[:3] + other_near
    to_x = near_sum[1].at[half:].add(by_y)
    to_y = near_sum[2].at[:half].add(by_x)
    by_x, by_y, arrived, new_tile, top = lax.optimization_barrier(
        (across(to_x, 1), across(to_y, 2), arrived, new_tile, top)
    )
    new_tile = with_top(new_tile, top, arrived, scale)
    summed = [near_sum[0, step] + by_x[step] + by_y[step] for step in range(layers)]
    fresh = divided(old, [summed[0]] + [up_layers(summed[step], step) for step in range(1, layers)])
    *others, new_tile = lax.optimization_barrier(
        (*[up_layers(fresh, step) for step in range(1, layers)], new_tile)
    )
    own = jnp.stack([fresh] + others)
    x, y = across(own, 1), across(own, 2)
    near = [own, x, y]
    placed = put_in_place(here, layers, tuple((0, hop, 0) for hop in range(3)), near, planes, side)
    far = [across(x[:half], 2), across(y[half:], 1)]
    *far, placed = lax.optimization_barrier((*far, placed))
    near = [from_partner(array) for array in near]
    placed = put_in_place(here, layers, tuple((1, hop, 0) for hop in range(3)), near, planes, side, placed)
    far = far + [from_partner(array) for array in far]
    pieces = tuple((flip, 3, start) for flip in range(2) for start in (0, half))
    placed = put_in_place(here, layers, pieces, far, planes, side, placed)
    return placed.reshape(probe.shape), new_tile


def probe_from_whole(probe, mine, near, far):
    side = probe.shape[2]
    own = mine.reshape(-1, *mine.shape[2:])
    rest = jnp.concatenate([near.reshape(-1, *near.shape[2:]), far])
    whole = lax.psum(jnp.concatenate([own, rest]), ("region", "group"))
    whole = whole.transpose(1, 0, 2, 3).reshape(-1, side, side)
    old = probe.reshape(-1, side, side)
    return ((EPSILON * old + whole[:-1]) / (whole[-1:] + EPSILON)).reshape(probe.shape)


def on_device(object_slab, probe, diffraction, positions, slot_counts):
    modes, parts, side, _ = probe.shape
    tile_rows, _, columns = object_slab.shape
    regions, groups = lax.axis_size("region"), lax.axis_size("group")
    region, group = lax.axis_index("region"), lax.axis_index("group")
    per_row = parts * columns // LANES
    assert per_row == SUBLANES
    layers = regions // 2
    sharded = groups == 4 and 2 * groups * layers * SUBLANES == side
    tile = packed(object_slab)
    halo = shifted(first_rows(tile, side * per_row), "region", -1)
    place = positions - jnp.stack([region * tile_rows, jnp.zeros_like(region)])[None, :].astype(jnp.int32)
    if sharded:
        here = jnp.stack([region % 2, group, region // 2]).astype(jnp.int32).reshape(1, 3)
    else:
        here = jnp.zeros((1, 3), jnp.int32)
        groups, layers = 4, side // SUBLANES // 8
    new_tile, top, scale, spill, mine, near, far, old = gradient_step(
        place, slot_counts, here, tile, halo, probe, diffraction, groups, layers
    )
    if sharded:
        new_probe, new_tile = probe_by_shards(
            probe, mine, near, far, old, here, layers, spill, new_tile, top, scale
        )
    else:
        new_tile = with_top(new_tile, top, shifted(spill, "region", 1), scale)
        new_probe = probe_from_whole(probe, mine, near, far)
    return (unpacked(new_tile, object_slab.shape), new_probe)


def solution(mesh):
    placed = (
        P("region", None, "group"),
        P(),
        P(("region", "group"), None, None),
        P(("region", "group"), None),
        P("group", "region"),
    )
    return jax.shard_map(
        on_device,
        mesh=mesh,
        in_specs=placed,
        out_specs=(P("region", None, "group"), P()),
        check_vma=False,
    )
```

```python
import functools
import math

import jax
import jax.numpy as jnp
import numpy as np
from jax import lax
from jax.experimental import pallas as pl
from jax.experimental.pallas import tpu as pltpu
from jax.sharding import PartitionSpec as P

LANES = 128
SUBLANES = 8
ROWS = 32
STREAM = 4
EPSILON = 1e-06


def shifted(block, axis, distance):
    devices = range(lax.axis_size(axis))
    route = [(i - distance, i) for i in devices if i - distance in devices]
    return lax.ppermute(block, axis, route)


def packed(block):
    rows, parts, columns = block.shape
    cut = block.reshape(rows, parts, columns // LANES, LANES).transpose(0, 2, 1, 3)
    return cut.reshape(rows * parts * columns // LANES, LANES)


def unpacked(block, shape):
    rows, parts, columns = shape
    cut = block.reshape(rows, columns // LANES, parts, LANES).transpose(0, 2, 1, 3)
    return cut.reshape(rows, parts, columns)


def tables(side):
    half = side // 2
    n, q = np.arange(half)[:, None], np.arange(half)[None, :]
    made = []
    for odd in range(2):
        angle = 2.0 * math.pi * ((n * (2 * q + odd)) % side) / side
        made += [np.cos(angle) / math.sqrt(side), -np.sin(angle) / math.sqrt(side)]
    return np.stack(made).astype(np.float32)


def fill_table(factor_ref, table_ref):
    half = factor_ref.shape[1]
    left, right = pl.ds(0, half), pl.ds(half, half)
    for odd in range(2):
        for turned in range(2):
            real, imag = factor_ref[2 * odd], factor_ref[2 * odd + 1]
            if turned:
                real, imag = real.T, -imag.T
            for term, (re, im, minus) in enumerate(zip(split(real), split(imag), split(-imag))):
                entry = 2 * turned + odd
                table_ref[term, entry, left, left] = re
                table_ref[term, entry, left, right] = im
                table_ref[term, entry, right, left] = minus
                table_ref[term, entry, right, right] = re


def parity_order(side):
    half = side // 2
    first = lax.broadcasted_iota(jnp.int32, (side, side), 0)
    second = lax.broadcasted_iota(jnp.int32, (side, side), 1)

    def moves(source, place):
        odd = (place >= half).astype(jnp.int32)
        hit = source == 2 * (place - odd * half) + odd
        return hit.astype(jnp.float32).astype(jnp.bfloat16)

    return moves(first, second), moves(second, first)


def split(x):
    high = x.astype(jnp.bfloat16)
    low = (x - high.astype(jnp.float32)).astype(jnp.bfloat16)
    return high, low


def dot(a, b):
    return jnp.dot(a, b, preferred_element_type=jnp.float32)


def transform(terms, rows, table_ref, table, out):
    side = out.shape[2]
    for half in range(2):
        high = terms[half, rows, pl.ds(0, side)]
        low = terms[half, rows, pl.ds(side, side)]
        t_high, t_low = table_ref[0, table + half], table_ref[1, table + half]
        out[half, rows, :] = dot(
            jnp.concatenate([high, low, high], axis=1),
            jnp.concatenate([t_high, t_high, t_low], axis=0),
        )


def keep(terms, half, start, real, imag):
    rows = pl.ds(start, real.shape[0])
    side = 2 * real.shape[1]
    high, low = split(jnp.concatenate([real, imag], axis=1))
    terms[half, rows, pl.ds(0, side)] = high
    terms[half, rows, pl.ds(side, side)] = low


def all_slots(
    local,
    tile_rows,
    place_ref,
    count_ref,
    probe_ref,
    table_ref,
    extended,
    gradient,
    sums,
    power,
    measured,
    window,
    terms,
    result,
    back,
):
    modes, _, side, _ = probe_ref.shape
    half = side // 2
    per_row = SUBLANES
    lane = lax.broadcasted_iota(jnp.int32, (side, LANES), 1)
    blocks = side // LANES
    left, right = pl.ds(0, half), pl.ds(half, half)
    pieces = [pl.ds(start, ROWS) for start in range(0, side, ROWS)]
    streams = [range(start, min(start + STREAM, modes)) for start in range(0, modes, STREAM)]

    def rows_of(stream):
        return pl.ds(stream[0] * side, len(stream) * side)

    def slot(index):
        row = place_ref[index, 0]
        column = place_ref[index, 1]
        first = column // LANES
        shift = column - first * LANES
        back_shift = lax.rem(LANES - shift, LANES)
        last = per_row // 2 - 1

        def strided(block, part):
            at = row * per_row + jnp.minimum(first + block, last) * 2 + part
            return pl.ds(at, side, stride=per_row)

        for part in range(2):
            rolled = [
                pltpu.roll(extended[strided(block, part), :], back_shift, 1) for block in range(blocks + 1)
            ]
            for block in range(blocks):
                window[part, :, pl.ds(block * LANES, LANES)] = jnp.where(
                    lane < LANES - shift, rolled[block], rolled[block + 1]
                )
        for stream in streams:
            for mode in stream:
                for rows in pieces:
                    w = [window[part, rows, side_] for part in range(2) for side_ in (left, right)]
                    p = [probe_ref[mode, part, rows, side_] for part in range(2) for side_ in (left, right)]
                    real = [p[k] * w[k] - p[2 + k] * w[2 + k] for k in range(2)]
                    imag = [p[k] * w[2 + k] + p[2 + k] * w[k] for k in range(2)]
                    start = mode * side + rows.start
                    keep(terms, 0, start, real[0] + real[1], imag[0] + imag[1])
                    keep(terms, 1, start, real[0] - real[1], imag[0] - imag[1])
            transform(terms, rows_of(stream), table_ref, 0, result)
        for stream in streams:
            for mode in stream:
                for odd in range(2):
                    top, bottom = pl.ds(mode * side, half), pl.ds(mode * side + half, half)
                    a = [result[odd, top, side_] for side_ in (left, right)]
                    b = [result[odd, bottom, side_] for side_ in (left, right)]
                    start = mode * side + odd * half
                    keep(terms, 0, start, (a[0] + b[0]).T, (a[1] + b[1]).T)
                    keep(terms, 1, start, (a[0] - b[0]).T, (a[1] - b[1]).T)
            transform(terms, rows_of(stream), table_ref, 0, result)
        for odd in range(2):
            for rows in pieces:
                far = [
                    [result[odd, pl.ds(mode * side + rows.start, ROWS), side_] for side_ in (left, right)]
                    for mode in range(modes)
                ]
                intensity = jnp.zeros((ROWS, half), jnp.float32)
                for real, imag in far:
                    intensity = intensity + real * real + imag * imag
                amount = measured[index, rows, pl.ds(odd * half, half)]
                ratio = amount * lax.rsqrt(amount * jnp.maximum(intensity, 1.0))
                for mode, (real, imag) in enumerate(far):
                    keep(terms, odd, mode * side + rows.start, real * ratio, imag * ratio)
        for stream in streams:
            transform(terms, rows_of(stream), table_ref, 2, result)
        for stream in streams:
            for mode in stream:
                for odd in range(2):
                    rows = pl.ds(mode * side + odd * half, half)
                    a = [result[0, rows, side_] for side_ in (left, right)]
                    b = [result[1, rows, side_] for side_ in (left, right)]
                    start = mode * side
                    keep(terms, odd, start, (a[0] + b[0]).T, (a[1] + b[1]).T)
                    keep(terms, odd, start + half, (a[0] - b[0]).T, (a[1] - b[1]).T)
            transform(terms, rows_of(stream), table_ref, 2, result)
        for number, stream in enumerate(streams):
            for rows in pieces:
                chunk = pl.ds(rows.start // SUBLANES, ROWS // SUBLANES)
                by_chunk = (ROWS // SUBLANES, SUBLANES, half)
                for lower, side_ in enumerate((left, right)):
                    w_r, w_i = window[0, rows, side_], window[1, rows, side_]
                    if number:
                        g_r, g_i = back[0, rows, side_], back[1, rows, side_]
                    else:
                        strength = power[rows, side_]
                        g_r, g_i = strength * w_r, strength * w_i
                    for mode in stream:
                        at = pl.ds(mode * side + rows.start, ROWS)
                        if lower:
                            c_r = result[0, at, left] - result[1, at, left]
                            c_i = result[0, at, right] - result[1, at, right]
                        else:
                            c_r = result[0, at, left] + result[1, at, left]
                            c_i = result[0, at, right] + result[1, at, right]
                        p_r, p_i = probe_ref[mode, 0, rows, side_], probe_ref[mode, 1, rows, side_]
                        g_r = g_r - (p_r * c_r + p_i * c_i)
                        g_i = g_i - (p_r * c_i - p_i * c_r)
                        sums[chunk, 2 * mode, :, side_] += (w_r * c_r + w_i * c_i).reshape(by_chunk)
                        sums[chunk, 2 * mode + 1, :, side_] += (w_r * c_i - w_i * c_r).reshape(by_chunk)
                    back[0, rows, side_] = g_r
                    back[1, rows, side_] = g_i
                    if not number:
                        sums[chunk, 2 * modes, :, side_] += (w_r * w_r + w_i * w_i).reshape(by_chunk)

        for part in range(2):
            rolled = [
                pltpu.roll(back[part, :, pl.ds(block * LANES, LANES)], shift, 1) for block in range(blocks)
            ]
            zero = jnp.zeros((side, LANES), jnp.float32)
            for block in range(blocks + 1):
                here = rolled[block] if block < blocks else zero
                before = rolled[block - 1] if block else zero
                at = strided(block, part)
                gradient[at, :] = gradient[at, :] + jnp.where(lane >= shift, here, before)

    def visit(index, carry):
        inside = place_ref[index, 0] + side <= tile_rows
        pl.when(inside if local else jnp.logical_not(inside))(lambda: slot(index))
        return carry

    lax.fori_loop(0, count_ref[0, 0], visit, 0)


def first_kernel(
    place_ref,
    count_ref,
    tile_hbm,
    probe_ref,
    diffraction_ref,
    factor_ref,
    tile_out,
    gradient,
    sums,
    measured,
    power,
    probe_out,
    table_out,
    scale_out,
    window,
    terms,
    result,
    back,
    semaphore,
):
    modes, _, side, _ = probe_ref.shape
    copy = pltpu.make_async_copy(tile_hbm, tile_out, semaphore)
    copy.start()
    gradient[...] = jnp.zeros_like(gradient)
    sums[...] = jnp.zeros_like(sums)
    total = jnp.zeros((side, side), jnp.float32)
    for mode in range(modes):
        total = total + probe_ref[mode, 0] * probe_ref[mode, 0] + probe_ref[mode, 1] * probe_ref[mode, 1]
    power[...] = total
    scale_out[...] = jnp.full(scale_out.shape, 1.0 / jnp.max(total))
    probe_out[...] = probe_ref[...]
    fill_table(factor_ref, table_out)
    by_lanes, by_rows = parity_order(side)

    def order(index, carry):
        high, low = split(diffraction_ref[index])
        seen = dot(jnp.concatenate([by_rows] * 2, axis=1), jnp.concatenate([high, low], axis=0))
        high, low = split(seen)
        seen = dot(jnp.concatenate([high, low], axis=1), jnp.concatenate([by_lanes] * 2, axis=0))
        measured[index] = seen.T
        return carry

    lax.fori_loop(0, count_ref[0, 0], order, 0)
    copy.wait()
    all_slots(
        True, tile_out.shape[0] // SUBLANES, place_ref, count_ref, probe_ref, table_out, tile_out,
        gradient, sums, power, measured, window, terms, result, back,
    )


def second_kernel(
    place_ref,
    count_ref,
    here_ref,
    halo_ref,
    tile_ref,
    gradient_ref,
    sums_ref,
    measured,
    power,
    probe_ref,
    table_ref,
    gradient,
    spill_out,
    more_out,
    mine_out,
    near_out,
    far_out,
    old_out,
    extended,
    sums,
    window,
    terms,
    result,
    back,
):
    modes = probe_ref.shape[0]
    tile_rows, halo_rows, chunks = tile_ref.shape[0], halo_ref.shape[0], sums.shape[0]
    extended[pl.ds(0, tile_rows), :] = tile_ref[...]
    extended[pl.ds(tile_rows, halo_rows), :] = halo_ref[...]
    gradient[pl.ds(0, tile_rows), :] = gradient_ref[...]
    gradient[pl.ds(tile_rows, halo_rows), :] = jnp.zeros((halo_rows, LANES), jnp.float32)
    sums[...] = sums_ref[...]
    all_slots(
        False, tile_rows // SUBLANES, place_ref, count_ref, probe_ref, table_ref, extended,
        gradient, sums, power, measured, window, terms, result, back,
    )
    part = spill_out.shape[0]
    spill_out[...] = gradient[pl.ds(tile_rows, part), :]
    more_out[...] = gradient[pl.ds(tile_rows + part, halo_rows - part), :]
    core, group, layer = here_ref[0, 0], here_ref[0, 1], here_ref[0, 2]
    groups, layers = mine_out.shape[0], mine_out.shape[1]
    for hop in range(groups):
        for step in range(layers):
            at = (group ^ hop) * layers + lax.rem(layer + step, layers)
            mine_out[hop, step] = sums[core * (chunks // 2) + at]
            if hop < groups - 1:
                near_out[hop, step] = sums[(1 - core) * (chunks // 2) + at]
            else:
                far_out[step] = sums[(1 - core) * (chunks // 2) + at]
    start = pl.multiple_of(((core * groups + group) * layers + layer) * SUBLANES, SUBLANES)
    for mode in range(modes):
        for part in range(2):
            old_out[2 * mode + part] = probe_ref[mode, part, pl.ds(start, SUBLANES), :]


def gradient_step(place, count, here, tile, halo, probe, diffraction, groups, layers):
    modes, parts, side, _ = probe.shape
    planes = parts * modes + 1
    chunks = side // SUBLANES
    f32 = jnp.float32
    smem = pl.BlockSpec(memory_space=pltpu.SMEM)
    vmem = pl.BlockSpec(memory_space=pltpu.VMEM)
    chunk = (planes, SUBLANES, side)
    products = 3 * 16 * modes * diffraction.shape[0] * side**3 // 2
    work = [
        pltpu.VMEM((2, side, side), f32),
        pltpu.VMEM((2, modes * side, 2 * side), jnp.bfloat16),
        pltpu.VMEM((2, modes * side, side), f32),
        pltpu.VMEM((2, side, side), f32),
    ]
    shape = jax.ShapeDtypeStruct
    cost = pl.CostEstimate(flops=2 * products, bytes_accessed=16 << 20, transcendentals=0)
    *begun, scale = pl.pallas_call(
        first_kernel,
        out_shape=(
            shape(tile.shape, f32),
            shape(tile.shape, f32),
            shape((chunks, *chunk), f32),
            shape(diffraction.shape, f32),
            shape((side, side), f32),
            shape(probe.shape, f32),
            shape((2, 4, side, side), jnp.bfloat16),
            shape((1, LANES), f32),
        ),
        in_specs=[smem, smem, pl.BlockSpec(memory_space=pl.ANY), vmem, vmem, vmem],
        out_specs=(vmem,) * 8,
        scratch_shapes=work + [pltpu.SemaphoreType.DMA],
        compiler_params=pltpu.CompilerParams(vmem_limit_bytes=28 * 1024 * 1024),
        cost_estimate=cost,
        name="slots_inside",
    )(place, count, tile, probe, diffraction, jnp.asarray(tables(side)))
    gradient, *rest = pl.pallas_call(
        second_kernel,
        out_shape=(
            shape((tile.shape[0] + halo.shape[0], LANES), f32),
            shape((halo.shape[0] // 4 * 3, LANES), f32),
            shape((halo.shape[0] // 4, LANES), f32),
            shape((groups, layers, *chunk), f32),
            shape((groups - 1, layers, *chunk), f32),
            shape((layers, *chunk), f32),
            shape((planes - 1, SUBLANES, side), f32),
        ),
        in_specs=[smem, smem, smem] + [vmem] * 8,
        out_specs=(vmem,) * 7,
        scratch_shapes=[
            pltpu.VMEM((tile.shape[0] + halo.shape[0], LANES), f32),
            pltpu.VMEM((chunks, *chunk), f32),
        ]
        + work,
        compiler_params=pltpu.CompilerParams(vmem_limit_bytes=30 * 1024 * 1024),
        cost_estimate=cost,
        name="slots_across",
    )(place, count, here, halo, *begun)
    new_tile, top = written(begun[0], gradient, scale, halo.shape[0])
    return new_tile, top, scale, *rest


def write_kernel(tile_ref, gradient_ref, scale_ref, out_ref, top_ref, rows, semaphores):
    scale = scale_ref[...]
    step = out_ref.shape[0] // 4
    copies = []
    for part in range(4):
        at = pl.ds(part * step, step)
        rows[at, :] = tile_ref[at, :] - gradient_ref[at, :] * scale
        copies.append(pltpu.make_async_copy(rows.at[at], out_ref.at[at], semaphores.at[part]))
        copies[-1].start()
    top_ref[...] = rows[pl.ds(0, top_ref.shape[0]), :]
    for copy in copies:
        copy.wait()


def written(tile, gradient, scale, top_rows):
    vmem, anywhere = pl.BlockSpec(memory_space=pltpu.VMEM), pl.BlockSpec(memory_space=pl.ANY)
    return pl.pallas_call(
        write_kernel,
        out_shape=(
            jax.ShapeDtypeStruct(tile.shape, jnp.float32),
            jax.ShapeDtypeStruct((top_rows, LANES), jnp.float32),
        ),
        in_specs=[vmem, vmem, vmem],
        out_specs=(anywhere, vmem),
        scratch_shapes=[pltpu.VMEM(tile.shape, jnp.float32), pltpu.SemaphoreType.DMA((4,))],
        compiler_params=pltpu.CompilerParams(vmem_limit_bytes=10 * 1024 * 1024),
        cost_estimate=pl.CostEstimate(flops=0, bytes_accessed=4 << 20, transcendentals=0),
        name="written",
    )(tile, gradient, scale)


def first_rows(tile, rows):
    def kernel(tile_ref, out_ref, semaphore):
        copy = pltpu.make_async_copy(tile_ref.at[pl.ds(0, rows)], out_ref, semaphore)
        copy.start()
        copy.wait()

    return pl.pallas_call(
        kernel,
        out_shape=jax.ShapeDtypeStruct((rows, LANES), jnp.float32),
        in_specs=[pl.BlockSpec(memory_space=pl.ANY)],
        out_specs=pl.BlockSpec(memory_space=pltpu.VMEM),
        scratch_shapes=[pltpu.SemaphoreType.DMA],
        compiler_params=pltpu.CompilerParams(vmem_limit_bytes=4 * 1024 * 1024),
        cost_estimate=pl.CostEstimate(flops=0, bytes_accessed=16 << 20, transcendentals=0),
        name="first_rows",
    )(tile)


def divide_kernel(old_ref, *refs):
    *parts, out_ref = refs
    total = parts[0][...]
    for part in parts[1:]:
        total = total + part[...]
    out_ref[...] = (EPSILON * old_ref[...] + total[:-1]) / (total[-1:] + EPSILON)


def divided(old, parts):
    return pl.pallas_call(
        divide_kernel,
        out_shape=jax.ShapeDtypeStruct(old.shape, jnp.float32),
        compiler_params=pltpu.CompilerParams(vmem_limit_bytes=4 * 1024 * 1024),
        name="divided",
    )(old, *parts)


def place_kernel(layers, pieces, here_ref, *refs):
    sources, out, semaphores = refs[: len(pieces)], refs[-2], refs[-1]
    core, group, layer = here_ref[0, 0], here_ref[0, 1], here_ref[0, 2]
    copies = []
    for source, (flip, hop, start) in zip(sources, pieces):
        for j in range(source.shape[0]):
            from_layer = lax.rem(layer + layers - (start + j), layers)
            at = (core ^ flip) * (out.shape[1] // 2) + (group ^ hop) * layers + from_layer
            copies.append(pltpu.make_async_copy(source.at[j], out.at[:, at], semaphores.at[len(copies)]))
    for copy in copies:
        copy.start()
    for copy in copies:
        copy.wait()


def put_in_place(here, layers, pieces, arrays, planes, side, held=None):
    vmem, anywhere = pl.BlockSpec(memory_space=pltpu.VMEM), pl.BlockSpec(memory_space=pl.ANY)
    rest = [] if held is None else [held]
    return pl.pallas_call(
        functools.partial(place_kernel, layers, pieces),
        out_shape=jax.ShapeDtypeStruct((planes, side // SUBLANES, SUBLANES, side), jnp.float32),
        in_specs=[pl.BlockSpec(memory_space=pltpu.SMEM)] + [vmem] * len(arrays) + [anywhere] * len(rest),
        out_specs=anywhere,
        scratch_shapes=[pltpu.SemaphoreType.DMA((sum(array.shape[0] for array in arrays),))],
        input_output_aliases={} if held is None else {1 + len(arrays): 0},
        compiler_params=pltpu.CompilerParams(vmem_limit_bytes=8 * 1024 * 1024),
        cost_estimate=pl.CostEstimate(flops=0, bytes_accessed=4 << 20, transcendentals=0),
        name="put_in_place",
    )(here, *arrays, *rest)


def top_kernel(held_ref, top_ref, arrived_ref, more_ref, scale_ref, out_ref, rows, semaphore):
    for start, source in ((0, arrived_ref), (arrived_ref.shape[0], more_ref)):
        at = pl.ds(start, source.shape[0])
        rows[at, :] = top_ref[at, :] - source[...] * scale_ref[...]
    copy = pltpu.make_async_copy(rows, out_ref.at[pl.ds(0, rows.shape[0])], semaphore)
    copy.start()
    copy.wait()


def with_top(tile, top, arrived, more, scale):
    vmem, anywhere = pl.BlockSpec(memory_space=pltpu.VMEM), pl.BlockSpec(memory_space=pl.ANY)
    return pl.pallas_call(
        top_kernel,
        out_shape=jax.ShapeDtypeStruct(tile.shape, jnp.float32),
        in_specs=[anywhere, vmem, vmem, vmem, vmem],
        out_specs=anywhere,
        scratch_shapes=[pltpu.VMEM(top.shape, jnp.float32), pltpu.SemaphoreType.DMA],
        input_output_aliases={0: 0},
        compiler_params=pltpu.CompilerParams(vmem_limit_bytes=8 * 1024 * 1024),
        cost_estimate=pl.CostEstimate(flops=0, bytes_accessed=2 << 20, transcendentals=0),
        name="with_top",
    )(tile, top, arrived, more, scale)


def across(block, hop):
    return lax.ppermute(block, "group", [(i, i ^ hop) for i in range(lax.axis_size("group"))])


def from_partner(block):
    return lax.ppermute(block, "region", [(i, i ^ 1) for i in range(lax.axis_size("region"))])


def up_layers(block, step):
    regions = lax.axis_size("region")
    return lax.ppermute(block, "region", [(i, (i + 2 * step) % regions) for i in range(regions)])


def probe_by_shards(probe, mine, near, far, old, here, layers, spill, more, new_tile, top, scale):
    modes, parts, side, _ = probe.shape
    planes = modes * parts
    half = layers // 2
    near, other_far = lax.optimization_barrier((near, from_partner(far)))
    other_near, spill = lax.optimization_barrier((from_partner(near), spill))
    arrived = shifted(spill, "region", 1)
    far_sum = mine[3] + other_far
    by_x, by_y = across(far_sum[:half], 1), across(far_sum[half:], 2)
    near_sum = mine[:3] + other_near
    to_x = near_sum[1].at[half:].add(by_y)
    to_y = near_sum[2].at[:half].add(by_x)
    by_x, by_y, arrived, new_tile, top = lax.optimization_barrier(
        (across(to_x, 1), across(to_y, 2), arrived, new_tile, top)
    )
    summed = [near_sum[0, step] + by_x[step] + by_y[step] for step in range(layers)]
    fresh = divided(old, [summed[0]] + [up_layers(summed[step], step) for step in range(1, layers)])
    own = jnp.stack([fresh] + [up_layers(fresh, step) for step in range(1, layers)])
    x, y = across(own, 1), across(own, 2)
    far = [across(x[:half], 2), across(y[half:], 1)]
    other_x, more = lax.optimization_barrier((from_partner(x), more))
    new_tile = with_top(new_tile, top, arrived, shifted(more, "region", 1), scale)
    near = [own, x, y, from_partner(own), other_x, from_partner(y)]
    placed = put_in_place(
        here, layers, tuple((flip, hop, 0) for flip in range(2) for hop in range(3)), near, planes, side
    )
    *far, placed = lax.optimization_barrier((*far, placed))
    far = far + [from_partner(array) for array in far]
    *far, new_tile = lax.optimization_barrier((*far, new_tile))
    pieces = tuple((flip, 3, start) for flip in range(2) for start in (0, half))
    placed = put_in_place(here, layers, pieces, far, planes, side, placed)
    return placed.reshape(probe.shape), new_tile


def probe_from_whole(probe, mine, near, far):
    side = probe.shape[2]
    own = mine.reshape(-1, *mine.shape[2:])
    rest = jnp.concatenate([near.reshape(-1, *near.shape[2:]), far])
    whole = lax.psum(jnp.concatenate([own, rest]), ("region", "group"))
    whole = whole.transpose(1, 0, 2, 3).reshape(-1, side, side)
    old = probe.reshape(-1, side, side)
    return ((EPSILON * old + whole[:-1]) / (whole[-1:] + EPSILON)).reshape(probe.shape)


def on_device(object_slab, probe, diffraction, positions, slot_counts):
    modes, parts, side, _ = probe.shape
    tile_rows, _, columns = object_slab.shape
    regions, groups = lax.axis_size("region"), lax.axis_size("group")
    region, group = lax.axis_index("region"), lax.axis_index("group")
    per_row = parts * columns // LANES
    assert per_row == SUBLANES
    layers = regions // 2
    sharded = groups == 4 and 2 * groups * layers * SUBLANES == side
    tile = packed(object_slab)
    halo = shifted(first_rows(tile, side * per_row), "region", -1)
    place = positions - jnp.stack([region * tile_rows, jnp.zeros_like(region)])[None, :].astype(jnp.int32)
    if sharded:
        here = jnp.stack([region % 2, group, region // 2]).astype(jnp.int32).reshape(1, 3)
    else:
        here = jnp.zeros((1, 3), jnp.int32)
        groups, layers = 4, side // SUBLANES // 8
    new_tile, top, scale, spill, more, mine, near, far, old = gradient_step(
        place, slot_counts, here, tile, halo, probe, diffraction, groups, layers
    )
    if sharded:
        new_probe, new_tile = probe_by_shards(
            probe, mine, near, far, old, here, layers, spill, more, new_tile, top, scale
        )
    else:
        new_tile = with_top(
            new_tile, top, shifted(spill, "region", 1), shifted(more, "region", 1), scale
        )
        new_probe = probe_from_whole(probe, mine, near, far)
    return (unpacked(new_tile, object_slab.shape), new_probe)


def solution(mesh):
    placed = (
        P("region", None, "group"),
        P(),
        P(("region", "group"), None, None),
        P(("region", "group"), None),
        P("group", "region"),
    )
    return jax.shard_map(
        on_device,
        mesh=mesh,
        in_specs=placed,
        out_specs=(P("region", None, "group"), P()),
        check_vma=False,
    )
```

```python
import functools
import math

import jax
import jax.numpy as jnp
import numpy as np
from jax import lax
from jax.experimental import pallas as pl
from jax.experimental.pallas import tpu as pltpu
from jax.sharding import PartitionSpec as P

LANES = 128
SUBLANES = 8
ROWS = 32
STREAM = 2
EPSILON = 1e-06


def shifted(block, axis, distance):
    devices = range(lax.axis_size(axis))
    route = [(i - distance, i) for i in devices if i - distance in devices]
    return lax.ppermute(block, axis, route)


def packed(block):
    rows, parts, columns = block.shape
    cut = block.reshape(rows, parts, columns // LANES, LANES).transpose(0, 2, 1, 3)
    return cut.reshape(rows * parts * columns // LANES, LANES)


def unpacked(block, shape):
    rows, parts, columns = shape
    cut = block.reshape(rows, columns // LANES, parts, LANES).transpose(0, 2, 1, 3)
    return cut.reshape(rows, parts, columns)


def tables(side):
    half = side // 2
    n, q = np.arange(half)[:, None], np.arange(half)[None, :]
    made = []
    for odd in range(2):
        angle = 2.0 * math.pi * ((n * (2 * q + odd)) % side) / side
        made += [np.cos(angle) / math.sqrt(side), -np.sin(angle) / math.sqrt(side)]
    return np.stack(made).astype(np.float32)


def fill_table(factor_ref, table_ref):
    half = factor_ref.shape[1]
    left, right = pl.ds(0, half), pl.ds(half, half)
    for odd in range(2):
        for turned in range(2):
            real, imag = factor_ref[2 * odd], factor_ref[2 * odd + 1]
            if turned:
                real, imag = real.T, -imag.T
            for term, (re, im, minus) in enumerate(zip(split(real), split(imag), split(-imag))):
                entry = 2 * turned + odd
                table_ref[term, entry, left, left] = re
                table_ref[term, entry, left, right] = im
                table_ref[term, entry, right, left] = minus
                table_ref[term, entry, right, right] = re


def parity_order(side):
    half = side // 2
    first = lax.broadcasted_iota(jnp.int32, (side, side), 0)
    second = lax.broadcasted_iota(jnp.int32, (side, side), 1)

    def moves(source, place):
        odd = (place >= half).astype(jnp.int32)
        hit = source == 2 * (place - odd * half) + odd
        return hit.astype(jnp.float32).astype(jnp.bfloat16)

    return moves(first, second), moves(second, first)


def split(x):
    high = x.astype(jnp.bfloat16)
    low = (x - high.astype(jnp.float32)).astype(jnp.bfloat16)
    return high, low


def dot(a, b):
    return jnp.dot(a, b, preferred_element_type=jnp.float32)


def transform(terms, rows, table_ref, table, out):
    side = out.shape[2]
    for half in range(2):
        high = terms[half, rows, pl.ds(0, side)]
        low = terms[half, rows, pl.ds(side, side)]
        t_high, t_low = table_ref[0, table + half], table_ref[1, table + half]
        out[half, rows, :] = dot(
            jnp.concatenate([high, low, high], axis=1),
            jnp.concatenate([t_high, t_high, t_low], axis=0),
        )


def transform_rows(terms, rows, table_ref, table, out):
    side = out.shape[2]
    for half in range(2):
        high = terms[half, rows, pl.ds(0, side)]
        low = terms[half, rows, pl.ds(side, side)]
        t_high, t_low = table_ref[0, table + half], table_ref[1, table + half]
        out[half, rows, :] = dot(
            jnp.concatenate([t_high, t_high, t_low], axis=1),
            jnp.concatenate([high, low, high], axis=0),
        )


def keep(terms, half, start, value):
    rows = pl.ds(start, value.shape[0])
    side = value.shape[1]
    high, low = split(value)
    terms[half, rows, pl.ds(0, side)] = high
    terms[half, rows, pl.ds(side, side)] = low


def beside(real, imag):
    return jnp.concatenate([real, imag], axis=1)


def all_slots(
    local,
    tile_rows,
    place_ref,
    count_ref,
    probe_ref,
    table_ref,
    extended,
    gradient,
    sums,
    power,
    measured,
    window,
    terms,
    result,
    back,
):
    modes, _, side, _ = probe_ref.shape
    half = side // 2
    per_row = SUBLANES
    lane = lax.broadcasted_iota(jnp.int32, (side, LANES), 1)
    blocks = side // LANES
    left, right = pl.ds(0, half), pl.ds(half, half)
    pieces = [pl.ds(start, ROWS) for start in range(0, side, ROWS)]
    streams = [range(start, min(start + STREAM, modes)) for start in range(0, modes, STREAM)]

    def rows_of(stream):
        return pl.ds(stream[0] * side, len(stream) * side)

    def slot(index):
        row = place_ref[index, 0]
        column = place_ref[index, 1]
        first = column // LANES
        shift = column - first * LANES
        back_shift = lax.rem(LANES - shift, LANES)
        last = per_row // 2 - 1

        def strided(block, part):
            at = row * per_row + jnp.minimum(first + block, last) * 2 + part
            return pl.ds(at, side, stride=per_row)

        for part in range(2):
            rolled = [
                pltpu.roll(extended[strided(block, part), :], back_shift, 1) for block in range(blocks + 1)
            ]
            for block in range(blocks):
                window[part, :, pl.ds(block * LANES, LANES)] = jnp.where(
                    lane < LANES - shift, rolled[block], rolled[block + 1]
                )
        for stream in streams:
            for mode in stream:
                for rows in pieces:
                    w = [window[part, rows, side_] for part in range(2) for side_ in (left, right)]
                    p = [probe_ref[mode, part, rows, side_] for part in range(2) for side_ in (left, right)]
                    real = [p[k] * w[k] - p[2 + k] * w[2 + k] for k in range(2)]
                    imag = [p[k] * w[2 + k] + p[2 + k] * w[k] for k in range(2)]
                    start = mode * side + rows.start
                    keep(terms, 0, start, beside(real[0] + real[1], imag[0] + imag[1]))
                    keep(terms, 1, start, beside(real[0] - real[1], imag[0] - imag[1]))
            transform(terms, rows_of(stream), table_ref, 0, result)
        halves = [pl.ds(start, ROWS) for start in range(0, half, ROWS)]
        for mode in range(modes):
            base = mode * side
            for rows in halves:
                for part, side_ in enumerate((left, right)):
                    top, bottom = pl.ds(base + rows.start, ROWS), pl.ds(base + half + rows.start, ROWS)
                    above = beside(result[0, top, side_], result[1, top, side_])
                    below = beside(result[0, bottom, side_], result[1, bottom, side_])
                    start = base + part * half + rows.start
                    keep(terms, 0, start, above + below)
                    keep(terms, 1, start, above - below)
            transform_rows(terms, pl.ds(base, side), table_ref, 2, result)
        for odd in range(2):
            for rows in halves:
                far = [
                    [result[odd, pl.ds(mode * side + part * half + rows.start, ROWS), :] for part in range(2)]
                    for mode in range(modes)
                ]
                intensity = jnp.zeros((ROWS, side), jnp.float32)
                for real, imag in far:
                    intensity = intensity + real * real + imag * imag
                amount = measured[index, pl.ds(odd * half + rows.start, ROWS), :]
                ratio = amount * lax.rsqrt(amount * jnp.maximum(intensity, 1.0))
                for mode in range(modes):
                    for part in range(2):
                        keep(terms, odd, mode * side + part * half + rows.start, far[mode][part] * ratio)
        for mode in range(modes):
            transform_rows(terms, pl.ds(mode * side, side), table_ref, 0, result)
        for stream in streams:
            for mode in stream:
                base = mode * side
                for rows in halves:
                    real, imag = pl.ds(base + rows.start, ROWS), pl.ds(base + half + rows.start, ROWS)
                    for odd, side_ in enumerate((left, right)):
                        a = beside(result[0, real, side_], result[0, imag, side_])
                        b = beside(result[1, real, side_], result[1, imag, side_])
                        keep(terms, odd, base + rows.start, a + b)
                        keep(terms, odd, base + half + rows.start, a - b)
            transform(terms, rows_of(stream), table_ref, 2, result)
        for number, stream in enumerate(streams):
            for rows in pieces:
                chunk = pl.ds(rows.start // SUBLANES, ROWS // SUBLANES)
                by_chunk = (ROWS // SUBLANES, SUBLANES, half)
                for lower, side_ in enumerate((left, right)):
                    w_r, w_i = window[0, rows, side_], window[1, rows, side_]
                    if number:
                        g_r, g_i = back[0, rows, side_], back[1, rows, side_]
                    else:
                        strength = power[rows, side_]
                        g_r, g_i = strength * w_r, strength * w_i
                    for mode in stream:
                        at = pl.ds(mode * side + rows.start, ROWS)
                        if lower:
                            c_r = result[0, at, left] - result[1, at, left]
                            c_i = result[0, at, right] - result[1, at, right]
                        else:
                            c_r = result[0, at, left] + result[1, at, left]
                            c_i = result[0, at, right] + result[1, at, right]
                        p_r, p_i = probe_ref[mode, 0, rows, side_], probe_ref[mode, 1, rows, side_]
                        g_r = g_r - (p_r * c_r + p_i * c_i)
                        g_i = g_i - (p_r * c_i - p_i * c_r)
                        sums[chunk, 2 * mode, :, side_] += (w_r * c_r + w_i * c_i).reshape(by_chunk)
                        sums[chunk, 2 * mode + 1, :, side_] += (w_r * c_i - w_i * c_r).reshape(by_chunk)
                    back[0, rows, side_] = g_r
                    back[1, rows, side_] = g_i
                    if not number:
                        sums[chunk, 2 * modes, :, side_] += (w_r * w_r + w_i * w_i).reshape(by_chunk)

        for part in range(2):
            rolled = [
                pltpu.roll(back[part, :, pl.ds(block * LANES, LANES)], shift, 1) for block in range(blocks)
            ]
            zero = jnp.zeros((side, LANES), jnp.float32)
            for block in range(blocks + 1):
                here = rolled[block] if block < blocks else zero
                before = rolled[block - 1] if block else zero
                at = strided(block, part)
                gradient[at, :] = gradient[at, :] + jnp.where(lane >= shift, here, before)

    def visit(index, carry):
        inside = place_ref[index, 0] + side <= tile_rows
        pl.when(inside if local else jnp.logical_not(inside))(lambda: slot(index))
        return carry

    lax.fori_loop(0, count_ref[0, 0], visit, 0)


def first_kernel(
    place_ref,
    count_ref,
    tile_hbm,
    probe_ref,
    diffraction_ref,
    factor_ref,
    tile_out,
    gradient,
    sums,
    measured,
    power,
    probe_out,
    table_out,
    scale_out,
    window,
    terms,
    result,
    back,
    semaphore,
):
    modes, _, side, _ = probe_ref.shape
    copy = pltpu.make_async_copy(tile_hbm, tile_out, semaphore)
    copy.start()
    gradient[...] = jnp.zeros_like(gradient)
    sums[...] = jnp.zeros_like(sums)
    total = jnp.zeros((side, side), jnp.float32)
    for mode in range(modes):
        total = total + probe_ref[mode, 0] * probe_ref[mode, 0] + probe_ref[mode, 1] * probe_ref[mode, 1]
    power[...] = total
    scale_out[...] = jnp.full(scale_out.shape, 1.0 / jnp.max(total))
    probe_out[...] = probe_ref[...]
    fill_table(factor_ref, table_out)
    by_lanes, by_rows = parity_order(side)

    def order(index, carry):
        high, low = split(diffraction_ref[index])
        seen = dot(jnp.concatenate([by_rows] * 2, axis=1), jnp.concatenate([high, low], axis=0))
        high, low = split(seen)
        seen = dot(jnp.concatenate([high, low], axis=1), jnp.concatenate([by_lanes] * 2, axis=0))
        measured[index] = seen
        return carry

    lax.fori_loop(0, count_ref[0, 0], order, 0)
    copy.wait()
    all_slots(
        True, tile_out.shape[0] // SUBLANES, place_ref, count_ref, probe_ref, table_out, tile_out,
        gradient, sums, power, measured, window, terms, result, back,
    )


def second_kernel(
    place_ref,
    count_ref,
    here_ref,
    halo_ref,
    tile_ref,
    gradient_ref,
    sums_ref,
    measured,
    power,
    probe_ref,
    table_ref,
    gradient,
    spill_out,
    mine_out,
    near_out,
    far_out,
    old_out,
    extended,
    sums,
    window,
    terms,
    result,
    back,
):
    modes = probe_ref.shape[0]
    tile_rows, halo_rows, chunks = tile_ref.shape[0], halo_ref.shape[0], sums.shape[0]
    extended[pl.ds(0, tile_rows), :] = tile_ref[...]
    extended[pl.ds(tile_rows, halo_rows), :] = halo_ref[...]
    gradient[pl.ds(0, tile_rows), :] = gradient_ref[...]
    gradient[pl.ds(tile_rows, halo_rows), :] = jnp.zeros((halo_rows, LANES), jnp.float32)
    sums[...] = sums_ref[...]
    all_slots(
        False, tile_rows // SUBLANES, place_ref, count_ref, probe_ref, table_ref, extended,
        gradient, sums, power, measured, window, terms, result, back,
    )
    spill_out[...] = gradient[pl.ds(tile_rows, halo_rows), :]
    core, group, layer = here_ref[0, 0], here_ref[0, 1], here_ref[0, 2]
    groups, layers = mine_out.shape[0], mine_out.shape[1]
    for hop in range(groups):
        for step in range(layers):
            at = (group ^ hop) * layers + lax.rem(layer + step, layers)
            mine_out[hop, step] = sums[core * (chunks // 2) + at]
            if hop < groups - 1:
                near_out[hop, step] = sums[(1 - core) * (chunks // 2) + at]
            else:
                far_out[step] = sums[(1 - core) * (chunks // 2) + at]
    start = pl.multiple_of(((core * groups + group) * layers + layer) * SUBLANES, SUBLANES)
    for mode in range(modes):
        for part in range(2):
            old_out[2 * mode + part] = probe_ref[mode, part, pl.ds(start, SUBLANES), :]


def gradient_step(place, count, here, tile, halo, probe, diffraction, groups, layers):
    modes, parts, side, _ = probe.shape
    planes = parts * modes + 1
    chunks = side // SUBLANES
    f32 = jnp.float32
    smem = pl.BlockSpec(memory_space=pltpu.SMEM)
    vmem = pl.BlockSpec(memory_space=pltpu.VMEM)
    chunk = (planes, SUBLANES, side)
    products = 3 * 16 * modes * diffraction.shape[0] * side**3 // 2
    work = [
        pltpu.VMEM((2, side, side), f32),
        pltpu.VMEM((2, modes * side, 2 * side), jnp.bfloat16),
        pltpu.VMEM((2, modes * side, side), f32),
        pltpu.VMEM((2, side, side), f32),
    ]
    shape = jax.ShapeDtypeStruct
    cost = pl.CostEstimate(flops=2 * products, bytes_accessed=16 << 20, transcendentals=0)
    *begun, scale = pl.pallas_call(
        first_kernel,
        out_shape=(
            shape(tile.shape, f32),
            shape(tile.shape, f32),
            shape((chunks, *chunk), f32),
            shape(diffraction.shape, f32),
            shape((side, side), f32),
            shape(probe.shape, f32),
            shape((2, 4, side, side), jnp.bfloat16),
            shape((1, LANES), f32),
        ),
        in_specs=[smem, smem, pl.BlockSpec(memory_space=pl.ANY), vmem, vmem, vmem],
        out_specs=(vmem,) * 8,
        scratch_shapes=work + [pltpu.SemaphoreType.DMA],
        compiler_params=pltpu.CompilerParams(vmem_limit_bytes=28 * 1024 * 1024),
        cost_estimate=cost,
        name="slots_inside",
    )(place, count, tile, probe, diffraction, jnp.asarray(tables(side)))
    gradient, *rest = pl.pallas_call(
        second_kernel,
        out_shape=(
            shape((tile.shape[0] + halo.shape[0], LANES), f32),
            shape(halo.shape, f32),
            shape((groups, layers, *chunk), f32),
            shape((groups - 1, layers, *chunk), f32),
            shape((layers, *chunk), f32),
            shape((planes - 1, SUBLANES, side), f32),
        ),
        in_specs=[smem, smem, smem] + [vmem] * 8,
        out_specs=(vmem,) * 6,
        scratch_shapes=[
            pltpu.VMEM((tile.shape[0] + halo.shape[0], LANES), f32),
            pltpu.VMEM((chunks, *chunk), f32),
        ]
        + work,
        compiler_params=pltpu.CompilerParams(vmem_limit_bytes=30 * 1024 * 1024),
        cost_estimate=cost,
        name="slots_across",
    )(place, count, here, halo, *begun)
    new_tile, top = written(begun[0], gradient, scale, halo.shape[0])
    return new_tile, top, scale, *rest


def write_kernel(tile_ref, gradient_ref, scale_ref, out_ref, top_ref, rows, semaphores):
    scale = scale_ref[...]
    step = out_ref.shape[0] // 4
    copies = []
    for part in range(4):
        at = pl.ds(part * step, step)
        rows[at, :] = tile_ref[at, :] - gradient_ref[at, :] * scale
        copies.append(pltpu.make_async_copy(rows.at[at], out_ref.at[at], semaphores.at[part]))
        copies[-1].start()
    top_ref[...] = rows[pl.ds(0, top_ref.shape[0]), :]
    for copy in copies:
        copy.wait()


def written(tile, gradient, scale, top_rows):
    vmem, anywhere = pl.BlockSpec(memory_space=pltpu.VMEM), pl.BlockSpec(memory_space=pl.ANY)
    return pl.pallas_call(
        write_kernel,
        out_shape=(
            jax.ShapeDtypeStruct(tile.shape, jnp.float32),
            jax.ShapeDtypeStruct((top_rows, LANES), jnp.float32),
        ),
        in_specs=[vmem, vmem, vmem],
        out_specs=(anywhere, vmem),
        scratch_shapes=[pltpu.VMEM(tile.shape, jnp.float32), pltpu.SemaphoreType.DMA((4,))],
        compiler_params=pltpu.CompilerParams(vmem_limit_bytes=10 * 1024 * 1024),
        cost_estimate=pl.CostEstimate(flops=0, bytes_accessed=4 << 20, transcendentals=0),
        name="written",
    )(tile, gradient, scale)


def first_rows(tile, rows):
    def kernel(tile_ref, out_ref, semaphore):
        copy = pltpu.make_async_copy(tile_ref.at[pl.ds(0, rows)], out_ref, semaphore)
        copy.start()
        copy.wait()

    return pl.pallas_call(
        kernel,
        out_shape=jax.ShapeDtypeStruct((rows, LANES), jnp.float32),
        in_specs=[pl.BlockSpec(memory_space=pl.ANY)],
        out_specs=pl.BlockSpec(memory_space=pltpu.VMEM),
        scratch_shapes=[pltpu.SemaphoreType.DMA],
        compiler_params=pltpu.CompilerParams(vmem_limit_bytes=4 * 1024 * 1024),
        cost_estimate=pl.CostEstimate(flops=0, bytes_accessed=16 << 20, transcendentals=0),
        name="first_rows",
    )(tile)


def divide_kernel(old_ref, *refs):
    *parts, out_ref = refs
    total = parts[0][...]
    for part in parts[1:]:
        total = total + part[...]
    out_ref[...] = (EPSILON * old_ref[...] + total[:-1]) / (total[-1:] + EPSILON)


def divided(old, parts):
    return pl.pallas_call(
        divide_kernel,
        out_shape=jax.ShapeDtypeStruct(old.shape, jnp.float32),
        compiler_params=pltpu.CompilerParams(vmem_limit_bytes=4 * 1024 * 1024),
        name="divided",
    )(old, *parts)


def place_kernel(layers, pieces, here_ref, *refs):
    sources, out, semaphores = refs[: len(pieces)], refs[-2], refs[-1]
    core, group, layer = here_ref[0, 0], here_ref[0, 1], here_ref[0, 2]
    copies = []
    for source, (flip, hop, start) in zip(sources, pieces):
        for j in range(source.shape[0]):
            from_layer = lax.rem(layer + layers - (start + j), layers)
            at = (core ^ flip) * (out.shape[1] // 2) + (group ^ hop) * layers + from_layer
            copies.append(pltpu.make_async_copy(source.at[j], out.at[:, at], semaphores.at[len(copies)]))
    for copy in copies:
        copy.start()
    for copy in copies:
        copy.wait()


def put_in_place(here, layers, pieces, arrays, planes, side, held=None):
    vmem, anywhere = pl.BlockSpec(memory_space=pltpu.VMEM), pl.BlockSpec(memory_space=pl.ANY)
    rest = [] if held is None else [held]
    return pl.pallas_call(
        functools.partial(place_kernel, layers, pieces),
        out_shape=jax.ShapeDtypeStruct((planes, side // SUBLANES, SUBLANES, side), jnp.float32),
        in_specs=[pl.BlockSpec(memory_space=pltpu.SMEM)] + [vmem] * len(arrays) + [anywhere] * len(rest),
        out_specs=anywhere,
        scratch_shapes=[pltpu.SemaphoreType.DMA((sum(array.shape[0] for array in arrays),))],
        input_output_aliases={} if held is None else {1 + len(arrays): 0},
        compiler_params=pltpu.CompilerParams(vmem_limit_bytes=8 * 1024 * 1024),
        cost_estimate=pl.CostEstimate(flops=0, bytes_accessed=4 << 20, transcendentals=0),
        name="put_in_place",
    )(here, *arrays, *rest)


def top_kernel(held_ref, top_ref, arrived_ref, scale_ref, out_ref, rows, semaphore):
    rows[...] = top_ref[...] - arrived_ref[...] * scale_ref[...]
    copy = pltpu.make_async_copy(rows, out_ref.at[pl.ds(0, rows.shape[0])], semaphore)
    copy.start()
    copy.wait()


def with_top(tile, top, arrived, scale):
    vmem, anywhere = pl.BlockSpec(memory_space=pltpu.VMEM), pl.BlockSpec(memory_space=pl.ANY)
    return pl.pallas_call(
        top_kernel,
        out_shape=jax.ShapeDtypeStruct(tile.shape, jnp.float32),
        in_specs=[anywhere, vmem, vmem, vmem],
        out_specs=anywhere,
        scratch_shapes=[pltpu.VMEM(top.shape, jnp.float32), pltpu.SemaphoreType.DMA],
        input_output_aliases={0: 0},
        compiler_params=pltpu.CompilerParams(vmem_limit_bytes=8 * 1024 * 1024),
        cost_estimate=pl.CostEstimate(flops=0, bytes_accessed=2 << 20, transcendentals=0),
        name="with_top",
    )(tile, top, arrived, scale)


def across(block, hop):
    return lax.ppermute(block, "group", [(i, i ^ hop) for i in range(lax.axis_size("group"))])


def from_partner(block):
    return lax.ppermute(block, "region", [(i, i ^ 1) for i in range(lax.axis_size("region"))])


def up_layers(block, step):
    regions = lax.axis_size("region")
    return lax.ppermute(block, "region", [(i, (i + 2 * step) % regions) for i in range(regions)])


def probe_by_shards(probe, mine, near, far, old, here, layers, spill, new_tile, top, scale):
    modes, parts, side, _ = probe.shape
    planes = modes * parts
    half = layers // 2
    near, other_far = lax.optimization_barrier((near, from_partner(far)))
    other_near, spill = lax.optimization_barrier((from_partner(near), spill))
    arrived = shifted(spill, "region", 1)
    far_sum = mine[3] + other_far
    by_x, by_y = across(far_sum[:half], 1), across(far_sum[half:], 2)
    near_sum = mine[:3] + other_near
    to_x = near_sum[1].at[half:].add(by_y)
    to_y = near_sum[2].at[:half].add(by_x)
    by_x, by_y, new_tile, top = lax.optimization_barrier((across(to_x, 1), across(to_y, 2), new_tile, top))
    summed = [near_sum[0, step] + by_x[step] + by_y[step] for step in range(layers)]
    *others, arrived = lax.optimization_barrier(
        (*[up_layers(summed[step], step) for step in range(1, layers)], arrived)
    )
    new_tile = with_top(new_tile, top, arrived, scale)
    fresh = divided(old, [summed[0]] + others)
    *others, new_tile = lax.optimization_barrier(
        (*[up_layers(fresh, step) for step in range(1, layers)], new_tile)
    )
    own = jnp.stack([fresh] + others)
    x, y = across(own, 1), across(own, 2)
    far = [across(x[:half], 2), across(y[half:], 1)]
    near = [own, x, y, from_partner(own), from_partner(x), from_partner(y)]
    placed = put_in_place(
        here, layers, tuple((flip, hop, 0) for flip in range(2) for hop in range(3)), near, planes, side
    )
    *far, placed = lax.optimization_barrier((*far, placed))
    far = far + [from_partner(array) for array in far]
    pieces = tuple((flip, 3, start) for flip in range(2) for start in (0, half))
    placed = put_in_place(here, layers, pieces, far, planes, side, placed)
    return placed.reshape(probe.shape), new_tile


def probe_from_whole(probe, mine, near, far):
    side = probe.shape[2]
    own = mine.reshape(-1, *mine.shape[2:])
    rest = jnp.concatenate([near.reshape(-1, *near.shape[2:]), far])
    whole = lax.psum(jnp.concatenate([own, rest]), ("region", "group"))
    whole = whole.transpose(1, 0, 2, 3).reshape(-1, side, side)
    old = probe.reshape(-1, side, side)
    return ((EPSILON * old + whole[:-1]) / (whole[-1:] + EPSILON)).reshape(probe.shape)


def on_device(object_slab, probe, diffraction, positions, slot_counts):
    modes, parts, side, _ = probe.shape
    tile_rows, _, columns = object_slab.shape
    regions, groups = lax.axis_size("region"), lax.axis_size("group")
    region, group = lax.axis_index("region"), lax.axis_index("group")
    per_row = parts * columns // LANES
    assert per_row == SUBLANES
    layers = regions // 2
    sharded = groups == 4 and 2 * groups * layers * SUBLANES == side
    tile = packed(object_slab)
    halo = shifted(first_rows(tile, side * per_row), "region", -1)
    place = positions - jnp.stack([region * tile_rows, jnp.zeros_like(region)])[None, :].astype(jnp.int32)
    if sharded:
        here = jnp.stack([region % 2, group, region // 2]).astype(jnp.int32).reshape(1, 3)
    else:
        here = jnp.zeros((1, 3), jnp.int32)
        groups, layers = 4, side // SUBLANES // 8
    new_tile, top, scale, spill, mine, near, far, old = gradient_step(
        place, slot_counts, here, tile, halo, probe, diffraction, groups, layers
    )
    if sharded:
        new_probe, new_tile = probe_by_shards(
            probe, mine, near, far, old, here, layers, spill, new_tile, top, scale
        )
    else:
        new_tile = with_top(new_tile, top, shifted(spill, "region", 1), scale)
        new_probe = probe_from_whole(probe, mine, near, far)
    return (unpacked(new_tile, object_slab.shape), new_probe)


def solution(mesh):
    placed = (
        P("region", None, "group"),
        P(),
        P(("region", "group"), None, None),
        P(("region", "group"), None),
        P("group", "region"),
    )
    return jax.shard_map(
        on_device,
        mesh=mesh,
        in_specs=placed,
        out_specs=(P("region", None, "group"), P()),
        check_vma=False,
    )
```

```python
import functools
import math

import jax
import jax.numpy as jnp
import numpy as np
from jax import lax
from jax.experimental import pallas as pl
from jax.experimental.pallas import tpu as pltpu
from jax.sharding import PartitionSpec as P

LANES = 128
SUBLANES = 8
PITCH = 9
ROWS = 32
STREAM = 2
EPSILON = 1e-06


def shifted(block, axis, distance):
    devices = range(lax.axis_size(axis))
    route = [(i - distance, i) for i in devices if i - distance in devices]
    return lax.ppermute(block, axis, route)


def packed(block):
    rows, parts, columns = block.shape
    cut = block.reshape(rows, parts, columns // LANES, LANES).transpose(0, 2, 1, 3)
    return cut.reshape(rows * parts * columns // LANES, LANES)


def unpacked(block, shape):
    rows, parts, columns = shape
    cut = block.reshape(rows, columns // LANES, parts, LANES).transpose(0, 2, 1, 3)
    return cut.reshape(rows, parts, columns)


def tables(side):
    half = side // 2
    n, q = np.arange(half)[:, None], np.arange(half)[None, :]
    made = []
    for odd in range(2):
        angle = 2.0 * math.pi * ((n * (2 * q + odd)) % side) / side
        made += [np.cos(angle) / math.sqrt(side), -np.sin(angle) / math.sqrt(side)]
    return np.stack(made).astype(np.float32)


def fill_table(factor_ref, table_ref):
    half = factor_ref.shape[1]
    left, right = pl.ds(0, half), pl.ds(half, half)
    for odd in range(2):
        for turned in range(2):
            real, imag = factor_ref[2 * odd], factor_ref[2 * odd + 1]
            if turned:
                real, imag = real.T, -imag.T
            for term, (re, im, minus) in enumerate(zip(split(real), split(imag), split(-imag))):
                entry = 2 * turned + odd
                table_ref[term, entry, left, left] = re
                table_ref[term, entry, left, right] = im
                table_ref[term, entry, right, left] = minus
                table_ref[term, entry, right, right] = re


def parity_order(side):
    half = side // 2
    first = lax.broadcasted_iota(jnp.int32, (side, side), 0)
    second = lax.broadcasted_iota(jnp.int32, (side, side), 1)

    def moves(source, place):
        odd = (place >= half).astype(jnp.int32)
        hit = source == 2 * (place - odd * half) + odd
        return hit.astype(jnp.float32).astype(jnp.bfloat16)

    return moves(first, second), moves(second, first)


def split(x):
    high = x.astype(jnp.bfloat16)
    low = (x - high.astype(jnp.float32)).astype(jnp.bfloat16)
    return high, low


def dot(a, b):
    return jnp.dot(a, b, preferred_element_type=jnp.float32)


def transform(terms, rows, table_ref, table, out):
    side = out.shape[2]
    for half in range(2):
        high = terms[half, rows, pl.ds(0, side)]
        low = terms[half, rows, pl.ds(side, side)]
        t_high, t_low = table_ref[0, table + half], table_ref[1, table + half]
        out[half, rows, :] = dot(
            jnp.concatenate([high, low, high], axis=1),
            jnp.concatenate([t_high, t_high, t_low], axis=0),
        )


def transform_rows(terms, rows, table_ref, table, out):
    side = out.shape[2]
    for half in range(2):
        high = terms[half, rows, pl.ds(0, side)]
        low = terms[half, rows, pl.ds(side, side)]
        t_high, t_low = table_ref[0, table + half], table_ref[1, table + half]
        out[half, rows, :] = dot(
            jnp.concatenate([t_high, t_high, t_low], axis=1),
            jnp.concatenate([high, low, high], axis=0),
        )


def keep(terms, half, start, value):
    rows = pl.ds(start, value.shape[0])
    side = value.shape[1]
    high, low = split(value)
    terms[half, rows, pl.ds(0, side)] = high
    terms[half, rows, pl.ds(side, side)] = low


def beside(real, imag):
    return jnp.concatenate([real, imag], axis=1)


def spread(source, target, first, rows):
    for row in range(rows):
        target[pl.ds((first + row) * PITCH, SUBLANES), :] = source[pl.ds(row * SUBLANES, SUBLANES), :]


def gathered(source, first, target, rows):
    for row in range(rows):
        target[pl.ds(row * SUBLANES, SUBLANES), :] = source[pl.ds((first + row) * PITCH, SUBLANES), :]


def all_slots(
    local,
    tile_rows,
    place_ref,
    count_ref,
    probe_ref,
    table_ref,
    extended,
    gradient,
    sums,
    power,
    measured,
    window,
    terms,
    result,
    back,
):
    modes, _, side, _ = probe_ref.shape
    half = side // 2
    per_row = SUBLANES
    lane = lax.broadcasted_iota(jnp.int32, (side, LANES), 1)
    blocks = side // LANES
    left, right = pl.ds(0, half), pl.ds(half, half)
    pieces = [pl.ds(start, ROWS) for start in range(0, side, ROWS)]
    streams = [range(start, min(start + STREAM, modes)) for start in range(0, modes, STREAM)]

    def rows_of(stream):
        return pl.ds(stream[0] * side, len(stream) * side)

    def slot(index):
        row = place_ref[index, 0]
        column = place_ref[index, 1]
        first = column // LANES
        shift = column - first * LANES
        back_shift = lax.rem(LANES - shift, LANES)
        last = per_row // 2 - 1

        def strided(block, part):
            at = row * PITCH + jnp.minimum(first + block, last) * 2 + part
            return pl.ds(at, side, stride=PITCH)

        for part in range(2):
            rolled = [
                pltpu.roll(extended[strided(block, part), :], back_shift, 1) for block in range(blocks + 1)
            ]
            for block in range(blocks):
                window[part, :, pl.ds(block * LANES, LANES)] = jnp.where(
                    lane < LANES - shift, rolled[block], rolled[block + 1]
                )
        for stream in streams:
            for mode in stream:
                for rows in pieces:
                    w = [window[part, rows, side_] for part in range(2) for side_ in (left, right)]
                    p = [probe_ref[mode, part, rows, side_] for part in range(2) for side_ in (left, right)]
                    real = [p[k] * w[k] - p[2 + k] * w[2 + k] for k in range(2)]
                    imag = [p[k] * w[2 + k] + p[2 + k] * w[k] for k in range(2)]
                    start = mode * side + rows.start
                    keep(terms, 0, start, beside(real[0] + real[1], imag[0] + imag[1]))
                    keep(terms, 1, start, beside(real[0] - real[1], imag[0] - imag[1]))
            transform(terms, rows_of(stream), table_ref, 0, result)
        halves = [pl.ds(start, ROWS) for start in range(0, half, ROWS)]
        for mode in range(modes):
            base = mode * side
            for rows in halves:
                for part, side_ in enumerate((left, right)):
                    top, bottom = pl.ds(base + rows.start, ROWS), pl.ds(base + half + rows.start, ROWS)
                    above = beside(result[0, top, side_], result[1, top, side_])
                    below = beside(result[0, bottom, side_], result[1, bottom, side_])
                    start = base + part * half + rows.start
                    keep(terms, 0, start, above + below)
                    keep(terms, 1, start, above - below)
            transform_rows(terms, pl.ds(base, side), table_ref, 2, result)
        for odd in range(2):
            for rows in halves:
                far = [
                    [result[odd, pl.ds(mode * side + part * half + rows.start, ROWS), :] for part in range(2)]
                    for mode in range(modes)
                ]
                intensity = jnp.zeros((ROWS, side), jnp.float32)
                for real, imag in far:
                    intensity = intensity + real * real + imag * imag
                amount = measured[index, pl.ds(odd * half + rows.start, ROWS), :]
                ratio = amount * lax.rsqrt(amount * jnp.maximum(intensity, 1.0))
                for mode in range(modes):
                    for part in range(2):
                        keep(terms, odd, mode * side + part * half + rows.start, far[mode][part] * ratio)
        for mode in range(modes):
            transform_rows(terms, pl.ds(mode * side, side), table_ref, 0, result)
        for stream in streams:
            for mode in stream:
                base = mode * side
                for rows in halves:
                    real, imag = pl.ds(base + rows.start, ROWS), pl.ds(base + half + rows.start, ROWS)
                    for odd, side_ in enumerate((left, right)):
                        a = beside(result[0, real, side_], result[0, imag, side_])
                        b = beside(result[1, real, side_], result[1, imag, side_])
                        keep(terms, odd, base + rows.start, a + b)
                        keep(terms, odd, base + half + rows.start, a - b)
            transform(terms, rows_of(stream), table_ref, 2, result)
        for number, stream in enumerate(streams):
            for rows in pieces:
                chunk = pl.ds(rows.start // SUBLANES, ROWS // SUBLANES)
                by_chunk = (ROWS // SUBLANES, SUBLANES, half)
                for lower, side_ in enumerate((left, right)):
                    w_r, w_i = window[0, rows, side_], window[1, rows, side_]
                    if number:
                        g_r, g_i = back[0, rows, side_], back[1, rows, side_]
                    else:
                        strength = power[rows, side_]
                        g_r, g_i = strength * w_r, strength * w_i
                    for mode in stream:
                        at = pl.ds(mode * side + rows.start, ROWS)
                        if lower:
                            c_r = result[0, at, left] - result[1, at, left]
                            c_i = result[0, at, right] - result[1, at, right]
                        else:
                            c_r = result[0, at, left] + result[1, at, left]
                            c_i = result[0, at, right] + result[1, at, right]
                        p_r, p_i = probe_ref[mode, 0, rows, side_], probe_ref[mode, 1, rows, side_]
                        g_r = g_r - (p_r * c_r + p_i * c_i)
                        g_i = g_i - (p_r * c_i - p_i * c_r)
                        sums[chunk, 2 * mode, :, side_] += (w_r * c_r + w_i * c_i).reshape(by_chunk)
                        sums[chunk, 2 * mode + 1, :, side_] += (w_r * c_i - w_i * c_r).reshape(by_chunk)
                    back[0, rows, side_] = g_r
                    back[1, rows, side_] = g_i
                    if not number:
                        sums[chunk, 2 * modes, :, side_] += (w_r * w_r + w_i * w_i).reshape(by_chunk)

        for part in range(2):
            rolled = [
                pltpu.roll(back[part, :, pl.ds(block * LANES, LANES)], shift, 1) for block in range(blocks)
            ]
            zero = jnp.zeros((side, LANES), jnp.float32)
            for block in range(blocks + 1):
                here = rolled[block] if block < blocks else zero
                before = rolled[block - 1] if block else zero
                at = strided(block, part)
                gradient[at, :] = gradient[at, :] + jnp.where(lane >= shift, here, before)

    def visit(index, carry):
        inside = place_ref[index, 0] + side <= tile_rows
        pl.when(inside if local else jnp.logical_not(inside))(lambda: slot(index))
        return carry

    lax.fori_loop(0, count_ref[0, 0], visit, 0)


def first_kernel(
    place_ref,
    count_ref,
    tile_hbm,
    probe_ref,
    diffraction_ref,
    factor_ref,
    tile_out,
    gradient,
    sums,
    measured,
    power,
    probe_out,
    table_out,
    scale_out,
    extended,
    window,
    terms,
    result,
    back,
    semaphore,
):
    modes, _, side, _ = probe_ref.shape
    copy = pltpu.make_async_copy(tile_hbm, tile_out, semaphore)
    copy.start()
    gradient[...] = jnp.zeros_like(gradient)
    sums[...] = jnp.zeros_like(sums)
    total = jnp.zeros((side, side), jnp.float32)
    for mode in range(modes):
        total = total + probe_ref[mode, 0] * probe_ref[mode, 0] + probe_ref[mode, 1] * probe_ref[mode, 1]
    power[...] = total
    scale_out[...] = jnp.full(scale_out.shape, 1.0 / jnp.max(total))
    probe_out[...] = probe_ref[...]
    fill_table(factor_ref, table_out)
    by_lanes, by_rows = parity_order(side)

    def order(index, carry):
        high, low = split(diffraction_ref[index])
        seen = dot(jnp.concatenate([by_rows] * 2, axis=1), jnp.concatenate([high, low], axis=0))
        high, low = split(seen)
        seen = dot(jnp.concatenate([high, low], axis=1), jnp.concatenate([by_lanes] * 2, axis=0))
        measured[index] = seen
        return carry

    lax.fori_loop(0, count_ref[0, 0], order, 0)
    copy.wait()
    rows = tile_out.shape[0] // SUBLANES
    spread(tile_out, extended, 0, rows)
    all_slots(
        True, rows, place_ref, count_ref, probe_ref, table_out, extended,
        gradient, sums, power, measured, window, terms, result, back,
    )


def second_kernel(
    place_ref,
    count_ref,
    here_ref,
    halo_ref,
    tile_ref,
    gradient_ref,
    sums_ref,
    measured,
    power,
    probe_ref,
    table_ref,
    gradient,
    spill_out,
    mine_out,
    near_out,
    far_out,
    old_out,
    extended,
    sums,
    window,
    terms,
    result,
    back,
):
    modes = probe_ref.shape[0]
    tile_rows, halo_rows = tile_ref.shape[0] // SUBLANES, halo_ref.shape[0] // SUBLANES
    chunks = sums.shape[0]
    spread(tile_ref, extended, 0, tile_rows)
    spread(halo_ref, extended, tile_rows, halo_rows)
    gradient[pl.ds(0, tile_rows * PITCH), :] = gradient_ref[...]
    gradient[pl.ds(tile_rows * PITCH, halo_rows * PITCH), :] = jnp.zeros((halo_rows * PITCH, LANES), jnp.float32)
    sums[...] = sums_ref[...]
    all_slots(
        False, tile_rows, place_ref, count_ref, probe_ref, table_ref, extended,
        gradient, sums, power, measured, window, terms, result, back,
    )
    gathered(gradient, tile_rows, spill_out, halo_rows)
    core, group, layer = here_ref[0, 0], here_ref[0, 1], here_ref[0, 2]
    groups, layers = mine_out.shape[0], mine_out.shape[1]
    for hop in range(groups):
        for step in range(layers):
            at = (group ^ hop) * layers + lax.rem(layer + step, layers)
            mine_out[hop, step] = sums[core * (chunks // 2) + at]
            if hop < groups - 1:
                near_out[hop, step] = sums[(1 - core) * (chunks // 2) + at]
            else:
                far_out[step] = sums[(1 - core) * (chunks // 2) + at]
    start = pl.multiple_of(((core * groups + group) * layers + layer) * SUBLANES, SUBLANES)
    for mode in range(modes):
        for part in range(2):
            old_out[2 * mode + part] = probe_ref[mode, part, pl.ds(start, SUBLANES), :]


def gradient_step(place, count, here, tile, halo, probe, diffraction, groups, layers):
    modes, parts, side, _ = probe.shape
    planes = parts * modes + 1
    chunks = side // SUBLANES
    f32 = jnp.float32
    smem = pl.BlockSpec(memory_space=pltpu.SMEM)
    vmem = pl.BlockSpec(memory_space=pltpu.VMEM)
    chunk = (planes, SUBLANES, side)
    tile_rows, halo_rows = tile.shape[0] // SUBLANES, halo.shape[0] // SUBLANES
    products = 3 * 16 * modes * diffraction.shape[0] * side**3 // 2
    work = [
        pltpu.VMEM((2, side, side), f32),
        pltpu.VMEM((2, modes * side, 2 * side), jnp.bfloat16),
        pltpu.VMEM((2, modes * side, side), f32),
        pltpu.VMEM((2, side, side), f32),
    ]
    shape = jax.ShapeDtypeStruct
    cost = pl.CostEstimate(flops=2 * products, bytes_accessed=16 << 20, transcendentals=0)
    *begun, scale = pl.pallas_call(
        first_kernel,
        out_shape=(
            shape(tile.shape, f32),
            shape((tile_rows * PITCH, LANES), f32),
            shape((chunks, *chunk), f32),
            shape(diffraction.shape, f32),
            shape((side, side), f32),
            shape(probe.shape, f32),
            shape((2, 4, side, side), jnp.bfloat16),
            shape((1, LANES), f32),
        ),
        in_specs=[smem, smem, pl.BlockSpec(memory_space=pl.ANY), vmem, vmem, vmem],
        out_specs=(vmem,) * 8,
        scratch_shapes=[pltpu.VMEM((tile_rows * PITCH, LANES), f32)] + work + [pltpu.SemaphoreType.DMA],
        compiler_params=pltpu.CompilerParams(vmem_limit_bytes=28 * 1024 * 1024),
        cost_estimate=cost,
        name="slots_inside",
    )(place, count, tile, probe, diffraction, jnp.asarray(tables(side)))
    gradient, *rest = pl.pallas_call(
        second_kernel,
        out_shape=(
            shape(((tile_rows + halo_rows) * PITCH, LANES), f32),
            shape(halo.shape, f32),
            shape((groups, layers, *chunk), f32),
            shape((groups - 1, layers, *chunk), f32),
            shape((layers, *chunk), f32),
            shape((planes - 1, SUBLANES, side), f32),
        ),
        in_specs=[smem, smem, smem] + [vmem] * 8,
        out_specs=(vmem,) * 6,
        scratch_shapes=[
            pltpu.VMEM(((tile_rows + halo_rows) * PITCH, LANES), f32),
            pltpu.VMEM((chunks, *chunk), f32),
        ]
        + work,
        compiler_params=pltpu.CompilerParams(vmem_limit_bytes=30 * 1024 * 1024),
        cost_estimate=cost,
        name="slots_across",
    )(place, count, here, halo, *begun)
    new_tile, top = written(begun[0], gradient, scale, halo.shape[0])
    return new_tile, top, scale, *rest


def write_kernel(tile_ref, gradient_ref, scale_ref, out_ref, top_ref, rows, semaphores):
    scale = scale_ref[...]
    step = out_ref.shape[0] // 4
    copies = []
    for part in range(4):
        at = pl.ds(part * step, step)
        gathered(gradient_ref, part * step // SUBLANES, rows.at[at], step // SUBLANES)
        rows[at, :] = tile_ref[at, :] - rows[at, :] * scale
        copies.append(pltpu.make_async_copy(rows.at[at], out_ref.at[at], semaphores.at[part]))
        copies[-1].start()
    top_ref[...] = rows[pl.ds(0, top_ref.shape[0]), :]
    for copy in copies:
        copy.wait()


def written(tile, gradient, scale, top_rows):
    vmem, anywhere = pl.BlockSpec(memory_space=pltpu.VMEM), pl.BlockSpec(memory_space=pl.ANY)
    return pl.pallas_call(
        write_kernel,
        out_shape=(
            jax.ShapeDtypeStruct(tile.shape, jnp.float32),
            jax.ShapeDtypeStruct((top_rows, LANES), jnp.float32),
        ),
        in_specs=[vmem, vmem, vmem],
        out_specs=(anywhere, vmem),
        scratch_shapes=[pltpu.VMEM(tile.shape, jnp.float32), pltpu.SemaphoreType.DMA((4,))],
        compiler_params=pltpu.CompilerParams(vmem_limit_bytes=10 * 1024 * 1024),
        cost_estimate=pl.CostEstimate(flops=0, bytes_accessed=4 << 20, transcendentals=0),
        name="written",
    )(tile, gradient, scale)


def first_rows(tile, rows):
    def kernel(tile_ref, out_ref, semaphore):
        copy = pltpu.make_async_copy(tile_ref.at[pl.ds(0, rows)], out_ref, semaphore)
        copy.start()
        copy.wait()

    return pl.pallas_call(
        kernel,
        out_shape=jax.ShapeDtypeStruct((rows, LANES), jnp.float32),
        in_specs=[pl.BlockSpec(memory_space=pl.ANY)],
        out_specs=pl.BlockSpec(memory_space=pltpu.VMEM),
        scratch_shapes=[pltpu.SemaphoreType.DMA],
        compiler_params=pltpu.CompilerParams(vmem_limit_bytes=4 * 1024 * 1024),
        cost_estimate=pl.CostEstimate(flops=0, bytes_accessed=16 << 20, transcendentals=0),
        name="first_rows",
    )(tile)


def divide_kernel(old_ref, *refs):
    *parts, out_ref = refs
    total = parts[0][...]
    for part in parts[1:]:
        total = total + part[...]
    out_ref[...] = (EPSILON * old_ref[...] + total[:-1]) / (total[-1:] + EPSILON)


def divided(old, parts):
    return pl.pallas_call(
        divide_kernel,
        out_shape=jax.ShapeDtypeStruct(old.shape, jnp.float32),
        compiler_params=pltpu.CompilerParams(vmem_limit_bytes=4 * 1024 * 1024),
        name="divided",
    )(old, *parts)


def place_kernel(layers, pieces, here_ref, *refs):
    sources, out, semaphores = refs[: len(pieces)], refs[-2], refs[-1]
    core, group, layer = here_ref[0, 0], here_ref[0, 1], here_ref[0, 2]
    copies = []
    for source, (flip, hop, start) in zip(sources, pieces):
        for j in range(source.shape[0]):
            from_layer = lax.rem(layer + layers - (start + j), layers)
            at = (core ^ flip) * (out.shape[1] // 2) + (group ^ hop) * layers + from_layer
            copies.append(pltpu.make_async_copy(source.at[j], out.at[:, at], semaphores.at[len(copies)]))
    for copy in copies:
        copy.start()
    for copy in copies:
        copy.wait()


def put_in_place(here, layers, pieces, arrays, planes, side, held=None):
    vmem, anywhere = pl.BlockSpec(memory_space=pltpu.VMEM), pl.BlockSpec(memory_space=pl.ANY)
    rest = [] if held is None else [held]
    return pl.pallas_call(
        functools.partial(place_kernel, layers, pieces),
        out_shape=jax.ShapeDtypeStruct((planes, side // SUBLANES, SUBLANES, side), jnp.float32),
        in_specs=[pl.BlockSpec(memory_space=pltpu.SMEM)] + [vmem] * len(arrays) + [anywhere] * len(rest),
        out_specs=anywhere,
        scratch_shapes=[pltpu.SemaphoreType.DMA((sum(array.shape[0] for array in arrays),))],
        input_output_aliases={} if held is None else {1 + len(arrays): 0},
        compiler_params=pltpu.CompilerParams(vmem_limit_bytes=8 * 1024 * 1024),
        cost_estimate=pl.CostEstimate(flops=0, bytes_accessed=4 << 20, transcendentals=0),
        name="put_in_place",
    )(here, *arrays, *rest)


def top_kernel(held_ref, top_ref, arrived_ref, scale_ref, out_ref, rows, semaphore):
    rows[...] = top_ref[...] - arrived_ref[...] * scale_ref[...]
    copy = pltpu.make_async_copy(rows, out_ref.at[pl.ds(0, rows.shape[0])], semaphore)
    copy.start()
    copy.wait()


def with_top(tile, top, arrived, scale):
    vmem, anywhere = pl.BlockSpec(memory_space=pltpu.VMEM), pl.BlockSpec(memory_space=pl.ANY)
    return pl.pallas_call(
        top_kernel,
        out_shape=jax.ShapeDtypeStruct(tile.shape, jnp.float32),
        in_specs=[anywhere, vmem, vmem, vmem],
        out_specs=anywhere,
        scratch_shapes=[pltpu.VMEM(top.shape, jnp.float32), pltpu.SemaphoreType.DMA],
        input_output_aliases={0: 0},
        compiler_params=pltpu.CompilerParams(vmem_limit_bytes=8 * 1024 * 1024),
        cost_estimate=pl.CostEstimate(flops=0, bytes_accessed=2 << 20, transcendentals=0),
        name="with_top",
    )(tile, top, arrived, scale)


def across(block, hop):
    return lax.ppermute(block, "group", [(i, i ^ hop) for i in range(lax.axis_size("group"))])


def from_partner(block):
    return lax.ppermute(block, "region", [(i, i ^ 1) for i in range(lax.axis_size("region"))])


def up_layers(block, step):
    regions = lax.axis_size("region")
    return lax.ppermute(block, "region", [(i, (i + 2 * step) % regions) for i in range(regions)])


def probe_by_shards(probe, mine, near, far, old, here, layers, spill, new_tile, top, scale):
    modes, parts, side, _ = probe.shape
    planes = modes * parts
    half = layers // 2
    near, other_far = lax.optimization_barrier((near, from_partner(far)))
    other_near, spill = lax.optimization_barrier((from_partner(near), spill))
    arrived = shifted(spill, "region", 1)
    far_sum = mine[3] + other_far
    by_x, by_y = across(far_sum[:half], 1), across(far_sum[half:], 2)
    near_sum = mine[:3] + other_near
    to_x = near_sum[1].at[half:].add(by_y)
    to_y = near_sum[2].at[:half].add(by_x)
    by_x, by_y, new_tile, top = lax.optimization_barrier((across(to_x, 1), across(to_y, 2), new_tile, top))
    summed = [near_sum[0, step] + by_x[step] + by_y[step] for step in range(layers)]
    *others, arrived = lax.optimization_barrier(
        (*[up_layers(summed[step], step) for step in range(1, layers)], arrived)
    )
    new_tile = with_top(new_tile, top, arrived, scale)
    fresh = divided(old, [summed[0]] + others)
    *others, new_tile = lax.optimization_barrier(
        (*[up_layers(fresh, step) for step in range(1, layers)], new_tile)
    )
    own = jnp.stack([fresh] + others)
    x, y = across(own, 1), across(own, 2)
    far = [across(x[:half], 2), across(y[half:], 1)]
    near = [own, x, y, from_partner(own), from_partner(x), from_partner(y)]
    placed = put_in_place(
        here, layers, tuple((flip, hop, 0) for flip in range(2) for hop in range(3)), near, planes, side
    )
    *far, placed = lax.optimization_barrier((*far, placed))
    far = far + [from_partner(array) for array in far]
    pieces = tuple((flip, 3, start) for flip in range(2) for start in (0, half))
    placed = put_in_place(here, layers, pieces, far, planes, side, placed)
    return placed.reshape(probe.shape), new_tile


def probe_from_whole(probe, mine, near, far):
    side = probe.shape[2]
    own = mine.reshape(-1, *mine.shape[2:])
    rest = jnp.concatenate([near.reshape(-1, *near.shape[2:]), far])
    whole = lax.psum(jnp.concatenate([own, rest]), ("region", "group"))
    whole = whole.transpose(1, 0, 2, 3).reshape(-1, side, side)
    old = probe.reshape(-1, side, side)
    return ((EPSILON * old + whole[:-1]) / (whole[-1:] + EPSILON)).reshape(probe.shape)


def on_device(object_slab, probe, diffraction, positions, slot_counts):
    modes, parts, side, _ = probe.shape
    tile_rows, _, columns = object_slab.shape
    regions, groups = lax.axis_size("region"), lax.axis_size("group")
    region, group = lax.axis_index("region"), lax.axis_index("group")
    per_row = parts * columns // LANES
    assert per_row == SUBLANES
    layers = regions // 2
    sharded = groups == 4 and 2 * groups * layers * SUBLANES == side
    tile = packed(object_slab)
    halo = shifted(first_rows(tile, side * per_row), "region", -1)
    place = positions - jnp.stack([region * tile_rows, jnp.zeros_like(region)])[None, :].astype(jnp.int32)
    if sharded:
        here = jnp.stack([region % 2, group, region // 2]).astype(jnp.int32).reshape(1, 3)
    else:
        here = jnp.zeros((1, 3), jnp.int32)
        groups, layers = 4, side // SUBLANES // 8
    new_tile, top, scale, spill, mine, near, far, old = gradient_step(
        place, slot_counts, here, tile, halo, probe, diffraction, groups, layers
    )
    if sharded:
        new_probe, new_tile = probe_by_shards(
            probe, mine, near, far, old, here, layers, spill, new_tile, top, scale
        )
    else:
        new_tile = with_top(new_tile, top, shifted(spill, "region", 1), scale)
        new_probe = probe_from_whole(probe, mine, near, far)
    return (unpacked(new_tile, object_slab.shape), new_probe)


def solution(mesh):
    placed = (
        P("region", None, "group"),
        P(),
        P(("region", "group"), None, None),
        P(("region", "group"), None),
        P("group", "region"),
    )
    return jax.shard_map(
        on_device,
        mesh=mesh,
        in_specs=placed,
        out_specs=(P("region", None, "group"), P()),
        check_vma=False,
    )
```

```python
import functools
import math

import jax
import jax.numpy as jnp
import numpy as np
from jax import lax
from jax.experimental import pallas as pl
from jax.experimental.pallas import tpu as pltpu
from jax.sharding import PartitionSpec as P

LANES = 128
SUBLANES = 8
ROWS = 32
STREAM = 2
EPSILON = 1e-06


def shifted(block, axis, distance):
    devices = range(lax.axis_size(axis))
    route = [(i - distance, i) for i in devices if i - distance in devices]
    return lax.ppermute(block, axis, route)


def packed(block):
    rows, parts, columns = block.shape
    cut = block.reshape(rows, parts, columns // LANES, LANES).transpose(0, 2, 1, 3)
    return cut.reshape(rows * parts * columns // LANES, LANES)


def unpacked(block, shape):
    rows, parts, columns = shape
    cut = block.reshape(rows, columns // LANES, parts, LANES).transpose(0, 2, 1, 3)
    return cut.reshape(rows, parts, columns)


def tables(side):
    half = side // 2
    n, q = np.arange(half)[:, None], np.arange(half)[None, :]
    made = []
    for odd in range(2):
        angle = 2.0 * math.pi * ((n * (2 * q + odd)) % side) / side
        made += [np.cos(angle) / math.sqrt(side), -np.sin(angle) / math.sqrt(side)]
    quarter = side // 4
    q, n = np.arange(quarter)[:, None], np.arange(quarter)[None, :]
    for rest in range(4):
        angle = 2.0 * math.pi * ((n * (4 * q + rest)) % side) / side
        re, im = np.cos(angle) / math.sqrt(side), -np.sin(angle) / math.sqrt(side)
        made.append(np.block([[re, -im], [im, re]]))
    return np.stack(made).astype(np.float32)


def fill_rows_table(factor_ref, rows_table_ref):
    half = factor_ref.shape[1]
    left, right = pl.ds(0, half), pl.ds(half, half)
    for rest in range(4):
        for turned in range(2):
            exact = factor_ref[4 + rest]
            for rows, term in zip((left, right), split(exact.T if turned else exact)):
                rows_table_ref[4 * turned + rest, rows, left] = term
                rows_table_ref[4 * turned + rest, rows, right] = term


def fill_table(factor_ref, table_ref):
    half = factor_ref.shape[1]
    left, right = pl.ds(0, half), pl.ds(half, half)
    for odd in range(2):
        for turned in range(2):
            real, imag = factor_ref[2 * odd], factor_ref[2 * odd + 1]
            if turned:
                real, imag = real.T, -imag.T
            for term, (re, im, minus) in enumerate(zip(split(real), split(imag), split(-imag))):
                entry = 2 * turned + odd
                table_ref[term, entry, left, left] = re
                table_ref[term, entry, left, right] = im
                table_ref[term, entry, right, left] = minus
                table_ref[term, entry, right, right] = re


def orders(side):
    half, quarter = side // 2, side // 4
    first = lax.broadcasted_iota(jnp.int32, (side, side), 0)
    second = lax.broadcasted_iota(jnp.int32, (side, side), 1)

    def moves(hit):
        return hit.astype(jnp.float32).astype(jnp.bfloat16)

    odd = second // half
    rest = first // quarter
    by_lanes = moves(first == 2 * (second - odd * half) + odd)
    by_rows = moves(second == 4 * (first - rest * quarter) + rest)
    return by_lanes, by_rows


def split(x):
    high = x.astype(jnp.bfloat16)
    low = (x - high.astype(jnp.float32)).astype(jnp.bfloat16)
    return high, low


def dot(a, b):
    return jnp.dot(a, b, preferred_element_type=jnp.float32)


def transform(terms, rows, table_ref, table, out):
    side = out.shape[2]
    for half in range(2):
        high = terms[half, rows, pl.ds(0, side)]
        low = terms[half, rows, pl.ds(side, side)]
        t_high, t_low = table_ref[0, table + half], table_ref[1, table + half]
        out[half, rows, :] = dot(
            jnp.concatenate([high, low, high], axis=1),
            jnp.concatenate([t_high, t_high, t_low], axis=0),
        )


def transform_rows(columns, rows, rows_table_ref, table, wide):
    for rest in range(4):
        wide[rest, rows, :] = dot(rows_table_ref[table + rest], columns[rest, rows, :])


def keep_rows(columns, rest, base, start, real, imag):
    quarter = columns.shape[2] // 4
    for part, value in enumerate((real, imag)):
        for term, piece in enumerate(split(value)):
            columns[rest, pl.ds(base + (2 * term + part) * quarter + start, value.shape[0]), :] = piece


def keep(terms, half, start, value):
    rows = pl.ds(start, value.shape[0])
    side = value.shape[1]
    high, low = split(value)
    terms[half, rows, pl.ds(0, side)] = high
    terms[half, rows, pl.ds(side, side)] = low


def beside(real, imag):
    return jnp.concatenate([real, imag], axis=1)


def all_slots(
    local,
    tile_rows,
    place_ref,
    count_ref,
    probe_ref,
    table_ref,
    rows_table_ref,
    extended,
    gradient,
    sums,
    power,
    measured,
    window,
    terms,
    result,
    columns,
    wide,
    back,
):
    modes, _, side, _ = probe_ref.shape
    half = side // 2
    per_row = SUBLANES
    lane = lax.broadcasted_iota(jnp.int32, (side, LANES), 1)
    blocks = side // LANES
    left, right = pl.ds(0, half), pl.ds(half, half)
    pieces = [pl.ds(start, ROWS) for start in range(0, side, ROWS)]
    streams = [range(start, min(start + STREAM, modes)) for start in range(0, modes, STREAM)]

    def rows_of(stream):
        return pl.ds(stream[0] * side, len(stream) * side)

    def slot(index):
        row = place_ref[index, 0]
        column = place_ref[index, 1]
        first = column // LANES
        shift = column - first * LANES
        back_shift = lax.rem(LANES - shift, LANES)
        last = per_row // 2 - 1

        def strided(block, part):
            at = row * per_row + jnp.minimum(first + block, last) * 2 + part
            return pl.ds(at, side, stride=per_row)

        for part in range(2):
            rolled = [
                pltpu.roll(extended[strided(block, part), :], back_shift, 1) for block in range(blocks + 1)
            ]
            for block in range(blocks):
                window[part, :, pl.ds(block * LANES, LANES)] = jnp.where(
                    lane < LANES - shift, rolled[block], rolled[block + 1]
                )
        for stream in streams:
            for mode in stream:
                for rows in pieces:
                    w = [window[part, rows, side_] for part in range(2) for side_ in (left, right)]
                    p = [probe_ref[mode, part, rows, side_] for part in range(2) for side_ in (left, right)]
                    real = [p[k] * w[k] - p[2 + k] * w[2 + k] for k in range(2)]
                    imag = [p[k] * w[2 + k] + p[2 + k] * w[k] for k in range(2)]
                    start = mode * side + rows.start
                    keep(terms, 0, start, beside(real[0] + real[1], imag[0] + imag[1]))
                    keep(terms, 1, start, beside(real[0] - real[1], imag[0] - imag[1]))
            transform(terms, rows_of(stream), table_ref, 0, result)
        quarter = side // 4
        quarters = range(0, quarter, ROWS // 2)

        def taken(rest, base, part, start):
            at = base + part * quarter + start
            return wide[rest, pl.ds(at, ROWS // 2), :] + wide[rest, pl.ds(at + half, ROWS // 2), :]

        for mode in range(modes):
            base = mode * side
            for start in quarters:
                x = [
                    [
                        beside(*[result[odd, pl.ds(base + j * quarter + start, ROWS // 2), side_] for odd in range(2)])
                        for side_ in (left, right)
                    ]
                    for j in range(4)
                ]
                s0, d0 = [x[0][p] + x[2][p] for p in range(2)], [x[0][p] - x[2][p] for p in range(2)]
                s1, d1 = [x[1][p] + x[3][p] for p in range(2)], [x[1][p] - x[3][p] for p in range(2)]
                keep_rows(columns, 0, base, start, s0[0] + s1[0], s0[1] + s1[1])
                keep_rows(columns, 1, base, start, d0[0] + d1[1], d0[1] - d1[0])
                keep_rows(columns, 2, base, start, s0[0] - s1[0], s0[1] - s1[1])
                keep_rows(columns, 3, base, start, d0[0] - d1[1], d0[1] + d1[0])
            transform_rows(columns, pl.ds(base, side), rows_table_ref, 0, wide)
        for rest in range(4):
            for start in quarters:
                far = [[taken(rest, mode * side, part, start) for part in range(2)] for mode in range(modes)]
                intensity = jnp.zeros((ROWS // 2, side), jnp.float32)
                for real, imag in far:
                    intensity = intensity + real * real + imag * imag
                amount = measured[index, pl.ds(rest * quarter + start, ROWS // 2), :]
                ratio = amount * lax.rsqrt(amount * jnp.maximum(intensity, 1.0))
                for mode, (real, imag) in enumerate(far):
                    keep_rows(columns, rest, mode * side, start, real * ratio, imag * ratio)
        for mode in range(modes):
            transform_rows(columns, pl.ds(mode * side, side), rows_table_ref, 4, wide)
        for stream in streams:
            for mode in stream:
                base = mode * side
                for start in quarters:
                    z = [[taken(rest, base, part, start) for part in range(2)] for rest in range(4)]
                    s0, d0 = [z[0][p] + z[2][p] for p in range(2)], [z[0][p] - z[2][p] for p in range(2)]
                    s1, d1 = [z[1][p] + z[3][p] for p in range(2)], [z[1][p] - z[3][p] for p in range(2)]
                    x = [
                        [s0[0] + s1[0], s0[1] + s1[1]],
                        [d0[0] - d1[1], d0[1] + d1[0]],
                        [s0[0] - s1[0], s0[1] - s1[1]],
                        [d0[0] + d1[1], d0[1] - d1[0]],
                    ]
                    for j, (real, imag) in enumerate(x):
                        at = base + j * quarter + start
                        keep(terms, 0, at, beside(real[:, :half], imag[:, :half]))
                        keep(terms, 1, at, beside(real[:, half:], imag[:, half:]))
            transform(terms, rows_of(stream), table_ref, 2, result)
        for number, stream in enumerate(streams):
            for rows in pieces:
                chunk = pl.ds(rows.start // SUBLANES, ROWS // SUBLANES)
                by_chunk = (ROWS // SUBLANES, SUBLANES, half)
                for lower, side_ in enumerate((left, right)):
                    w_r, w_i = window[0, rows, side_], window[1, rows, side_]
                    if number:
                        g_r, g_i = back[0, rows, side_], back[1, rows, side_]
                    else:
                        strength = power[rows, side_]
                        g_r, g_i = strength * w_r, strength * w_i
                    for mode in stream:
                        at = pl.ds(mode * side + rows.start, ROWS)
                        if lower:
                            c_r = result[0, at, left] - result[1, at, left]
                            c_i = result[0, at, right] - result[1, at, right]
                        else:
                            c_r = result[0, at, left] + result[1, at, left]
                            c_i = result[0, at, right] + result[1, at, right]
                        p_r, p_i = probe_ref[mode, 0, rows, side_], probe_ref[mode, 1, rows, side_]
                        g_r = g_r - (p_r * c_r + p_i * c_i)
                        g_i = g_i - (p_r * c_i - p_i * c_r)
                        sums[chunk, 2 * mode, :, side_] += (w_r * c_r + w_i * c_i).reshape(by_chunk)
                        sums[chunk, 2 * mode + 1, :, side_] += (w_r * c_i - w_i * c_r).reshape(by_chunk)
                    back[0, rows, side_] = g_r
                    back[1, rows, side_] = g_i
                    if not number:
                        sums[chunk, 2 * modes, :, side_] += (w_r * w_r + w_i * w_i).reshape(by_chunk)

        for part in range(2):
            rolled = [
                pltpu.roll(back[part, :, pl.ds(block * LANES, LANES)], shift, 1) for block in range(blocks)
            ]
            zero = jnp.zeros((side, LANES), jnp.float32)
            for block in range(blocks + 1):
                here = rolled[block] if block < blocks else zero
                before = rolled[block - 1] if block else zero
                at = strided(block, part)
                gradient[at, :] = gradient[at, :] + jnp.where(lane >= shift, here, before)

    def visit(index, carry):
        inside = place_ref[index, 0] + side <= tile_rows
        pl.when(inside if local else jnp.logical_not(inside))(lambda: slot(index))
        return carry

    lax.fori_loop(0, count_ref[0, 0], visit, 0)


def first_kernel(
    place_ref,
    count_ref,
    tile_hbm,
    probe_ref,
    diffraction_ref,
    factor_ref,
    tile_out,
    gradient,
    sums,
    measured,
    power,
    probe_out,
    table_out,
    rows_table_out,
    scale_out,
    window,
    terms,
    result,
    columns,
    wide,
    back,
    semaphore,
):
    modes, _, side, _ = probe_ref.shape
    copy = pltpu.make_async_copy(tile_hbm, tile_out, semaphore)
    copy.start()
    gradient[...] = jnp.zeros_like(gradient)
    sums[...] = jnp.zeros_like(sums)
    total = jnp.zeros((side, side), jnp.float32)
    for mode in range(modes):
        total = total + probe_ref[mode, 0] * probe_ref[mode, 0] + probe_ref[mode, 1] * probe_ref[mode, 1]
    power[...] = total
    scale_out[...] = jnp.full(scale_out.shape, 1.0 / jnp.max(total))
    probe_out[...] = probe_ref[...]
    fill_table(factor_ref, table_out)
    by_lanes, by_rows = orders(side)
    fill_rows_table(factor_ref, rows_table_out)

    def order(index, carry):
        high, low = split(diffraction_ref[index])
        seen = dot(jnp.concatenate([by_rows] * 2, axis=1), jnp.concatenate([high, low], axis=0))
        high, low = split(seen)
        seen = dot(jnp.concatenate([high, low], axis=1), jnp.concatenate([by_lanes] * 2, axis=0))
        measured[index] = seen
        return carry

    lax.fori_loop(0, count_ref[0, 0], order, 0)
    copy.wait()
    all_slots(
        True, tile_out.shape[0] // SUBLANES, place_ref, count_ref, probe_ref, table_out, rows_table_out, tile_out,
        gradient, sums, power, measured, window, terms, result, columns, wide, back,
    )


def second_kernel(
    place_ref,
    count_ref,
    here_ref,
    halo_ref,
    tile_ref,
    gradient_ref,
    sums_ref,
    measured,
    power,
    probe_ref,
    table_ref,
    rows_table_ref,
    gradient,
    spill_out,
    mine_out,
    near_out,
    far_out,
    old_out,
    extended,
    sums,
    window,
    terms,
    result,
    columns,
    wide,
    back,
):
    modes = probe_ref.shape[0]
    tile_rows, halo_rows, chunks = tile_ref.shape[0], halo_ref.shape[0], sums.shape[0]
    extended[pl.ds(0, tile_rows), :] = tile_ref[...]
    extended[pl.ds(tile_rows, halo_rows), :] = halo_ref[...]
    gradient[pl.ds(0, tile_rows), :] = gradient_ref[...]
    gradient[pl.ds(tile_rows, halo_rows), :] = jnp.zeros((halo_rows, LANES), jnp.float32)
    sums[...] = sums_ref[...]
    all_slots(
        False, tile_rows // SUBLANES, place_ref, count_ref, probe_ref, table_ref, rows_table_ref, extended,
        gradient, sums, power, measured, window, terms, result, columns, wide, back,
    )
    spill_out[...] = gradient[pl.ds(tile_rows, halo_rows), :]
    core, group, layer = here_ref[0, 0], here_ref[0, 1], here_ref[0, 2]
    groups, layers = mine_out.shape[0], mine_out.shape[1]
    for hop in range(groups):
        for step in range(layers):
            at = (group ^ hop) * layers + lax.rem(layer + step, layers)
            mine_out[hop, step] = sums[core * (chunks // 2) + at]
            if hop < groups - 1:
                near_out[hop, step] = sums[(1 - core) * (chunks // 2) + at]
            else:
                far_out[step] = sums[(1 - core) * (chunks // 2) + at]
    start = pl.multiple_of(((core * groups + group) * layers + layer) * SUBLANES, SUBLANES)
    for mode in range(modes):
        for part in range(2):
            old_out[2 * mode + part] = probe_ref[mode, part, pl.ds(start, SUBLANES), :]


def gradient_step(place, count, here, tile, halo, probe, diffraction, groups, layers):
    modes, parts, side, _ = probe.shape
    planes = parts * modes + 1
    chunks = side // SUBLANES
    f32 = jnp.float32
    smem = pl.BlockSpec(memory_space=pltpu.SMEM)
    vmem = pl.BlockSpec(memory_space=pltpu.VMEM)
    chunk = (planes, SUBLANES, side)
    products = 3 * 16 * modes * diffraction.shape[0] * side**3 // 2
    work = [
        pltpu.VMEM((2, side, side), f32),
        pltpu.VMEM((2, modes * side, 2 * side), jnp.bfloat16),
        pltpu.VMEM((2, modes * side, side), f32),
        pltpu.VMEM((4, modes * side, side), jnp.bfloat16),
        pltpu.VMEM((4, modes * side, side), f32),
        pltpu.VMEM((2, side, side), f32),
    ]
    shape = jax.ShapeDtypeStruct
    cost = pl.CostEstimate(flops=2 * products, bytes_accessed=16 << 20, transcendentals=0)
    *begun, scale = pl.pallas_call(
        first_kernel,
        out_shape=(
            shape(tile.shape, f32),
            shape(tile.shape, f32),
            shape((chunks, *chunk), f32),
            shape(diffraction.shape, f32),
            shape((side, side), f32),
            shape(probe.shape, f32),
            shape((2, 4, side, side), jnp.bfloat16),
            shape((8, side, side), jnp.bfloat16),
            shape((1, LANES), f32),
        ),
        in_specs=[smem, smem, pl.BlockSpec(memory_space=pl.ANY), vmem, vmem, vmem],
        out_specs=(vmem,) * 9,
        scratch_shapes=work + [pltpu.SemaphoreType.DMA],
        compiler_params=pltpu.CompilerParams(vmem_limit_bytes=32 * 1024 * 1024),
        cost_estimate=cost,
        name="slots_inside",
    )(place, count, tile, probe, diffraction, jnp.asarray(tables(side)))
    gradient, *rest = pl.pallas_call(
        second_kernel,
        out_shape=(
            shape((tile.shape[0] + halo.shape[0], LANES), f32),
            shape(halo.shape, f32),
            shape((groups, layers, *chunk), f32),
            shape((groups - 1, layers, *chunk), f32),
            shape((layers, *chunk), f32),
            shape((planes - 1, SUBLANES, side), f32),
        ),
        in_specs=[smem, smem, smem] + [vmem] * 9,
        out_specs=(vmem,) * 6,
        scratch_shapes=[
            pltpu.VMEM((tile.shape[0] + halo.shape[0], LANES), f32),
            pltpu.VMEM((chunks, *chunk), f32),
        ]
        + work,
        compiler_params=pltpu.CompilerParams(vmem_limit_bytes=34 * 1024 * 1024),
        cost_estimate=cost,
        name="slots_across",
    )(place, count, here, halo, *begun)
    new_tile, top = written(begun[0], gradient, scale, halo.shape[0])
    return new_tile, top, scale, *rest


def write_kernel(tile_ref, gradient_ref, scale_ref, out_ref, top_ref, rows, semaphores):
    scale = scale_ref[...]
    step = out_ref.shape[0] // 4
    copies = []
    for part in range(4):
        at = pl.ds(part * step, step)
        rows[at, :] = tile_ref[at, :] - gradient_ref[at, :] * scale
        copies.append(pltpu.make_async_copy(rows.at[at], out_ref.at[at], semaphores.at[part]))
        copies[-1].start()
    top_ref[...] = rows[pl.ds(0, top_ref.shape[0]), :]
    for copy in copies:
        copy.wait()


def written(tile, gradient, scale, top_rows):
    vmem, anywhere = pl.BlockSpec(memory_space=pltpu.VMEM), pl.BlockSpec(memory_space=pl.ANY)
    return pl.pallas_call(
        write_kernel,
        out_shape=(
            jax.ShapeDtypeStruct(tile.shape, jnp.float32),
            jax.ShapeDtypeStruct((top_rows, LANES), jnp.float32),
        ),
        in_specs=[vmem, vmem, vmem],
        out_specs=(anywhere, vmem),
        scratch_shapes=[pltpu.VMEM(tile.shape, jnp.float32), pltpu.SemaphoreType.DMA((4,))],
        compiler_params=pltpu.CompilerParams(vmem_limit_bytes=10 * 1024 * 1024),
        cost_estimate=pl.CostEstimate(flops=0, bytes_accessed=4 << 20, transcendentals=0),
        name="written",
    )(tile, gradient, scale)


def first_rows(tile, rows):
    def kernel(tile_ref, out_ref, semaphore):
        copy = pltpu.make_async_copy(tile_ref.at[pl.ds(0, rows)], out_ref, semaphore)
        copy.start()
        copy.wait()

    return pl.pallas_call(
        kernel,
        out_shape=jax.ShapeDtypeStruct((rows, LANES), jnp.float32),
        in_specs=[pl.BlockSpec(memory_space=pl.ANY)],
        out_specs=pl.BlockSpec(memory_space=pltpu.VMEM),
        scratch_shapes=[pltpu.SemaphoreType.DMA],
        compiler_params=pltpu.CompilerParams(vmem_limit_bytes=4 * 1024 * 1024),
        cost_estimate=pl.CostEstimate(flops=0, bytes_accessed=16 << 20, transcendentals=0),
        name="first_rows",
    )(tile)


def divide_kernel(old_ref, *refs):
    *parts, out_ref = refs
    total = parts[0][...]
    for part in parts[1:]:
        total = total + part[...]
    out_ref[...] = (EPSILON * old_ref[...] + total[:-1]) / (total[-1:] + EPSILON)


def divided(old, parts):
    return pl.pallas_call(
        divide_kernel,
        out_shape=jax.ShapeDtypeStruct(old.shape, jnp.float32),
        compiler_params=pltpu.CompilerParams(vmem_limit_bytes=4 * 1024 * 1024),
        name="divided",
    )(old, *parts)


def place_kernel(layers, pieces, here_ref, *refs):
    sources, out, semaphores = refs[: len(pieces)], refs[-2], refs[-1]
    core, group, layer = here_ref[0, 0], here_ref[0, 1], here_ref[0, 2]
    copies = []
    for source, (flip, hop, start) in zip(sources, pieces):
        for j in range(source.shape[0]):
            from_layer = lax.rem(layer + layers - (start + j), layers)
            at = (core ^ flip) * (out.shape[1] // 2) + (group ^ hop) * layers + from_layer
            copies.append(pltpu.make_async_copy(source.at[j], out.at[:, at], semaphores.at[len(copies)]))
    for copy in copies:
        copy.start()
    for copy in copies:
        copy.wait()


def put_in_place(here, layers, pieces, arrays, planes, side, held=None):
    vmem, anywhere = pl.BlockSpec(memory_space=pltpu.VMEM), pl.BlockSpec(memory_space=pl.ANY)
    rest = [] if held is None else [held]
    return pl.pallas_call(
        functools.partial(place_kernel, layers, pieces),
        out_shape=jax.ShapeDtypeStruct((planes, side // SUBLANES, SUBLANES, side), jnp.float32),
        in_specs=[pl.BlockSpec(memory_space=pltpu.SMEM)] + [vmem] * len(arrays) + [anywhere] * len(rest),
        out_specs=anywhere,
        scratch_shapes=[pltpu.SemaphoreType.DMA((sum(array.shape[0] for array in arrays),))],
        input_output_aliases={} if held is None else {1 + len(arrays): 0},
        compiler_params=pltpu.CompilerParams(vmem_limit_bytes=8 * 1024 * 1024),
        cost_estimate=pl.CostEstimate(flops=0, bytes_accessed=4 << 20, transcendentals=0),
        name="put_in_place",
    )(here, *arrays, *rest)


def top_kernel(held_ref, top_ref, arrived_ref, scale_ref, out_ref, rows, semaphore):
    rows[...] = top_ref[...] - arrived_ref[...] * scale_ref[...]
    copy = pltpu.make_async_copy(rows, out_ref.at[pl.ds(0, rows.shape[0])], semaphore)
    copy.start()
    copy.wait()


def with_top(tile, top, arrived, scale):
    vmem, anywhere = pl.BlockSpec(memory_space=pltpu.VMEM), pl.BlockSpec(memory_space=pl.ANY)
    return pl.pallas_call(
        top_kernel,
        out_shape=jax.ShapeDtypeStruct(tile.shape, jnp.float32),
        in_specs=[anywhere, vmem, vmem, vmem],
        out_specs=anywhere,
        scratch_shapes=[pltpu.VMEM(top.shape, jnp.float32), pltpu.SemaphoreType.DMA],
        input_output_aliases={0: 0},
        compiler_params=pltpu.CompilerParams(vmem_limit_bytes=8 * 1024 * 1024),
        cost_estimate=pl.CostEstimate(flops=0, bytes_accessed=2 << 20, transcendentals=0),
        name="with_top",
    )(tile, top, arrived, scale)


def across(block, hop):
    return lax.ppermute(block, "group", [(i, i ^ hop) for i in range(lax.axis_size("group"))])


def from_partner(block):
    return lax.ppermute(block, "region", [(i, i ^ 1) for i in range(lax.axis_size("region"))])


def up_layers(block, step):
    regions = lax.axis_size("region")
    return lax.ppermute(block, "region", [(i, (i + 2 * step) % regions) for i in range(regions)])


def probe_by_shards(probe, mine, near, far, old, here, layers, spill, new_tile, top, scale):
    modes, parts, side, _ = probe.shape
    planes = modes * parts
    half = layers // 2
    near, other_far = lax.optimization_barrier((near, from_partner(far)))
    other_near, spill = lax.optimization_barrier((from_partner(near), spill))
    arrived = shifted(spill, "region", 1)
    far_sum = mine[3] + other_far
    by_x, by_y = across(far_sum[:half], 1), across(far_sum[half:], 2)
    near_sum = mine[:3] + other_near
    to_x = near_sum[1].at[half:].add(by_y)
    to_y = near_sum[2].at[:half].add(by_x)
    by_x, by_y, new_tile, top = lax.optimization_barrier((across(to_x, 1), across(to_y, 2), new_tile, top))
    summed = [near_sum[0, step] + by_x[step] + by_y[step] for step in range(layers)]
    *others, arrived = lax.optimization_barrier(
        (*[up_layers(summed[step], step) for step in range(1, layers)], arrived)
    )
    new_tile = with_top(new_tile, top, arrived, scale)
    fresh = divided(old, [summed[0]] + others)
    *others, new_tile = lax.optimization_barrier(
        (*[up_layers(fresh, step) for step in range(1, layers)], new_tile)
    )
    own = jnp.stack([fresh] + others)
    x, y = across(own, 1), across(own, 2)
    far = [across(x[:half], 2), across(y[half:], 1)]
    near = [own, x, y, from_partner(own), from_partner(x), from_partner(y)]
    placed = put_in_place(
        here, layers, tuple((flip, hop, 0) for flip in range(2) for hop in range(3)), near, planes, side
    )
    *far, placed = lax.optimization_barrier((*far, placed))
    far = far + [from_partner(array) for array in far]
    pieces = tuple((flip, 3, start) for flip in range(2) for start in (0, half))
    placed = put_in_place(here, layers, pieces, far, planes, side, placed)
    return placed.reshape(probe.shape), new_tile


def probe_from_whole(probe, mine, near, far):
    side = probe.shape[2]
    own = mine.reshape(-1, *mine.shape[2:])
    rest = jnp.concatenate([near.reshape(-1, *near.shape[2:]), far])
    whole = lax.psum(jnp.concatenate([own, rest]), ("region", "group"))
    whole = whole.transpose(1, 0, 2, 3).reshape(-1, side, side)
    old = probe.reshape(-1, side, side)
    return ((EPSILON * old + whole[:-1]) / (whole[-1:] + EPSILON)).reshape(probe.shape)


def on_device(object_slab, probe, diffraction, positions, slot_counts):
    modes, parts, side, _ = probe.shape
    tile_rows, _, columns = object_slab.shape
    regions, groups = lax.axis_size("region"), lax.axis_size("group")
    region, group = lax.axis_index("region"), lax.axis_index("group")
    per_row = parts * columns // LANES
    assert per_row == SUBLANES
    layers = regions // 2
    sharded = groups == 4 and 2 * groups * layers * SUBLANES == side
    tile = packed(object_slab)
    halo = shifted(first_rows(tile, side * per_row), "region", -1)
    place = positions - jnp.stack([region * tile_rows, jnp.zeros_like(region)])[None, :].astype(jnp.int32)
    if sharded:
        here = jnp.stack([region % 2, group, region // 2]).astype(jnp.int32).reshape(1, 3)
    else:
        here = jnp.zeros((1, 3), jnp.int32)
        groups, layers = 4, side // SUBLANES // 8
    new_tile, top, scale, spill, mine, near, far, old = gradient_step(
        place, slot_counts, here, tile, halo, probe, diffraction, groups, layers
    )
    if sharded:
        new_probe, new_tile = probe_by_shards(
            probe, mine, near, far, old, here, layers, spill, new_tile, top, scale
        )
    else:
        new_tile = with_top(new_tile, top, shifted(spill, "region", 1), scale)
        new_probe = probe_from_whole(probe, mine, near, far)
    return (unpacked(new_tile, object_slab.shape), new_probe)


def solution(mesh):
    placed = (
        P("region", None, "group"),
        P(),
        P(("region", "group"), None, None),
        P(("region", "group"), None),
        P("group", "region"),
    )
    return jax.shard_map(
        on_device,
        mesh=mesh,
        in_specs=placed,
        out_specs=(P("region", None, "group"), P()),
        check_vma=False,
    )
```

```python
import functools
import math

import jax
import jax.numpy as jnp
import numpy as np
from jax import lax
from jax.experimental import pallas as pl
from jax.experimental.pallas import tpu as pltpu
from jax.sharding import PartitionSpec as P

LANES = 128
SUBLANES = 8
ROWS = 32
STREAM = 2
EPSILON = 1e-06


def shifted(block, axis, distance):
    devices = range(lax.axis_size(axis))
    route = [(i - distance, i) for i in devices if i - distance in devices]
    return lax.ppermute(block, axis, route)


def packed(block):
    rows, parts, columns = block.shape
    cut = block.reshape(rows, parts, columns // LANES, LANES).transpose(0, 2, 1, 3)
    return cut.reshape(rows * parts * columns // LANES, LANES)


def unpacked(block, shape):
    rows, parts, columns = shape
    cut = block.reshape(rows, columns // LANES, parts, LANES).transpose(0, 2, 1, 3)
    return cut.reshape(rows, parts, columns)


def tables(side):
    half = side // 2
    n, q = np.arange(half)[:, None], np.arange(half)[None, :]
    made = []
    for odd in range(2):
        angle = 2.0 * math.pi * ((n * (2 * q + odd)) % side) / side
        made += [np.cos(angle) / math.sqrt(side), -np.sin(angle) / math.sqrt(side)]
    quarter = side // 4
    q, n = np.arange(quarter)[:, None], np.arange(quarter)[None, :]
    for rest in range(4):
        angle = 2.0 * math.pi * ((n * (4 * q + rest)) % side) / side
        re, im = np.cos(angle) / math.sqrt(side), -np.sin(angle) / math.sqrt(side)
        made.append(np.block([[re, -im], [im, re]]))
    return np.stack(made).astype(np.float32)


def fill_rows_table(quarter_ref, rows_table_ref):
    half = quarter_ref.shape[1]
    left, right = pl.ds(0, half), pl.ds(half, half)
    for rest in range(4):
        for turned in range(2):
            exact = quarter_ref[rest]
            for rows, term in zip((left, right), split(exact.T if turned else exact)):
                rows_table_ref[4 * turned + rest, rows, left] = term
                rows_table_ref[4 * turned + rest, rows, right] = term


def fill_table(factor_ref, table_ref):
    half = factor_ref.shape[1]
    left, right = pl.ds(0, half), pl.ds(half, half)
    for odd in range(2):
        for turned in range(2):
            real, imag = factor_ref[2 * odd], factor_ref[2 * odd + 1]
            if turned:
                real, imag = real.T, -imag.T
            for term, (re, im, minus) in enumerate(zip(split(real), split(imag), split(-imag))):
                entry = 2 * turned + odd
                table_ref[term, entry, left, left] = re
                table_ref[term, entry, left, right] = im
                table_ref[term, entry, right, left] = minus
                table_ref[term, entry, right, right] = re


def orders(side):
    half, quarter = side // 2, side // 4
    first = lax.broadcasted_iota(jnp.int32, (side, side), 0)
    second = lax.broadcasted_iota(jnp.int32, (side, side), 1)

    def moves(hit):
        return hit.astype(jnp.float32).astype(jnp.bfloat16)

    odd = second // half
    rest = first // quarter
    by_lanes = moves(first == 2 * (second - odd * half) + odd)
    by_rows = moves(second == 4 * (first - rest * quarter) + rest)
    return by_lanes, by_rows


def split(x):
    high = x.astype(jnp.bfloat16)
    low = (x - high.astype(jnp.float32)).astype(jnp.bfloat16)
    return high, low


def dot(a, b):
    return jnp.dot(a, b, preferred_element_type=jnp.float32)


def transform(terms, rows, table_ref, table, out):
    side = out.shape[2]
    for half in range(2):
        high = terms[half, rows, pl.ds(0, side)]
        low = terms[half, rows, pl.ds(side, side)]
        t_high, t_low = table_ref[0, table + half], table_ref[1, table + half]
        out[half, rows, :] = dot(
            jnp.concatenate([high, low, high], axis=1),
            jnp.concatenate([t_high, t_high, t_low], axis=0),
        )


def transform_rows(columns, rows, rows_table_ref, table, wide):
    for rest in range(4):
        wide[rest, rows, :] = dot(rows_table_ref[table + rest], columns[rest, rows, :])


def keep_rows(columns, rest, base, start, real, imag):
    quarter = columns.shape[2] // 4
    for part, value in enumerate((real, imag)):
        for term, piece in enumerate(split(value)):
            columns[rest, pl.ds(base + (2 * term + part) * quarter + start, value.shape[0]), :] = piece


def keep(terms, half, start, value):
    rows = pl.ds(start, value.shape[0])
    side = value.shape[1]
    high, low = split(value)
    terms[half, rows, pl.ds(0, side)] = high
    terms[half, rows, pl.ds(side, side)] = low


def beside(real, imag):
    return jnp.concatenate([real, imag], axis=1)


def all_slots(
    local,
    tile_rows,
    place_ref,
    count_ref,
    probe_ref,
    table_ref,
    rows_table_ref,
    extended,
    gradient,
    sums,
    power,
    measured,
    window,
    terms,
    result,
    columns,
    wide,
    back,
):
    modes, _, side, _ = probe_ref.shape
    half = side // 2
    per_row = SUBLANES
    lane = lax.broadcasted_iota(jnp.int32, (side, LANES), 1)
    blocks = side // LANES
    left, right = pl.ds(0, half), pl.ds(half, half)
    pieces = [pl.ds(start, ROWS) for start in range(0, side, ROWS)]
    streams = [range(start, min(start + STREAM, modes)) for start in range(0, modes, STREAM)]

    def slot(index):
        row = place_ref[index, 0]
        column = place_ref[index, 1]
        first = column // LANES
        shift = column - first * LANES
        back_shift = lax.rem(LANES - shift, LANES)
        last = per_row // 2 - 1

        def strided(block, part):
            at = row * per_row + jnp.minimum(first + block, last) * 2 + part
            return pl.ds(at, side, stride=per_row)

        for part in range(2):
            rolled = [
                pltpu.roll(extended[strided(block, part), :], back_shift, 1) for block in range(blocks + 1)
            ]
            for block in range(blocks):
                window[part, :, pl.ds(block * LANES, LANES)] = jnp.where(
                    lane < LANES - shift, rolled[block], rolled[block + 1]
                )
        for stream in streams:
            for mode in stream:
                for rows in pieces:
                    w = [window[part, rows, side_] for part in range(2) for side_ in (left, right)]
                    p = [probe_ref[mode, part, rows, side_] for part in range(2) for side_ in (left, right)]
                    real = [p[k] * w[k] - p[2 + k] * w[2 + k] for k in range(2)]
                    imag = [p[k] * w[2 + k] + p[2 + k] * w[k] for k in range(2)]
                    start = mode * side + rows.start
                    keep(terms, 0, start, beside(real[0] + real[1], imag[0] + imag[1]))
                    keep(terms, 1, start, beside(real[0] - real[1], imag[0] - imag[1]))
                transform(terms, pl.ds(mode * side, side), table_ref, 0, result)
        quarter = side // 4
        quarters = range(0, quarter, ROWS // 2)

        def taken(rest, base, part, start):
            at = base + part * quarter + start
            return wide[rest, pl.ds(at, ROWS // 2), :] + wide[rest, pl.ds(at + half, ROWS // 2), :]

        for mode in range(modes):
            base = mode * side
            for start in quarters:
                x = [
                    [
                        beside(*[result[odd, pl.ds(base + j * quarter + start, ROWS // 2), side_] for odd in range(2)])
                        for side_ in (left, right)
                    ]
                    for j in range(4)
                ]
                s0, d0 = [x[0][p] + x[2][p] for p in range(2)], [x[0][p] - x[2][p] for p in range(2)]
                s1, d1 = [x[1][p] + x[3][p] for p in range(2)], [x[1][p] - x[3][p] for p in range(2)]
                keep_rows(columns, 0, base, start, s0[0] + s1[0], s0[1] + s1[1])
                keep_rows(columns, 1, base, start, d0[0] + d1[1], d0[1] - d1[0])
                keep_rows(columns, 2, base, start, s0[0] - s1[0], s0[1] - s1[1])
                keep_rows(columns, 3, base, start, d0[0] - d1[1], d0[1] + d1[0])
            transform_rows(columns, pl.ds(base, side), rows_table_ref, 0, wide)
        for rest in range(4):
            for start in quarters:
                far = [[taken(rest, mode * side, part, start) for part in range(2)] for mode in range(modes)]
                intensity = jnp.zeros((ROWS // 2, side), jnp.float32)
                for real, imag in far:
                    intensity = intensity + real * real + imag * imag
                amount = measured[index, pl.ds(rest * quarter + start, ROWS // 2), :]
                ratio = amount * lax.rsqrt(amount * jnp.maximum(intensity, 1.0))
                for mode, (real, imag) in enumerate(far):
                    keep_rows(columns, rest, mode * side, start, real * ratio, imag * ratio)
        for mode in range(modes):
            transform_rows(columns, pl.ds(mode * side, side), rows_table_ref, 4, wide)
        for stream in streams:
            for mode in stream:
                base = mode * side
                for start in quarters:
                    z = [[taken(rest, base, part, start) for part in range(2)] for rest in range(4)]
                    s0, d0 = [z[0][p] + z[2][p] for p in range(2)], [z[0][p] - z[2][p] for p in range(2)]
                    s1, d1 = [z[1][p] + z[3][p] for p in range(2)], [z[1][p] - z[3][p] for p in range(2)]
                    x = [
                        [s0[0] + s1[0], s0[1] + s1[1]],
                        [d0[0] - d1[1], d0[1] + d1[0]],
                        [s0[0] - s1[0], s0[1] - s1[1]],
                        [d0[0] + d1[1], d0[1] - d1[0]],
                    ]
                    for j, (real, imag) in enumerate(x):
                        at = base + j * quarter + start
                        keep(terms, 0, at, beside(real[:, :half], imag[:, :half]))
                        keep(terms, 1, at, beside(real[:, half:], imag[:, half:]))
                transform(terms, pl.ds(base, side), table_ref, 2, result)
        for number, stream in enumerate(streams):
            for rows in pieces:
                chunk = pl.ds(rows.start // SUBLANES, ROWS // SUBLANES)
                by_chunk = (ROWS // SUBLANES, SUBLANES, half)
                for lower, side_ in enumerate((left, right)):
                    w_r, w_i = window[0, rows, side_], window[1, rows, side_]
                    if number:
                        g_r, g_i = back[0, rows, side_], back[1, rows, side_]
                    else:
                        strength = power[rows, side_]
                        g_r, g_i = strength * w_r, strength * w_i
                    for mode in stream:
                        at = pl.ds(mode * side + rows.start, ROWS)
                        if lower:
                            c_r = result[0, at, left] - result[1, at, left]
                            c_i = result[0, at, right] - result[1, at, right]
                        else:
                            c_r = result[0, at, left] + result[1, at, left]
                            c_i = result[0, at, right] + result[1, at, right]
                        p_r, p_i = probe_ref[mode, 0, rows, side_], probe_ref[mode, 1, rows, side_]
                        g_r = g_r - (p_r * c_r + p_i * c_i)
                        g_i = g_i - (p_r * c_i - p_i * c_r)
                        sums[chunk, 2 * mode, :, side_] += (w_r * c_r + w_i * c_i).reshape(by_chunk)
                        sums[chunk, 2 * mode + 1, :, side_] += (w_r * c_i - w_i * c_r).reshape(by_chunk)
                    back[0, rows, side_] = g_r
                    back[1, rows, side_] = g_i
                    if not number:
                        sums[chunk, 2 * modes, :, side_] += (w_r * w_r + w_i * w_i).reshape(by_chunk)

        for part in range(2):
            rolled = [
                pltpu.roll(back[part, :, pl.ds(block * LANES, LANES)], shift, 1) for block in range(blocks)
            ]
            zero = jnp.zeros((side, LANES), jnp.float32)
            for block in range(blocks + 1):
                here = rolled[block] if block < blocks else zero
                before = rolled[block - 1] if block else zero
                at = strided(block, part)
                gradient[at, :] = gradient[at, :] + jnp.where(lane >= shift, here, before)

    def visit(index, carry):
        inside = place_ref[index, 0] + side <= tile_rows
        pl.when(inside if local else jnp.logical_not(inside))(lambda: slot(index))
        return carry

    lax.fori_loop(0, count_ref[0, 0], visit, 0)


def first_kernel(
    place_ref,
    count_ref,
    tile_hbm,
    probe_ref,
    diffraction_ref,
    factor_ref,
    quarter_ref,
    tile_out,
    gradient,
    sums,
    measured,
    power,
    probe_out,
    table_out,
    rows_table_out,
    scale_out,
    window,
    terms,
    result,
    columns,
    wide,
    back,
    semaphore,
):
    modes, _, side, _ = probe_ref.shape
    copy = pltpu.make_async_copy(tile_hbm, tile_out, semaphore)
    copy.start()
    gradient[...] = jnp.zeros_like(gradient)
    sums[...] = jnp.zeros_like(sums)
    total = jnp.zeros((side, side), jnp.float32)
    for mode in range(modes):
        total = total + probe_ref[mode, 0] * probe_ref[mode, 0] + probe_ref[mode, 1] * probe_ref[mode, 1]
    power[...] = total
    scale_out[...] = jnp.full(scale_out.shape, 1.0 / jnp.max(total))
    probe_out[...] = probe_ref[...]
    fill_table(factor_ref, table_out)
    by_lanes, by_rows = orders(side)
    fill_rows_table(quarter_ref, rows_table_out)

    def order(index, carry):
        high, low = split(diffraction_ref[index])
        seen = dot(jnp.concatenate([by_rows] * 2, axis=1), jnp.concatenate([high, low], axis=0))
        high, low = split(seen)
        seen = dot(jnp.concatenate([high, low], axis=1), jnp.concatenate([by_lanes] * 2, axis=0))
        measured[index] = seen
        return carry

    lax.fori_loop(0, count_ref[0, 0], order, 0)
    copy.wait()
    all_slots(
        True, tile_out.shape[0] // SUBLANES, place_ref, count_ref, probe_ref, table_out, rows_table_out, tile_out,
        gradient, sums, power, measured, window, terms, result, columns, wide, back,
    )


def second_kernel(
    place_ref,
    count_ref,
    here_ref,
    halo_ref,
    tile_ref,
    gradient_ref,
    sums_ref,
    measured,
    power,
    probe_ref,
    table_ref,
    rows_table_ref,
    gradient,
    spill_out,
    mine_out,
    near_out,
    far_out,
    old_out,
    extended,
    sums,
    window,
    terms,
    result,
    columns,
    wide,
    back,
):
    modes = probe_ref.shape[0]
    tile_rows, halo_rows, chunks = tile_ref.shape[0], halo_ref.shape[0], sums.shape[0]
    extended[pl.ds(0, tile_rows), :] = tile_ref[...]
    extended[pl.ds(tile_rows, halo_rows), :] = halo_ref[...]
    gradient[pl.ds(0, tile_rows), :] = gradient_ref[...]
    gradient[pl.ds(tile_rows, halo_rows), :] = jnp.zeros((halo_rows, LANES), jnp.float32)
    sums[...] = sums_ref[...]
    all_slots(
        False, tile_rows // SUBLANES, place_ref, count_ref, probe_ref, table_ref, rows_table_ref, extended,
        gradient, sums, power, measured, window, terms, result, columns, wide, back,
    )
    spill_out[...] = gradient[pl.ds(tile_rows, halo_rows), :]
    core, group, layer = here_ref[0, 0], here_ref[0, 1], here_ref[0, 2]
    groups, layers = mine_out.shape[0], mine_out.shape[1]
    for hop in range(groups):
        for step in range(layers):
            at = (group ^ hop) * layers + lax.rem(layer + step, layers)
            mine_out[hop, step] = sums[core * (chunks // 2) + at]
            if hop < groups - 1:
                near_out[hop, step] = sums[(1 - core) * (chunks // 2) + at]
            else:
                far_out[step] = sums[(1 - core) * (chunks // 2) + at]
    start = pl.multiple_of(((core * groups + group) * layers + layer) * SUBLANES, SUBLANES)
    for mode in range(modes):
        for part in range(2):
            old_out[2 * mode + part] = probe_ref[mode, part, pl.ds(start, SUBLANES), :]


def gradient_step(place, count, here, tile, halo, probe, diffraction, groups, layers):
    modes, parts, side, _ = probe.shape
    planes = parts * modes + 1
    chunks = side // SUBLANES
    f32 = jnp.float32
    smem = pl.BlockSpec(memory_space=pltpu.SMEM)
    vmem = pl.BlockSpec(memory_space=pltpu.VMEM)
    chunk = (planes, SUBLANES, side)
    products = 3 * 16 * modes * diffraction.shape[0] * side**3 // 2
    factors = tables(side)
    work = [
        pltpu.VMEM((2, side, side), f32),
        pltpu.VMEM((2, modes * side, 2 * side), jnp.bfloat16),
        pltpu.VMEM((2, modes * side, side), f32),
        pltpu.VMEM((4, modes * side, side), jnp.bfloat16),
        pltpu.VMEM((4, modes * side, side), f32),
        pltpu.VMEM((2, side, side), f32),
    ]
    shape = jax.ShapeDtypeStruct
    cost = pl.CostEstimate(flops=2 * products, bytes_accessed=16 << 20, transcendentals=0)
    *begun, scale = pl.pallas_call(
        first_kernel,
        out_shape=(
            shape(tile.shape, f32),
            shape(tile.shape, f32),
            shape((chunks, *chunk), f32),
            shape(diffraction.shape, f32),
            shape((side, side), f32),
            shape(probe.shape, f32),
            shape((2, 4, side, side), jnp.bfloat16),
            shape((8, side, side), jnp.bfloat16),
            shape((1, LANES), f32),
        ),
        in_specs=[smem, smem, pl.BlockSpec(memory_space=pl.ANY), vmem, vmem, vmem, vmem],
        out_specs=(vmem,) * 9,
        scratch_shapes=work + [pltpu.SemaphoreType.DMA],
        compiler_params=pltpu.CompilerParams(vmem_limit_bytes=32 * 1024 * 1024),
        cost_estimate=cost,
        name="slots_inside",
    )(place, count, tile, probe, diffraction, jnp.asarray(factors[:4]), jnp.asarray(factors[4:]))
    gradient, *rest = pl.pallas_call(
        second_kernel,
        out_shape=(
            shape((tile.shape[0] + halo.shape[0], LANES), f32),
            shape(halo.shape, f32),
            shape((groups, layers, *chunk), f32),
            shape((groups - 1, layers, *chunk), f32),
            shape((layers, *chunk), f32),
            shape((planes - 1, SUBLANES, side), f32),
        ),
        in_specs=[smem, smem, smem] + [vmem] * 9,
        out_specs=(vmem,) * 6,
        scratch_shapes=[
            pltpu.VMEM((tile.shape[0] + halo.shape[0], LANES), f32),
            pltpu.VMEM((chunks, *chunk), f32),
        ]
        + work,
        compiler_params=pltpu.CompilerParams(vmem_limit_bytes=34 * 1024 * 1024),
        cost_estimate=cost,
        name="slots_across",
    )(place, count, here, halo, *begun)
    new_tile, top = written(begun[0], gradient, scale, halo.shape[0])
    return new_tile, top, scale, *rest


def write_kernel(tile_ref, gradient_ref, scale_ref, out_ref, top_ref, rows, semaphores):
    scale = scale_ref[...]
    step = out_ref.shape[0] // 4
    copies = []
    for part in range(4):
        at = pl.ds(part * step, step)
        rows[at, :] = tile_ref[at, :] - gradient_ref[at, :] * scale
        copies.append(pltpu.make_async_copy(rows.at[at], out_ref.at[at], semaphores.at[part]))
        copies[-1].start()
    top_ref[...] = rows[pl.ds(0, top_ref.shape[0]), :]
    for copy in copies:
        copy.wait()


def written(tile, gradient, scale, top_rows):
    vmem, anywhere = pl.BlockSpec(memory_space=pltpu.VMEM), pl.BlockSpec(memory_space=pl.ANY)
    return pl.pallas_call(
        write_kernel,
        out_shape=(
            jax.ShapeDtypeStruct(tile.shape, jnp.float32),
            jax.ShapeDtypeStruct((top_rows, LANES), jnp.float32),
        ),
        in_specs=[vmem, vmem, vmem],
        out_specs=(anywhere, vmem),
        scratch_shapes=[pltpu.VMEM(tile.shape, jnp.float32), pltpu.SemaphoreType.DMA((4,))],
        compiler_params=pltpu.CompilerParams(vmem_limit_bytes=10 * 1024 * 1024),
        cost_estimate=pl.CostEstimate(flops=0, bytes_accessed=4 << 20, transcendentals=0),
        name="written",
    )(tile, gradient, scale)


def first_rows(tile, rows):
    def kernel(tile_ref, out_ref, semaphore):
        copy = pltpu.make_async_copy(tile_ref.at[pl.ds(0, rows)], out_ref, semaphore)
        copy.start()
        copy.wait()

    return pl.pallas_call(
        kernel,
        out_shape=jax.ShapeDtypeStruct((rows, LANES), jnp.float32),
        in_specs=[pl.BlockSpec(memory_space=pl.ANY)],
        out_specs=pl.BlockSpec(memory_space=pltpu.VMEM),
        scratch_shapes=[pltpu.SemaphoreType.DMA],
        compiler_params=pltpu.CompilerParams(vmem_limit_bytes=4 * 1024 * 1024),
        cost_estimate=pl.CostEstimate(flops=0, bytes_accessed=16 << 20, transcendentals=0),
        name="first_rows",
    )(tile)


def divide_kernel(old_ref, *refs):
    *parts, out_ref = refs
    total = parts[0][...]
    for part in parts[1:]:
        total = total + part[...]
    out_ref[...] = (EPSILON * old_ref[...] + total[:-1]) / (total[-1:] + EPSILON)


def divided(old, parts):
    return pl.pallas_call(
        divide_kernel,
        out_shape=jax.ShapeDtypeStruct(old.shape, jnp.float32),
        compiler_params=pltpu.CompilerParams(vmem_limit_bytes=4 * 1024 * 1024),
        name="divided",
    )(old, *parts)


def place_kernel(layers, pieces, here_ref, *refs):
    sources, out, semaphores = refs[: len(pieces)], refs[-2], refs[-1]
    core, group, layer = here_ref[0, 0], here_ref[0, 1], here_ref[0, 2]
    copies = []
    for source, (flip, hop, start) in zip(sources, pieces):
        for j in range(source.shape[0]):
            from_layer = lax.rem(layer + layers - (start + j), layers)
            at = (core ^ flip) * (out.shape[1] // 2) + (group ^ hop) * layers + from_layer
            copies.append(pltpu.make_async_copy(source.at[j], out.at[:, at], semaphores.at[len(copies)]))
    for copy in copies:
        copy.start()
    for copy in copies:
        copy.wait()


def put_in_place(here, layers, pieces, arrays, planes, side, held=None):
    vmem, anywhere = pl.BlockSpec(memory_space=pltpu.VMEM), pl.BlockSpec(memory_space=pl.ANY)
    rest = [] if held is None else [held]
    return pl.pallas_call(
        functools.partial(place_kernel, layers, pieces),
        out_shape=jax.ShapeDtypeStruct((planes, side // SUBLANES, SUBLANES, side), jnp.float32),
        in_specs=[pl.BlockSpec(memory_space=pltpu.SMEM)] + [vmem] * len(arrays) + [anywhere] * len(rest),
        out_specs=anywhere,
        scratch_shapes=[pltpu.SemaphoreType.DMA((sum(array.shape[0] for array in arrays),))],
        input_output_aliases={} if held is None else {1 + len(arrays): 0},
        compiler_params=pltpu.CompilerParams(vmem_limit_bytes=8 * 1024 * 1024),
        cost_estimate=pl.CostEstimate(flops=0, bytes_accessed=4 << 20, transcendentals=0),
        name="put_in_place",
    )(here, *arrays, *rest)


def top_kernel(held_ref, top_ref, arrived_ref, scale_ref, out_ref, rows, semaphore):
    rows[...] = top_ref[...] - arrived_ref[...] * scale_ref[...]
    copy = pltpu.make_async_copy(rows, out_ref.at[pl.ds(0, rows.shape[0])], semaphore)
    copy.start()
    copy.wait()


def with_top(tile, top, arrived, scale):
    vmem, anywhere = pl.BlockSpec(memory_space=pltpu.VMEM), pl.BlockSpec(memory_space=pl.ANY)
    return pl.pallas_call(
        top_kernel,
        out_shape=jax.ShapeDtypeStruct(tile.shape, jnp.float32),
        in_specs=[anywhere, vmem, vmem, vmem],
        out_specs=anywhere,
        scratch_shapes=[pltpu.VMEM(top.shape, jnp.float32), pltpu.SemaphoreType.DMA],
        input_output_aliases={0: 0},
        compiler_params=pltpu.CompilerParams(vmem_limit_bytes=8 * 1024 * 1024),
        cost_estimate=pl.CostEstimate(flops=0, bytes_accessed=2 << 20, transcendentals=0),
        name="with_top",
    )(tile, top, arrived, scale)


def across(block, hop):
    return lax.ppermute(block, "group", [(i, i ^ hop) for i in range(lax.axis_size("group"))])


def from_partner(block):
    return lax.ppermute(block, "region", [(i, i ^ 1) for i in range(lax.axis_size("region"))])


def up_layers(block, step):
    regions = lax.axis_size("region")
    return lax.ppermute(block, "region", [(i, (i + 2 * step) % regions) for i in range(regions)])


def probe_by_shards(probe, mine, near, far, old, here, layers, spill, new_tile, top, scale):
    modes, parts, side, _ = probe.shape
    planes = modes * parts
    half = layers // 2
    near, other_far = lax.optimization_barrier((near, from_partner(far)))
    other_near, spill = lax.optimization_barrier((from_partner(near), spill))
    arrived = shifted(spill, "region", 1)
    far_sum = mine[3] + other_far
    by_x, by_y = across(far_sum[:half], 1), across(far_sum[half:], 2)
    near_sum = mine[:3] + other_near
    to_x = near_sum[1].at[half:].add(by_y)
    to_y = near_sum[2].at[:half].add(by_x)
    by_x, by_y, new_tile, top = lax.optimization_barrier((across(to_x, 1), across(to_y, 2), new_tile, top))
    summed = [near_sum[0, step] + by_x[step] + by_y[step] for step in range(layers)]
    *others, arrived = lax.optimization_barrier(
        (*[up_layers(summed[step], step) for step in range(1, layers)], arrived)
    )
    new_tile = with_top(new_tile, top, arrived, scale)
    fresh = divided(old, [summed[0]] + others)
    *others, new_tile = lax.optimization_barrier(
        (*[up_layers(fresh, step) for step in range(1, layers)], new_tile)
    )
    own = jnp.stack([fresh] + others)
    x, y = across(own, 1), across(own, 2)
    far = [across(x[:half], 2), across(y[half:], 1)]
    near = [own, x, y, from_partner(own), from_partner(x), from_partner(y)]
    placed = put_in_place(
        here, layers, tuple((flip, hop, 0) for flip in range(2) for hop in range(3)), near, planes, side
    )
    *far, placed = lax.optimization_barrier((*far, placed))
    far = far + [from_partner(array) for array in far]
    pieces = tuple((flip, 3, start) for flip in range(2) for start in (0, half))
    placed = put_in_place(here, layers, pieces, far, planes, side, placed)
    return placed.reshape(probe.shape), new_tile


def probe_from_whole(probe, mine, near, far):
    side = probe.shape[2]
    own = mine.reshape(-1, *mine.shape[2:])
    rest = jnp.concatenate([near.reshape(-1, *near.shape[2:]), far])
    whole = lax.psum(jnp.concatenate([own, rest]), ("region", "group"))
    whole = whole.transpose(1, 0, 2, 3).reshape(-1, side, side)
    old = probe.reshape(-1, side, side)
    return ((EPSILON * old + whole[:-1]) / (whole[-1:] + EPSILON)).reshape(probe.shape)


def on_device(object_slab, probe, diffraction, positions, slot_counts):
    modes, parts, side, _ = probe.shape
    tile_rows, _, columns = object_slab.shape
    regions, groups = lax.axis_size("region"), lax.axis_size("group")
    region, group = lax.axis_index("region"), lax.axis_index("group")
    per_row = parts * columns // LANES
    assert per_row == SUBLANES
    layers = regions // 2
    sharded = groups == 4 and 2 * groups * layers * SUBLANES == side
    tile = packed(object_slab)
    halo = shifted(first_rows(tile, side * per_row), "region", -1)
    place = positions - jnp.stack([region * tile_rows, jnp.zeros_like(region)])[None, :].astype(jnp.int32)
    if sharded:
        here = jnp.stack([region % 2, group, region // 2]).astype(jnp.int32).reshape(1, 3)
    else:
        here = jnp.zeros((1, 3), jnp.int32)
        groups, layers = 4, side // SUBLANES // 8
    new_tile, top, scale, spill, mine, near, far, old = gradient_step(
        place, slot_counts, here, tile, halo, probe, diffraction, groups, layers
    )
    if sharded:
        new_probe, new_tile = probe_by_shards(
            probe, mine, near, far, old, here, layers, spill, new_tile, top, scale
        )
    else:
        new_tile = with_top(new_tile, top, shifted(spill, "region", 1), scale)
        new_probe = probe_from_whole(probe, mine, near, far)
    return (unpacked(new_tile, object_slab.shape), new_probe)


def solution(mesh):
    placed = (
        P("region", None, "group"),
        P(),
        P(("region", "group"), None, None),
        P(("region", "group"), None),
        P("group", "region"),
    )
    return jax.shard_map(
        on_device,
        mesh=mesh,
        in_specs=placed,
        out_specs=(P("region", None, "group"), P()),
        check_vma=False,
    )
```
